32 devices in a mesh: ctx: 8 (over y, x, core), exp: 4 (over z).
Axes of the slice: x: 2, y: 2, z: 4, core: 2. Of those that a mesh axis runs over, the one named last changes fastest.
Arguments:
- tokens: bfloat16 [4, 1024, 1536], P('exp', 'ctx'), may hold values from -6 to 6
- out_grad: bfloat16 [4, 1024, 1536], P('exp', 'ctx'), may hold values from -6 to 6
- attn_gain: float32 [1536], replicated, may hold values from 0.5 to 1.5
- moe_gain: float32 [1536], replicated, may hold values from 0.5 to 1.5
- w_query: bfloat16 [1536, 1536], P(('ctx', 'exp')), may hold values from -0.15625 to 0.15625
- lock_projection: bfloat16 [1536, 512], P(('ctx', 'exp')), may hold values from -0.15625 to 0.15625
- content_projection: bfloat16 [1536, 512], P(('ctx', 'exp')), may hold values from -0.15625 to 0.15625
- w_out: bfloat16 [1536, 1536], P(('ctx', 'exp')), may hold values from -0.875 to 0.875
- sigmoid_matrices: bfloat16 [40, 1536, 512], P('exp'), may hold values from -0.15625 to 0.15625
- widener_matrices: bfloat16 [40, 1536, 512], P('exp'), may hold values from -0.15625 to 0.15625
- reducer_matrices: bfloat16 [40, 512, 1536], P('exp'), may hold values from -0.5 to 0.5
- segment_ids: int32 [4, 1024], P('exp', 'ctx'), may hold values from 0 to 2, as said below
- expert_routes: int32 [4, 1024, 8], P('exp', 'ctx'), may hold values from 0 to 39, all different within a row; in each aligned block of 128 rows (0 to 127, 128 to 255, ..., all dimensions but the last counted through in order) at most 48 rows name the same one
- route_weights: float32 [4, 1024, 8], P('exp', 'ctx'), may hold values from 0.06 to 0.2
- adapter_index: int32 [4], replicated, may hold values from 0 to 7
- query_first: bfloat16 [8, 16, 1536], replicated, may hold values from -0.15625 to 0.15625
- query_second: bfloat16 [8, 16, 1536], replicated, may hold values from -0.75 to 0.75
- key_first: bfloat16 [8, 16, 1536], replicated, may hold values from -0.15625 to 0.15625
- lock_final_matrices: bfloat16 [8, 16, 512], replicated, may hold values from -0.75 to 0.75
- value_first: bfloat16 [8, 16, 1536], replicated, may hold values from -0.15625 to 0.15625
- content_final_matrices: bfloat16 [8, 16, 512], replicated, may hold values from -0.75 to 0.75
- output_first: bfloat16 [8, 16, 1536], replicated, may hold values from -0.15625 to 0.15625
- output_second: bfloat16 [8, 16, 1536], replicated, may hold values from -1.5 to 1.5
- gate_first: bfloat16 [8, 40, 16, 1536], P(None, 'exp'), may hold values from -0.15625 to 0.15625
- gate_second: bfloat16 [8, 40, 16, 512], P(None, 'exp'), may hold values from -0.75 to 0.75
- upward_first: bfloat16 [8, 40, 16, 1536], P(None, 'exp'), may hold values from -0.15625 to 0.15625
- upward_second: bfloat16 [8, 40, 16, 512], P(None, 'exp'), may hold values from -0.75 to 0.75
- down_first: bfloat16 [8, 40, 16, 512], P(None, 'exp'), may hold values from -0.25 to 0.25
- down_second: bfloat16 [8, 40, 16, 1536], P(None, 'exp'), may hold values from -1.5 to 1.5
Outputs:
- block_out: bfloat16 [4, 1024, 1536], P('exp', 'ctx')
- tokens_grad: bfloat16 [4, 1024, 1536], P('exp', 'ctx')
- grad_query_first: float32 [8, 16, 1536], replicated
- grad_query_second: float32 [8, 16, 1536], replicated
- grad_key_first: float32 [8, 16, 1536], replicated
- grad_key_second: float32 [8, 16, 512], replicated
- grad_value_first: float32 [8, 16, 1536], replicated
- grad_value_second: float32 [8, 16, 512], replicated
- grad_output_first: float32 [8, 16, 1536], replicated
- grad_output_second: float32 [8, 16, 1536], replicated
- grad_gate_first: float32 [8, 40, 16, 1536], P(None, 'exp', None, 'ctx')
- grad_gate_second: float32 [8, 40, 16, 512], P(None, 'exp', None, 'ctx')
- grad_upward_first: float32 [8, 40, 16, 1536], P(None, 'exp', None, 'ctx')
- grad_upward_second: float32 [8, 40, 16, 512], P(None, 'exp', None, 'ctx')
- grad_down_first: float32 [8, 40, 16, 512], P(None, 'exp', None, 'ctx')
- grad_down_second: float32 [8, 40, 16, 1536], P(None, 'exp', None, 'ctx')
The draws below stay inside these ranges and needn't reach their ends.
Inputs may be any that keep to these rules, and one draw needn't show every extreme that they name: `segment_ids`: in each group the prompt (segment 0) is the first 512 to 576 tokens; then continuations 1 to 2 follow in order, none empty. `expert_routes`: A token names 8 different experts. Among the 128 tokens of one group on one index of ctx (aligned blocks), no expert is named more than 48 times, and in some blocks one is named exactly 48 times.
All inputs are finite; a program needn't handle non-finite values.
Results may differ from the reference program's by a relative error of at most 0.024.
Values may be sent and summed in bfloat16 or wider, within the bound.
No kernel may reach another device: no remote copies, remote signals or barrier semaphores. Data moves between devices by JAX's collectives and lax.ppermute only.
A program may use at most 384 MiB of HBM per device.

```python
import math
import jax
import jax.numpy as jnp
import numpy as np
from jax import lax

EMBEDDING = 1536
ASKING_ATTENDERS = 24
PAIRED_ATTENDERS = 8
ATTENTION_EXTENT = 64
FFE = 512
EXPERTS = 40
TOPK = 8
BOTTLENECK = 16
NUM_CHOICES_X = 8
TOK_DEV = 128
GROUPS = 4
COHORT_LENGTH = 1024
CONT = 2
CAP = 48
JITTER = 4
N_CTX = 8


def draw_segment_ids(key, part):
    key = jax.random.fold_in(key, 5)

    def single_group(group_key):
        prompt_key, jitter_key = jax.random.split(group_key)
        prompt = jax.random.randint(prompt_key, (), COHORT_LENGTH // 2, COHORT_LENGTH * 9 // 16 + 1)
        remain = COHORT_LENGTH - prompt
        counter = jnp.arange(1, CONT, dtype=jnp.int32)
        jitter = jax.random.randint(jitter_key, (CONT - 1,), -JITTER, JITTER + 1)
        bounds = prompt + counter * remain // CONT + jitter
        places = jnp.arange(COHORT_LENGTH, dtype=jnp.int32)
        passed = jnp.sum((places[:, None] >= bounds[None, :]).astype(jnp.int32), axis=1)
        return jnp.where(places < prompt, 0, 1 + passed).astype(jnp.int32)
    return jax.vmap(single_group)(jax.random.split(key, GROUPS))


def plant(values, stream_key, least, top_value):
    place = [jax.random.randint(jax.random.fold_in(stream_key, axis), (), 0, length) for axis, length in enumerate(values.shape)]
    widest = values.shape.index(max(values.shape))
    next_to = place[:widest] + [(place[widest] + 1) % values.shape[widest]] + place[widest + 1:]
    return values.at[tuple(place)].set(least).at[tuple(next_to)].set(top_value)


def steps_of(key, shape, pieces, least, largest):
    loudness = 1.0
    for dim, shards_of in pieces:
        steps = jax.random.uniform(jax.random.fold_in(jax.random.fold_in(key, 6), dim), (shards_of,), jnp.float32, least / len(pieces), largest / len(pieces))
        loudness = loudness * jnp.repeat(jnp.exp(steps), shape[dim] // shards_of).reshape((-1,) + (1,) * (len(shape) - 1 - dim))
    return loudness


def assign_block(stream_key, own, number, rows, number_of, top, bound, lean):
    order = jax.random.permutation(stream_key, number_of)
    packed, usual = load_shares(number_of, rows * top, bound, lean, True), load_shares(number_of, rows * top, bound, lean, False)
    places = jnp.arange(number_of)

    def named(tallies, offset_by):
        used = int((tallies > 0).sum())
        fixed = max(1, used // 4)
        shifted = fixed + (places - fixed + offset_by * (used - fixed)) % max(1, number_of - fixed)
        return jnp.zeros((number_of,), jnp.int32).at[order[jnp.where(places < fixed, places, shifted)]].set(jnp.asarray(tallies, jnp.int32))

    tallies = jnp.where(number % 4 == 0, named(packed, number // 4), named(usual, number - number // 4 - 1))
    mixed = jax.random.permutation(jax.random.fold_in(own, 3), number_of)
    source_of, taker = mixed[0:number_of // 2 * 2:2], mixed[1:number_of // 2 * 2:2]
    margin = jnp.minimum(tallies[source_of] - 1, bound - tallies[taker]) // 2
    margin = jnp.where((source_of == order[0]) | (taker == order[0]) | (tallies[taker] == 0), 0, jnp.maximum(margin, 0))
    shifted = jax.random.randint(jax.random.fold_in(own, 4), (number_of // 2,), 0, 1 << 20) % (margin + 1)
    tallies = tallies.at[source_of].add(-shifted).at[taker].add(shifted)
    labels = jnp.searchsorted(jnp.cumsum(tallies), jnp.arange(rows * top), side="right").astype(jnp.int32)
    listing = labels.reshape(top, rows).T
    listing = listing[jax.random.permutation(jax.random.fold_in(own, 1), rows)]
    offset_by = jax.random.randint(jax.random.fold_in(own, 2), (rows, 1), 0, top)
    return jnp.take_along_axis(listing, (jnp.arange(top)[None, :] + offset_by) % top, axis=1)


def load_shares(count, total, reach, skew, full):
    portions = [(1 << 20) // math.isqrt(standing ** skew) + 1 for standing in range(1, count + 1)]
    largest = reach if full else min(reach, max(-(-total // count), total * portions[0] // sum(portions)))
    least = 1 if total - largest >= count - 1 else 0
    counts, rest = [largest] + [least] * (count - 1), total - largest - least * (count - 1)
    while rest > 0:
        movable = [i for i in range(1, count) if counts[i] < largest] or [i for i in range(1, count) if counts[i] < reach]
        mass, remaining = sum([portions[i] for i in movable]), rest
        for i in movable:
            addition = min(reach - counts[i], max(1, remaining * portions[i] // mass), rest)
            counts[i] = counts[i] + addition
            rest = rest - addition
    return np.array(counts)


def scatter_about(own_key, extent, width, reach, pieces=(), kind=jnp.bfloat16):
    entries = jax.random.normal(own_key, extent, jnp.float32) * width
    if len(pieces) > 0:
        entries = steps_of(own_key, extent, pieces, -0.22, 0.18) * entries
    return jnp.clip(entries, min=-reach, max=reach).astype(kind)


def setup_inputs(seed: int = 0) -> dict:
    streams_of = jax.random.split(jax.random.key(seed), 30)
    tokens = scatter_about(streams_of[0], (GROUPS, COHORT_LENGTH, EMBEDDING), 1.0, 6.0, ((0, 4), (1, 8)))
    out_grad = scatter_about(streams_of[1], (GROUPS, COHORT_LENGTH, EMBEDDING), 1.0, 6.0, ((0, 4), (1, 8)))
    attn_gain = jnp.clip(1.0 + 0.1 * jax.random.normal(streams_of[2], (EMBEDDING,), jnp.float32), 0.5, 1.5)
    moe_gain = jnp.clip(1.0 + 0.1 * jax.random.normal(streams_of[3], (EMBEDDING,), jnp.float32), 0.5, 1.5)
    w_query = scatter_about(streams_of[4], (EMBEDDING, ASKING_ATTENDERS * ATTENTION_EXTENT), EMBEDDING ** -0.5, 0.15625, ((0, 32),))
    lock_projection = scatter_about(streams_of[5], (EMBEDDING, PAIRED_ATTENDERS * ATTENTION_EXTENT), EMBEDDING ** -0.5, 0.15625, ((0, 32),))
    content_projection = scatter_about(streams_of[6], (EMBEDDING, PAIRED_ATTENDERS * ATTENTION_EXTENT), EMBEDDING ** -0.5, 0.15625, ((0, 32),))
    w_out = scatter_about(streams_of[7], (ASKING_ATTENDERS * ATTENTION_EXTENT, EMBEDDING), (ASKING_ATTENDERS * ATTENTION_EXTENT // 32) ** -0.5, 0.875, ((0, 32),))
    sigmoid_matrices = scatter_about(streams_of[8], (EXPERTS, EMBEDDING, FFE), EMBEDDING ** -0.5, 0.15625, ((0, 4),))
    widener_matrices = scatter_about(streams_of[9], (EXPERTS, EMBEDDING, FFE), EMBEDDING ** -0.5, 0.15625, ((0, 4),))
    reducer_matrices = scatter_about(streams_of[10], (EXPERTS, FFE, EMBEDDING), (FFE // 4) ** -0.5, 0.5, ((0, 4),))
    segment_ids = draw_segment_ids(jax.random.fold_in(streams_of[29], 71), 0)
    expert_routes_keys = jax.random.split(jax.random.fold_in(streams_of[12], 1), GROUPS * COHORT_LENGTH // TOK_DEV)
    expert_routes_turns = jax.random.permutation(jax.random.fold_in(streams_of[12], 3), GROUPS * COHORT_LENGTH // TOK_DEV)
    expert_routes = jax.vmap(lambda own, number: assign_block(jax.random.fold_in(streams_of[12], 2), own, number, TOK_DEV, EXPERTS, TOPK, CAP, 1))(expert_routes_keys, expert_routes_turns).reshape((GROUPS, COHORT_LENGTH, TOPK))
    route_weights = jnp.clip(jnp.exp(math.log(0.2) - 1.2039728 * jax.random.uniform(streams_of[13], (GROUPS, COHORT_LENGTH, TOPK), jnp.float32) ** steps_of(streams_of[13], (GROUPS, COHORT_LENGTH, TOPK), ((0, 4), (1, 8)), -0.2, 0.2)), 0.06, 0.2)
    adapter_index = plant(jax.random.randint(streams_of[14], (GROUPS,), 0, NUM_CHOICES_X), jax.random.fold_in(streams_of[14], 1), 0, NUM_CHOICES_X - 1).astype(jnp.int32)
    query_first = scatter_about(streams_of[15], (NUM_CHOICES_X, BOTTLENECK, EMBEDDING), EMBEDDING ** -0.5, 0.15625)
    query_second = scatter_about(streams_of[16], (NUM_CHOICES_X, BOTTLENECK, ASKING_ATTENDERS * ATTENTION_EXTENT), (4 * BOTTLENECK) ** -0.5, 0.75)
    key_first = scatter_about(streams_of[17], (NUM_CHOICES_X, BOTTLENECK, EMBEDDING), EMBEDDING ** -0.5, 0.15625)
    lock_final_matrices = scatter_about(streams_of[18], (NUM_CHOICES_X, BOTTLENECK, PAIRED_ATTENDERS * ATTENTION_EXTENT), (4 * BOTTLENECK) ** -0.5, 0.75)
    value_first = scatter_about(streams_of[19], (NUM_CHOICES_X, BOTTLENECK, EMBEDDING), EMBEDDING ** -0.5, 0.15625)
    content_final_matrices = scatter_about(streams_of[20], (NUM_CHOICES_X, BOTTLENECK, PAIRED_ATTENDERS * ATTENTION_EXTENT), (4 * BOTTLENECK) ** -0.5, 0.75)
    output_first = scatter_about(streams_of[21], (NUM_CHOICES_X, BOTTLENECK, ASKING_ATTENDERS * ATTENTION_EXTENT), (ASKING_ATTENDERS * ATTENTION_EXTENT) ** -0.5, 0.15625)
    output_second = scatter_about(streams_of[22], (NUM_CHOICES_X, BOTTLENECK, EMBEDDING), BOTTLENECK ** -0.5, 1.5)
    gate_first = scatter_about(streams_of[23], (NUM_CHOICES_X, EXPERTS, BOTTLENECK, EMBEDDING), EMBEDDING ** -0.5, 0.15625, ((1, 4),))
    gate_second = scatter_about(streams_of[24], (NUM_CHOICES_X, EXPERTS, BOTTLENECK, FFE), (4 * BOTTLENECK) ** -0.5, 0.75, ((1, 4),))
    upward_first = scatter_about(streams_of[25], (NUM_CHOICES_X, EXPERTS, BOTTLENECK, EMBEDDING), EMBEDDING ** -0.5, 0.15625, ((1, 4),))
    upward_second = scatter_about(streams_of[26], (NUM_CHOICES_X, EXPERTS, BOTTLENECK, FFE), (4 * BOTTLENECK) ** -0.5, 0.75, ((1, 4),))
    down_first = scatter_about(streams_of[27], (NUM_CHOICES_X, EXPERTS, BOTTLENECK, FFE), FFE ** -0.5, 0.25, ((1, 4),))
    down_second = scatter_about(streams_of[28], (NUM_CHOICES_X, EXPERTS, BOTTLENECK, EMBEDDING), BOTTLENECK ** -0.5, 1.5, ((1, 4),))
    return dict(tokens=tokens, out_grad=out_grad, attn_gain=attn_gain, moe_gain=moe_gain, w_query=w_query, lock_projection=lock_projection, content_projection=content_projection, w_out=w_out, sigmoid_matrices=sigmoid_matrices, widener_matrices=widener_matrices, reducer_matrices=reducer_matrices, segment_ids=segment_ids, expert_routes=expert_routes, route_weights=route_weights, adapter_index=adapter_index, query_first=query_first, query_second=query_second, key_first=key_first, lock_final_matrices=lock_final_matrices, value_first=value_first, content_final_matrices=content_final_matrices, output_first=output_first, output_second=output_second, gate_first=gate_first, gate_second=gate_second, upward_first=upward_first, upward_second=upward_second, down_first=down_first, down_second=down_second)


@jax.custom_vjp
def low(v):
    return lax.optimization_barrier(v.astype(jnp.bfloat16)).astype(jnp.float32)

@jax.custom_vjp
def reduced_adjoint(v):
    return v

def low_keep(v):
    return (low(v), None)

def low_pass(kept, adjoint_signal):
    return (adjoint_signal,)

def back_keep(v):
    return (v, None)

def back_low(kept, adjoint_signal):
    return (low(adjoint_signal),)
low.defvjp(low_keep, low_pass)
reduced_adjoint.defvjp(back_keep, back_low)
EPS = 1e-06
LOW_FACTORED = 2.0
MASKED_FLOOR = -1e+30
SCALE = 0.125
STRICT_ACCURACY = lax.Precision.HIGHEST

def matrix_produce(left, right):
    return jnp.dot(left, right, precision=STRICT_ACCURACY, preferred_element_type=jnp.float32)

def root_scaled(content_entries, gain):
    return content_entries * lax.rsqrt(lax.optimization_barrier(jnp.mean(content_entries * content_entries, axis=-1, keepdims=True)) + EPS) * gain

def adapted(record_lines, frozen_plain, first, closing_factor):
    central_values = low(reduced_adjoint(matrix_produce(record_lines, first.T)))
    return matrix_produce(record_lines, frozen_plain) + LOW_FACTORED * matrix_produce(central_values, closing_factor)

def attention(question_entries, lock_entries, content_entries, segments):
    question_tile = min(512, COHORT_LENGTH)
    attender_wise = ASKING_ATTENDERS // PAIRED_ATTENDERS
    question_attenders = question_entries.reshape(COHORT_LENGTH // question_tile, question_tile, PAIRED_ATTENDERS, attender_wise, ATTENTION_EXTENT)
    lock_attenders = lock_entries.reshape(COHORT_LENGTH, PAIRED_ATTENDERS, ATTENTION_EXTENT)
    content_attenders = content_entries.reshape(COHORT_LENGTH, PAIRED_ATTENDERS, ATTENTION_EXTENT)
    places = jnp.arange(COHORT_LENGTH, dtype=jnp.int32)

    def block_scores(item):
        block_queries, block_places, block_segments = item
        score = reduced_adjoint(jnp.einsum('thgd,khd->hgtk', block_queries, lock_attenders, precision=STRICT_ACCURACY) * SCALE)
        later = places[None, :] <= block_places[:, None]
        same = (segments[None, :] == block_segments[:, None]) | (segments[None, :] == 0)
        allowed = later & same
        masked = jnp.where(allowed, score, MASKED_FLOOR)
        highest = lax.optimization_barrier(jnp.max(masked, axis=-1, keepdims=True))
        exponent = jnp.where(allowed, jnp.exp(masked - highest), 0.0)
        weights = exponent / lax.optimization_barrier(jnp.sum(exponent, axis=-1, keepdims=True))
        return jnp.einsum('hgtk,khd->thgd', low(weights), content_attenders, precision=STRICT_ACCURACY)
    blocks = lax.map(jax.checkpoint(block_scores), (question_attenders, places.reshape(-1, question_tile), segments.reshape(-1, question_tile)))
    return blocks.reshape(COHORT_LENGTH, ASKING_ATTENDERS * ATTENTION_EXTENT)

def mixture(normed_mid, routes, gates, frozen, tables, adapter):
    sigmoid_matrices, widener_matrices, reducer_matrices = frozen

    def elected_ones(index):
        return tables[index][adapter]
    flat_routes = routes.reshape(-1)
    onehot = (flat_routes[:, None] == jnp.arange(EXPERTS, dtype=jnp.int32)[None, :]).astype(jnp.int32)
    counted = jnp.cumsum(onehot.reshape(N_CTX, TOK_DEV * TOPK, EXPERTS), axis=1).reshape(-1, EXPERTS)
    slot_rank = lax.optimization_barrier(jnp.sum((counted - 1) * onehot, axis=1))
    block_of = jnp.arange(COHORT_LENGTH * TOPK, dtype=jnp.int32) // (TOK_DEV * TOPK)
    expert_rows = N_CTX * CAP
    target = flat_routes * expert_rows + block_of * CAP + slot_rank
    record_lines = reduced_adjoint(jnp.repeat(normed_mid, TOPK, axis=0))
    holding_place = jnp.zeros((EXPERTS * expert_rows, EMBEDDING), jnp.float32).at[target].set(record_lines).reshape(EXPERTS, expert_rows, EMBEDDING)
    central_sigmoid = low(reduced_adjoint(jnp.einsum('emd,erd->emr', holding_place, elected_ones(8), precision=STRICT_ACCURACY)))
    sigmoidal_input = reduced_adjoint(jnp.einsum('scz,szt->sct', holding_place, sigmoid_matrices, precision=STRICT_ACCURACY) + LOW_FACTORED * jnp.einsum('izk,ikq->izq', central_sigmoid, elected_ones(9), precision=STRICT_ACCURACY))
    central_widener = low(reduced_adjoint(jnp.einsum('emd,erd->emr', holding_place, elected_ones(10), precision=STRICT_ACCURACY)))
    widening_input = reduced_adjoint(jnp.einsum('scz,szt->sct', holding_place, widener_matrices, precision=STRICT_ACCURACY) + LOW_FACTORED * jnp.einsum('izk,ikq->izq', central_widener, elected_ones(11), precision=STRICT_ACCURACY))
    residual_flow = low(sigmoidal_input * jax.nn.sigmoid(sigmoidal_input) * widening_input)
    central_reducer = low(reduced_adjoint(jnp.einsum('emf,erf->emr', residual_flow, elected_ones(12), precision=STRICT_ACCURACY)))
    specialist_answer = jnp.einsum('wor,wrl->wol', residual_flow, reducer_matrices, precision=STRICT_ACCURACY) + LOW_FACTORED * jnp.einsum('usg,ugy->usy', central_reducer, elected_ones(13), precision=STRICT_ACCURACY)
    specialist_answer = low(reduced_adjoint(specialist_answer)).reshape(EXPERTS * expert_rows, EMBEDDING)
    returned = specialist_answer[target].reshape(COHORT_LENGTH, TOPK, EMBEDDING)
    return lax.optimization_barrier(jnp.sum(gates[..., None] * returned, axis=1))

def layer(item, frozen, tables):
    rows_in, segments, routes, gates, adapter = item
    attn_gain, moe_gain, w_query, lock_projection, content_projection, w_out, sigmoid_matrices, widener_matrices, reducer_matrices = frozen

    def elected_ones(index):
        return tables[index][adapter]
    normed_in = low(root_scaled(rows_in, attn_gain))
    question_entries = low(reduced_adjoint(adapted(normed_in, w_query, elected_ones(0), elected_ones(1))))
    lock_entries = low(reduced_adjoint(adapted(normed_in, lock_projection, elected_ones(2), elected_ones(3))))
    content_entries = low(reduced_adjoint(adapted(normed_in, content_projection, elected_ones(4), elected_ones(5))))
    attended = low(reduced_adjoint(attention(question_entries, lock_entries, content_entries, segments)))
    branch = reduced_adjoint(adapted(attended, w_out, elected_ones(6), elected_ones(7)))
    mid = rows_in + branch
    normed_mid = low(root_scaled(mid, moe_gain))
    return mid + mixture(normed_mid, routes, gates, (sigmoid_matrices, widener_matrices, reducer_matrices), tables, adapter)

def reference(tokens, out_grad, attn_gain, moe_gain, w_query, lock_projection, content_projection, w_out, sigmoid_matrices, widener_matrices, reducer_matrices, segment_ids, expert_routes, route_weights, adapter_index, query_first, query_second, key_first, lock_final_matrices, value_first, content_final_matrices, output_first, output_second, gate_first, gate_second, upward_first, upward_second, down_first, down_second):
    unique_one = jnp.float32
    frozen = (attn_gain.astype(unique_one), moe_gain.astype(unique_one), w_query.astype(unique_one), lock_projection.astype(unique_one), content_projection.astype(unique_one), w_out.astype(unique_one), sigmoid_matrices.astype(unique_one), widener_matrices.astype(unique_one), reducer_matrices.astype(unique_one))
    tables = (query_first.astype(unique_one), query_second.astype(unique_one), key_first.astype(unique_one), lock_final_matrices.astype(unique_one), value_first.astype(unique_one), content_final_matrices.astype(unique_one), output_first.astype(unique_one), output_second.astype(unique_one), gate_first.astype(unique_one), gate_second.astype(unique_one), upward_first.astype(unique_one), upward_second.astype(unique_one), down_first.astype(unique_one), down_second.astype(unique_one))

    def forward(inputs, params):

        def group_layer(item):
            return layer(item, frozen, params)
        return lax.map(jax.checkpoint(group_layer), (inputs, segment_ids, expert_routes, route_weights, adapter_index))
    outputs, pullback = jax.vjp(forward, tokens.astype(unique_one), tables)
    grad_tokens, grad_tables = pullback(out_grad.astype(unique_one))
    return (outputs.astype(jnp.bfloat16), grad_tokens.astype(jnp.bfloat16), grad_tables[0], grad_tables[1], grad_tables[2], grad_tables[3], grad_tables[4], grad_tables[5], grad_tables[6], grad_tables[7], grad_tables[8], grad_tables[9], grad_tables[10], grad_tables[11], grad_tables[12], grad_tables[13])
```

```python
import functools

import jax
import jax.numpy as jnp
from jax import lax
from jax.experimental import pallas as pl
from jax.experimental.pallas import tpu as pltpu
from jax.sharding import PartitionSpec as P

ASKING_ATTENDERS = 24
PAIRED_ATTENDERS = 8
ATTENTION_EXTENT = 64
HEADS_PER_PAIR = ASKING_ATTENDERS // PAIRED_ATTENDERS
QUERY_COLS = HEADS_PER_PAIR * ATTENTION_EXTENT
EXPERTS = 40
TOPK = 8
NUM_CHOICES_X = 8
CAP = 48
RANK = 16
LANES = 128

EPS = 1e-06
LOW_FACTORED = 2.0
MASKED_FLOOR = -1e30
SCALE = 0.125
VMEM_LIMIT = 56 * 1024 * 1024

bf16 = jnp.bfloat16
f32 = jnp.float32

HEAD_COLS = 384


def nn(left, right):
    return jnp.dot(left, right, preferred_element_type=f32)


def nt(left, right):
    return lax.dot_general(left, right, (((1,), (1,)), ((), ())), preferred_element_type=f32)


def tn(left, right):
    return lax.dot_general(left, right, (((0,), (0,)), ((), ())), preferred_element_type=f32)


def normed(rows, gain):
    factor = lax.rsqrt(jnp.mean(rows * rows, axis=-1, keepdims=True) + EPS)
    return rows * factor * gain, factor


def norm_back(rows, factor, gain, adjoint):
    weighted = adjoint * gain
    central = jnp.mean(weighted * rows, axis=-1, keepdims=True)
    return factor * (weighted - rows * factor * factor * central)


def whole_block(shape):
    return pl.BlockSpec(shape, lambda *ids: (0,) * len(shape))


def call_params(axes=1):
    return pltpu.CompilerParams(
        dimension_semantics=("arbitrary",) * axes, vmem_limit_bytes=VMEM_LIMIT
    )


def key_mask(seg_col, seg_row, tile, start, kmax):
    key_place = lax.broadcasted_iota(jnp.int32, (kmax, tile), 0)
    query_place = start + lax.broadcasted_iota(jnp.int32, (kmax, tile), 1)
    key_seg = seg_col[pl.ds(0, kmax), :]
    query_seg = seg_row[:, pl.ds(start, tile)]
    same = (key_seg == query_seg) | (key_seg == 0.0)
    return (key_place <= query_place) & same


def project_attend_kernel(
    blocks, ways, order_ref, x_ref, w_ref, first_ref, second_ref, seg_col, seg_row,
    qkv_ref, inner_ref, att_ref, lse_ref, turned,
):
    step = pl.program_id(0)
    rows = x_ref.shape[1]
    x = x_ref[0]
    inner = nt(x, first_ref[...]).astype(bf16)
    qkv = (nn(x, w_ref[...]) + LOW_FACTORED * nn(inner, second_ref[...])).astype(bf16)
    here = pl.ds(pl.multiple_of(step * rows, rows), rows)
    qkv_ref[here, :] = qkv
    inner_ref[here, :] = inner
    turned[:, here] = qkv.astype(f32).T.astype(bf16)

    @pl.when(step == blocks - 1)
    def _():
        part = order_ref[blocks]
        if ways > 1:
            att_ref[...] = jnp.zeros_like(att_ref)
            lse_ref[...] = jnp.zeros_like(lse_ref)
        per_tile = 2 if ways == 1 else 1
        tile = per_tile * rows
        for index in range(blocks // ways // per_tile):
            kmax = (index + 1) * per_tile * ways * rows
            start = pl.multiple_of((index * per_tile * ways + part) * rows, rows)
            if ways == 1:
                start = index * tile
            allowed = key_mask(seg_col, seg_row, tile, start, kmax)
            keys = qkv_ref[pl.ds(0, kmax), 0:LANES]
            values_t = turned[ATTENTION_EXTENT:LANES, pl.ds(0, kmax)]
            outs = []
            sums = []
            for head in range(HEADS_PER_PAIR):
                base = LANES + head * ATTENTION_EXTENT
                q_t = turned[base : base + ATTENTION_EXTENT, pl.ds(start, tile)] * SCALE
                q_pad = jnp.concatenate([q_t, jnp.zeros_like(q_t)], axis=0)
                score = jnp.where(allowed, nn(keys, q_pad), MASKED_FLOOR)
                top = jnp.max(score, axis=0, keepdims=True)
                weight = jnp.exp(score - top)
                total = jnp.sum(weight, axis=0, keepdims=True)
                prob = (weight * (1.0 / total)).astype(bf16)
                outs.append(nn(values_t, prob))
                sums.append(top + jnp.log(total))
            packed = jnp.concatenate(outs, axis=0)
            att_ref[pl.ds(start, tile), :] = packed.T.astype(bf16)
            lse_ref[:, pl.ds(start, tile)] = jnp.concatenate(
                sums + [jnp.zeros((8 - HEADS_PER_PAIR, tile), f32)], axis=0
            )


def project_attend(order, x_blocks, weights, first, second, seg_col, seg_row, ways):
    blocks, rows, width = x_blocks.shape
    total = blocks * rows
    return pl.pallas_call(
        functools.partial(project_attend_kernel, blocks, ways),
        grid_spec=pltpu.PrefetchScalarGridSpec(
            num_scalar_prefetch=1,
            grid=(blocks,),
            in_specs=[
                pl.BlockSpec((1, rows, width), lambda i, order: (order[i], 0, 0)),
                whole_block(weights.shape),
                whole_block(first.shape),
                whole_block(second.shape),
                whole_block(seg_col.shape),
                whole_block(seg_row.shape),
            ],
            out_specs=[
                whole_block((total, HEAD_COLS)),
                whole_block((total, LANES)),
                whole_block((total, QUERY_COLS)),
                whole_block((8, total)),
            ],
            scratch_shapes=[pltpu.VMEM((HEAD_COLS, total), bf16)],
        ),
        out_shape=[
            jax.ShapeDtypeStruct((total, HEAD_COLS), bf16),
            jax.ShapeDtypeStruct((total, LANES), bf16),
            jax.ShapeDtypeStruct((total, QUERY_COLS), bf16),
            jax.ShapeDtypeStruct((8, total), f32),
        ],
        compiler_params=call_params(),
        cost_estimate=pl.CostEstimate(
            flops=2 * total * width * 512 + 8 * total * total * 256,
            bytes_accessed=2 * total * width * 2,
            transcendentals=HEADS_PER_PAIR * total * total,
        ),
        name="project_attend",
    )(order, x_blocks, weights, first, second, seg_col, seg_row)


def attend_back_kernel(
    blocks, ways, order_ref, qkv_ref, adj_ref, lse_ref, second_ref, inner_ref, seg_col, seg_row,
    grad_ref, grad_inner_ref, grad_second_ref, turned, adj_turned, grad_kv,
):
    total = qkv_ref.shape[0]
    rows = total // blocks
    part = order_ref[blocks]
    half = ATTENTION_EXTENT
    for index in range(blocks):
        here = pl.ds(index * rows, rows)
        turned[:, here] = qkv_ref[here, :].astype(f32).T.astype(bf16)
        adj_turned[:, here] = adj_ref[here, :].astype(f32).T.astype(bf16)
    grad_kv[...] = jnp.zeros_like(grad_kv)
    if ways > 1:
        grad_ref[...] = jnp.zeros_like(grad_ref)
    per_tile = 2 if ways == 1 else 1
    tile = per_tile * rows
    zero = jnp.zeros((half, tile), bf16)
    for index in range(blocks // ways // per_tile):
        kmax = (index + 1) * per_tile * ways * rows
        start = pl.multiple_of((index * per_tile * ways + part) * rows, rows)
        if ways == 1:
            start = index * tile
        allowed = key_mask(seg_col, seg_row, tile, start, kmax)
        keys = qkv_ref[pl.ds(0, kmax), 0:LANES]
        keys_t = turned[0:half, pl.ds(0, kmax)]
        grads_q = []
        update = jnp.zeros((kmax, LANES), f32)
        for head in range(HEADS_PER_PAIR):
            base = LANES + head * half
            q_t = turned[base : base + half, pl.ds(start, tile)] * SCALE
            q_pad = jnp.concatenate([q_t, zero], axis=0)
            a_t = adj_turned[head * half : (head + 1) * half, pl.ds(start, tile)]
            a_pad = jnp.concatenate([zero, a_t], axis=0)
            score = nn(keys, q_pad) - lse_ref[head : head + 1, pl.ds(start, tile)]
            prob = jnp.where(allowed, jnp.exp(jnp.where(allowed, score, 0.0)), 0.0)
            grad_prob = nn(keys, a_pad)
            both = prob * grad_prob
            delta = jnp.sum(both, axis=0, keepdims=True)
            grad_score = (both - prob * delta).astype(bf16)
            update = update + nt(grad_score, q_pad) + nt(prob.astype(bf16), a_pad)
            grads_q.append(nn(keys_t, grad_score) * SCALE)
        grad_kv[pl.ds(0, kmax), :] += update
        packed = jnp.concatenate(grads_q + [jnp.zeros((half, tile), f32)], axis=0)
        grad_ref[pl.ds(start, tile), LANES:] = packed.T.astype(bf16)
    grad_ref[:, 0:LANES] = grad_kv[...].astype(bf16)
    grad = grad_ref[...]
    grad_inner_ref[...] = (LOW_FACTORED * nt(grad, second_ref[...])).astype(bf16)
    grad_second_ref[...] = LOW_FACTORED * tn(inner_ref[...], grad)


def attend_back(order, qkv, adj, lse, second, inner, seg_col, seg_row, blocks, ways):
    total = qkv.shape[0]
    return pl.pallas_call(
        functools.partial(attend_back_kernel, blocks, ways),
        grid_spec=pltpu.PrefetchScalarGridSpec(
            num_scalar_prefetch=1,
            grid=(1,),
            in_specs=[
                whole_block(v.shape) for v in (qkv, adj, lse, second, inner, seg_col, seg_row)
            ],
            out_specs=[
                whole_block((total, HEAD_COLS)),
                whole_block((total, LANES)),
                whole_block((LANES, HEAD_COLS)),
            ],
            scratch_shapes=[
                pltpu.VMEM((HEAD_COLS, total), bf16),
                pltpu.VMEM((QUERY_COLS, total), bf16),
                pltpu.VMEM((total, LANES), f32),
            ],
        ),
        out_shape=[
            jax.ShapeDtypeStruct((total, HEAD_COLS), bf16),
            jax.ShapeDtypeStruct((total, LANES), bf16),
            jax.ShapeDtypeStruct((LANES, HEAD_COLS), f32),
        ],
        compiler_params=call_params(),
        cost_estimate=pl.CostEstimate(
            flops=20 * total * total * 256,
            bytes_accessed=total * 2000,
            transcendentals=HEADS_PER_PAIR * total * total,
        ),
        name="attend_back",
    )(order, qkv, adj, lse, second, inner, seg_col, seg_row)


def first_grad_kernel(order_ref, x_ref, grad_inner_ref, out_ref):
    @pl.when(pl.program_id(0) == 0)
    def _():
        out_ref[...] = jnp.zeros_like(out_ref)

    out_ref[...] += tn(grad_inner_ref[...], x_ref[0])


def first_grad(order, x_blocks, grad_inner):
    blocks, rows, width = x_blocks.shape
    return pl.pallas_call(
        first_grad_kernel,
        grid_spec=pltpu.PrefetchScalarGridSpec(
            num_scalar_prefetch=1,
            grid=(blocks,),
            in_specs=[
                pl.BlockSpec((1, rows, width), lambda i, order: (order[i], 0, 0)),
                pl.BlockSpec((rows, LANES), lambda i, order: (i, 0)),
            ],
            out_specs=whole_block((LANES, width)),
        ),
        out_shape=jax.ShapeDtypeStruct((LANES, width), f32),
        compiler_params=call_params(),
        cost_estimate=pl.CostEstimate(
            flops=2 * blocks * rows * width * LANES,
            bytes_accessed=blocks * rows * width * 2,
            transcendentals=0,
        ),
        name="first_grad",
    )(order, x_blocks, grad_inner)


def source_mask(shape, sources):
    row = lax.broadcasted_iota(jnp.int32, shape, 0)
    col = lax.broadcasted_iota(jnp.int32, shape, 1)
    keep = None
    for source in range(sources):
        inside = (row >= source * CAP) & (row < (source + 1) * CAP)
        inside &= (lax.rem(col, sources * RANK) >= source * RANK) & (
            lax.rem(col, sources * RANK) < (source + 1) * RANK
        )
        keep = inside if keep is None else keep | inside
    return keep


def masked(values, sources):
    return jnp.where(source_mask(values.shape, sources), values, 0.0)


def picks(slot_ref, pair, tokens):
    slots = slot_ref[0, :, pair * 2 * tokens : (pair + 1) * 2 * tokens]
    place = lax.broadcasted_iota(jnp.int32, (2 * CAP, 2 * tokens), 0)
    return place == slots


def picked_rows(slot_ref, rows_ref, sources):
    tokens = rows_ref.shape[0] // sources
    parts = []
    for pair in range(sources // 2):
        pick = picks(slot_ref, pair, tokens).astype(f32).astype(bf16)
        rows = rows_ref[pair * 2 * tokens : (pair + 1) * 2 * tokens, :]
        parts.append(nn(pick, rows))
    return jnp.concatenate(parts, axis=0)


def picked_gates(slot_ref, gate_ref, sources):
    tokens = gate_ref.shape[2] // sources
    parts = []
    for pair in range(sources // 2):
        gate = gate_ref[0, :, pair * 2 * tokens : (pair + 1) * 2 * tokens]
        kept = jnp.where(picks(slot_ref, pair, tokens), gate, 0.0)
        parts.append(jnp.sum(kept, axis=1, keepdims=True))
    return jnp.concatenate(parts, axis=0)


def combine(target_ref, values, out_ref, sources):
    tokens = target_ref.shape[0] // sources
    slots = values.shape[1]
    for source in range(sources):
        target = target_ref[source * tokens : (source + 1) * tokens, :]
        place = lax.broadcasted_iota(jnp.int32, (tokens, slots), 1)
        hit = place == target[:, 0:1]
        for choice in range(1, TOPK):
            hit |= place == target[:, choice : choice + 1]
        out_ref[source] = nn(hit.astype(f32).astype(bf16), values[source]).astype(bf16)


def keep_rows(values, rows, expert, sources):
    for source in range(sources):
        values[source, pl.ds(pl.multiple_of(expert * CAP, CAP), CAP), :] = rows[
            source * CAP : (source + 1) * CAP
        ]


def experts_pre_kernel(
    sources, slot_ref, gate_ref, grads_ref, down_ref, down_first, down_second,
    picked_ref, hidden_ref, inner_ref,
):
    grads = picked_rows(slot_ref, grads_ref, sources)
    grads = (grads * picked_gates(slot_ref, gate_ref, sources)).astype(bf16)
    picked_ref[0] = grads
    inner = LOW_FACTORED * nt(grads, down_second[0])
    inner = masked(inner, sources).astype(bf16)
    inner_ref[0] = inner
    hidden_ref[0] = nt(grads, down_ref[0]) + nn(inner, down_first[0])


def experts_main_kernel(
    sources, slot_ref, x_ref, firsts, seconds, gate_w, up_w, grad_hidden, target_ref,
    picked_ref, hidden_ref, adj_ref, inner_ref, out_ref, values,
):
    expert = pl.program_id(0)
    inner_size = gate_w.shape[2]
    x = picked_rows(slot_ref, x_ref, sources).astype(bf16)
    picked_ref[0] = x
    inner = masked(nt(x, firsts[0]), sources).astype(bf16)
    added = LOW_FACTORED * nn(inner, seconds[0])
    gate = nn(x, gate_w[0]) + added[:, :inner_size]
    up = nn(x, up_w[0]) + added[:, inner_size:]
    sigma = 1.0 / (1.0 + jnp.exp(-gate))
    active = gate * sigma
    hidden_ref[0] = (active * up).astype(bf16)
    adj = grad_hidden[0]
    grad_gate = (adj * up * sigma * (1.0 + gate * (1.0 - sigma))).astype(bf16)
    grad_up = (adj * active).astype(bf16)
    both = jnp.concatenate([grad_gate, grad_up], axis=1)
    adj_ref[0] = both
    grad_inner = masked(LOW_FACTORED * nt(both, seconds[0]), sources).astype(bf16)
    inner_ref[0] = jnp.concatenate([inner, grad_inner], axis=1)
    rows = nt(grad_gate, gate_w[0]) + nt(grad_up, up_w[0]) + nn(grad_inner, firsts[0])
    keep_rows(values, rows.astype(bf16), expert, sources)

    @pl.when(expert == pl.num_programs(0) - 1)
    def _():
        combine(target_ref, values, out_ref, sources)


def experts_post_kernel(
    sources, cohort, slot_ref, gate_ref, down_ref, down_first, down_second, picked_ref, hidden_ref,
    adj_ref, inner_ref, picked_grads, grad_inner_down, target_ref,
    table_ref, out_ref, values,
):
    expert = pl.program_id(0)
    span = sources * RANK
    hidden = hidden_ref[0]
    inner_down = masked(nt(hidden, down_first[0]), sources).astype(bf16)
    answer = nn(hidden, down_ref[0]) + LOW_FACTORED * nn(inner_down, down_second[0])
    answer = answer.astype(bf16).astype(f32) * picked_gates(slot_ref, gate_ref, sources)
    keep_rows(values, answer.astype(bf16), expert, sources)
    width = picked_ref.shape[2]
    inner_size = hidden.shape[1]
    inner = inner_ref[0, :, : 2 * span]
    grad_inner = inner_ref[0, :, 2 * span :]
    firsts = tn(grad_inner, picked_ref[0])
    seconds = LOW_FACTORED * tn(inner, adj_ref[0])
    down_firsts = tn(grad_inner_down[0], hidden)
    down_seconds = LOW_FACTORED * tn(inner_down, picked_grads[0])
    wide, slim = width // cohort, inner_size // cohort
    wide_parts = (firsts[:span], firsts[span:], down_seconds)
    slim_parts = (seconds[:span, :inner_size], seconds[span:, inner_size:], down_firsts)
    for place in range(cohort):
        pieces = [v[:, place * wide : (place + 1) * wide] for v in wide_parts]
        pieces += [v[:, place * slim : (place + 1) * slim] for v in slim_parts]
        table_ref[place, 0] = jnp.concatenate(pieces, axis=1).astype(bf16)

    @pl.when(expert == pl.num_programs(0) - 1)
    def _():
        combine(target_ref, values, out_ref, sources)


def per_expert(array):
    rest = array.shape[1:]
    return pl.BlockSpec((1,) + rest, lambda e: (e,) + (0,) * len(rest))


def experts_pre(slots, gates, grads, down, down_first, down_second):
    experts, sources = slots.shape[0], down_first.shape[1] // RANK
    width, inner_size = down.shape[2], down.shape[1]
    rows = sources * CAP
    return pl.pallas_call(
        functools.partial(experts_pre_kernel, sources),
        grid=(experts,),
        in_specs=[
            per_expert(slots),
            per_expert(gates),
            whole_block((grads.shape[0], width)),
            per_expert(down),
            per_expert(down_first),
            per_expert(down_second),
        ],
        out_specs=[
            pl.BlockSpec((1, rows, width), lambda e: (e, 0, 0)),
            pl.BlockSpec((1, rows, inner_size), lambda e: (e, 0, 0)),
            pl.BlockSpec((1, rows, sources * RANK), lambda e: (e, 0, 0)),
        ],
        out_shape=[
            jax.ShapeDtypeStruct((experts, rows, width), bf16),
            jax.ShapeDtypeStruct((experts, rows, inner_size), f32),
            jax.ShapeDtypeStruct((experts, rows, sources * RANK), bf16),
        ],
        compiler_params=call_params(),
        cost_estimate=pl.CostEstimate(
            flops=2 * experts * rows * width * inner_size * 2,
            bytes_accessed=experts * width * (inner_size * 2 + rows * 2),
            transcendentals=0,
        ),
        name="experts_pre",
    )(slots, gates, grads, down, down_first, down_second)


def experts_main(slots, x, firsts, seconds, gate_w, up_w, grad_hidden, target):
    experts, width, inner_size = gate_w.shape
    sources = firsts.shape[1] // (2 * RANK)
    rows = sources * CAP
    tokens = x.shape[0] // sources
    return pl.pallas_call(
        functools.partial(experts_main_kernel, sources),
        grid=(experts,),
        in_specs=[
            per_expert(slots),
            whole_block(x.shape),
            per_expert(firsts),
            per_expert(seconds),
            per_expert(gate_w),
            per_expert(up_w),
            per_expert(grad_hidden),
            whole_block(target.shape),
        ],
        out_specs=[
            pl.BlockSpec((1, rows, width), lambda e: (e, 0, 0)),
            pl.BlockSpec((1, rows, inner_size), lambda e: (e, 0, 0)),
            pl.BlockSpec((1, rows, 2 * inner_size), lambda e: (e, 0, 0)),
            pl.BlockSpec((1, rows, 4 * sources * RANK), lambda e: (e, 0, 0)),
            whole_block((sources, tokens, width)),
        ],
        out_shape=[
            jax.ShapeDtypeStruct((experts, rows, width), bf16),
            jax.ShapeDtypeStruct((experts, rows, inner_size), bf16),
            jax.ShapeDtypeStruct((experts, rows, 2 * inner_size), bf16),
            jax.ShapeDtypeStruct((experts, rows, 4 * sources * RANK), bf16),
            jax.ShapeDtypeStruct((sources, tokens, width), bf16),
        ],
        scratch_shapes=[pltpu.VMEM((sources, experts * CAP, width), bf16)],
        compiler_params=call_params(),
        cost_estimate=pl.CostEstimate(
            flops=2 * experts * rows * width * inner_size * 5,
            bytes_accessed=experts * width * (inner_size * 4 + rows * 4),
            transcendentals=experts * rows * inner_size,
        ),
        name="experts_main",
    )(slots, x, firsts, seconds, gate_w, up_w, grad_hidden, target)


def experts_post(
    slots, gates, down, down_first, down_second, picked, hidden, adj, inner, picked_grads,
    grad_inner_down, target, cohort,
):
    experts, inner_size, width = down.shape
    sources = down_first.shape[1] // RANK
    rows = sources * CAP
    tokens = target.shape[0] // sources
    lanes = 3 * (width + inner_size) // cohort
    return pl.pallas_call(
        functools.partial(experts_post_kernel, sources, cohort),
        grid=(experts,),
        in_specs=[
            per_expert(v)
            for v in (
                slots, gates, down, down_first, down_second, picked, hidden, adj, inner,
                picked_grads, grad_inner_down,
            )
        ]
        + [whole_block(target.shape)],
        out_specs=[
            pl.BlockSpec((cohort, 1, sources * RANK, lanes), lambda e: (0, e, 0, 0)),
            whole_block((sources, tokens, width)),
        ],
        out_shape=[
            jax.ShapeDtypeStruct((cohort, experts, sources * RANK, lanes), bf16),
            jax.ShapeDtypeStruct((sources, tokens, width), bf16),
        ],
        scratch_shapes=[pltpu.VMEM((sources, experts * CAP, width), bf16)],
        compiler_params=call_params(),
        cost_estimate=pl.CostEstimate(
            flops=2 * experts * rows * width * inner_size * 2,
            bytes_accessed=experts * width * (inner_size * 2 + rows * 6),
            transcendentals=0,
        ),
        name="experts_post",
    )(
        slots, gates, down, down_first, down_second, picked, hidden, adj, inner, picked_grads,
        grad_inner_down, target,
    )


def shifted(array, axis, size, shift):
    return lax.ppermute(array, axis, [(i, (i + shift) % size) for i in range(size)])


def gather_shifted(array, axis, size):
    return [array] + [shifted(array, axis, size, r) for r in range(1, size)]


def return_shifted(blocks, axis, size):
    total = blocks[0].astype(f32)
    for r in range(1, size):
        total = total + shifted(blocks[r], axis, size, -r).astype(f32)
    return total


def flipped(array, axis, size, mask):
    return lax.ppermute(array, axis, [(i, i ^ mask) for i in range(size)])


def gather_cohort(array, size):
    place = jnp.arange(size, dtype=jnp.int32)
    if size != 8:
        return lax.all_gather(array, "ctx", axis=0, tiled=False), place
    half = array.shape[0] // 2
    near = flipped(array, "ctx", size, 2)
    far = flipped(array, "ctx", size, 4)
    low = flipped(near[:half], "ctx", size, 4)
    high = flipped(far[half:], "ctx", size, 2)
    mine = jnp.stack([array, near, far, jnp.concatenate([low, high], axis=0)])
    other = flipped(mine, "ctx", size, 1)
    blocks = jnp.concatenate([mine, other], axis=0)
    mask = place ^ lax.axis_index("ctx")
    return blocks, (mask & 1) * 4 + mask // 2


def head_columns(query, key, value):
    rows = query.shape[0]

    def split(array):
        return jnp.transpose(array.reshape(rows, PAIRED_ATTENDERS, -1), (1, 0, 2))

    parts = [split(key), split(value), split(query)]
    pad = HEAD_COLS - sum(p.shape[2] for p in parts)
    parts.append(jnp.zeros((PAIRED_ATTENDERS, rows, pad), query.dtype))
    return jnp.concatenate(parts, axis=2)


def body(
    tokens, out_grad, attn_gain, moe_gain, w_query, lock_projection, content_projection, w_out,
    sigmoid_matrices, widener_matrices, reducer_matrices, segment_ids, expert_routes,
    route_weights, adapter_index, query_first, query_second, key_first, lock_final_matrices,
    value_first, content_final_matrices, output_first, output_second, gate_first, gate_second,
    upward_first, upward_second, down_first, down_second,
):
    rows_in = tokens[0].astype(f32)
    count, width = rows_in.shape
    cohort = lax.axis_size("ctx")
    sources = lax.axis_size("exp")
    experts = sigmoid_matrices.shape[0]
    ctx = lax.axis_index("ctx")
    exp = lax.axis_index("exp")
    ways = cohort // PAIRED_ATTENDERS
    head = ctx // ways
    adapter = adapter_index[exp]

    def elected(table):
        return lax.dynamic_index_in_dim(table, adapter, 0, keepdims=False)

    full_out = lax.all_gather(w_out, ("ctx", "exp"), axis=0, tiled=True)
    head_w = head_columns(w_query, lock_projection, content_projection)
    to_all = jnp.broadcast_to(
        head_w[:, None], (PAIRED_ATTENDERS, ways * sources) + head_w.shape[1:]
    ).reshape((cohort * sources,) + head_w.shape[1:])
    own_w = lax.all_to_all(to_all, ("ctx", "exp"), 0, 0, tiled=True).reshape(width, HEAD_COLS)

    normed_in = normed(rows_in, attn_gain)[0].astype(bf16)
    factor_in = normed(rows_in, attn_gain)[1]
    x_blocks, place = gather_cohort(normed_in, cohort)
    segments = lax.all_gather(segment_ids[0].astype(bf16), "ctx", axis=0, tiled=True).astype(f32)
    seg_row, seg_col = segments[None, :], segments[:, None]
    order = jnp.concatenate([place, (ctx % ways)[None].astype(jnp.int32)])

    routes = expert_routes[0].astype(bf16)
    weight_high = route_weights[0].astype(bf16)
    weight_low = (route_weights[0] - weight_high.astype(f32)).astype(bf16)
    parcel = jnp.concatenate(
        [
            out_grad[0], routes, weight_high, weight_low,
            jnp.zeros((count, LANES - 3 * TOPK), bf16),
        ],
        axis=1,
    )
    parcels = jnp.concatenate(gather_shifted(parcel, "exp", sources), axis=0)
    full_in = lax.all_gather(
        jnp.concatenate([w_query, lock_projection, content_projection], axis=1),
        ("ctx", "exp"), axis=0, tiled=True,
    )
    attended_cols = ASKING_ATTENDERS * ATTENTION_EXTENT
    key_cols = PAIRED_ATTENDERS * ATTENTION_EXTENT

    extra = parcels[:, width:].astype(f32)
    all_routes = extra[:, :TOPK].astype(jnp.int32) - exp * experts
    all_gates = extra[:, TOPK : 2 * TOPK] + extra[:, 2 * TOPK : 3 * TOPK]
    hits = all_routes[None] == jnp.arange(experts, dtype=jnp.int32)[:, None, None]
    named = jnp.any(hits, axis=2)
    gates = jnp.sum(jnp.where(hits, all_gates[None], 0.0), axis=2)
    earlier = jnp.tril(jnp.ones((count, count), bf16), -1)
    rank = lax.dot_general(
        named.astype(bf16).reshape(experts * sources, count), earlier,
        (((1,), (1,)), ((), ())), preferred_element_type=f32,
    ).astype(jnp.int32).reshape(experts, sources, count)
    side = (jnp.arange(sources, dtype=jnp.int32) % 2 * CAP)[None, :, None]
    slots = jnp.where(named, (rank + side).reshape(experts, -1), -1)[:, None]
    gates = gates[:, None]
    rank = rank.reshape(experts, sources * count)
    places = jnp.arange(experts, dtype=jnp.int32)[:, None] * CAP + rank + 1
    target = jnp.sum(jnp.where(hits, places[:, :, None], 0), axis=0) - 1

    source_adapters = adapter_index[
        (exp - jnp.arange(sources, dtype=jnp.int32) + sources) % sources
    ]

    def chosen(table):
        taken = jnp.stack([
            lax.dynamic_index_in_dim(table, source_adapters[s], 0, keepdims=False)
            for s in range(sources)
        ], axis=1)
        return taken.reshape(experts, sources * RANK, table.shape[3])

    firsts = jnp.concatenate([chosen(gate_first), chosen(upward_first)], axis=1)
    gate_seconds, up_seconds = chosen(gate_second), chosen(upward_second)
    blank = jnp.zeros_like(gate_seconds)
    seconds = jnp.concatenate(
        [
            jnp.concatenate([gate_seconds, blank], axis=2),
            jnp.concatenate([blank, up_seconds], axis=2),
        ],
        axis=1,
    )
    down_firsts, down_seconds = chosen(down_first), chosen(down_second)

    picked_grads, grad_hidden, grad_inner_down = experts_pre(
        slots, gates, parcels, reducer_matrices, down_firsts, down_seconds
    )

    own_firsts = jnp.concatenate(
        [elected(query_first), elected(key_first), elected(value_first)], axis=0
    )
    own_firsts = jnp.pad(own_firsts, ((0, LANES - 3 * RANK), (0, 0)))

    def head_part(table):
        part = elected(table)
        size = part.shape[1] // PAIRED_ATTENDERS
        return lax.dynamic_slice_in_dim(part, head * size, size, 1)

    def placed(part, row, col):
        return jnp.pad(
            part, ((row, LANES - row - RANK), (col, HEAD_COLS - col - part.shape[1]))
        )

    own_seconds = (
        placed(head_part(query_second), 0, LANES)
        + placed(head_part(lock_final_matrices), RANK, 0)
        + placed(head_part(content_final_matrices), 2 * RANK, ATTENTION_EXTENT)
    )
    qkv, inner, attended_heads, lse = project_attend(
        order, x_blocks, own_w, own_firsts, own_seconds, seg_col, seg_row, ways
    )

    def to_tokens(array):
        got = lax.all_to_all(
            array.reshape(cohort, count, array.shape[1]), "ctx", 0, 0, tiled=True
        )
        if ways > 1:
            got = got.reshape(PAIRED_ATTENDERS, ways, count, -1).astype(f32).sum(1).astype(bf16)
        return got

    attended = jnp.transpose(to_tokens(attended_heads), (1, 0, 2)).reshape(count, attended_cols)
    out_first, out_second = elected(output_first), elected(output_second)
    inner_out = nt(attended, out_first).astype(bf16)
    mid = rows_in + nn(attended, full_out) + LOW_FACTORED * nn(inner_out, out_second)
    normed_mid_f, factor_mid = normed(mid, moe_gain)
    normed_mid = normed_mid_f.astype(bf16)

    x_all = jnp.concatenate(gather_shifted(normed_mid, "exp", sources), axis=0)
    picked, hidden, adj, inner_rows, grad_parts = experts_main(
        slots, x_all, firsts, seconds, sigmoid_matrices, widener_matrices, grad_hidden, target
    )
    grad_normed_mid = return_shifted(
        [grad_parts[r] for r in range(sources)], "exp", sources
    )
    tables, answer_parts = experts_post(
        slots, gates, reducer_matrices, down_firsts, down_seconds, picked, hidden, adj,
        inner_rows, picked_grads, grad_inner_down, target, cohort,
    )
    answers = return_shifted([answer_parts[r] for r in range(sources)], "exp", sources)
    block_out = (mid + answers).astype(bf16)[None]
    table_rows = lax.psum_scatter(tables, "ctx", scatter_dimension=0, tiled=False)

    grad_out = out_grad[0].astype(f32)
    grad_mid = grad_out + norm_back(mid, factor_mid, moe_gain, grad_normed_mid)
    grad_branch = grad_mid.astype(bf16)
    grad_inner_out = (LOW_FACTORED * nt(grad_branch, out_second)).astype(bf16)
    grad_attended = (nt(grad_branch, full_out) + nn(grad_inner_out, out_first)).astype(bf16)
    adj_heads = jnp.transpose(
        grad_attended.reshape(count, PAIRED_ATTENDERS, QUERY_COLS), (1, 0, 2)
    )
    if ways > 1:
        adj_heads = jnp.repeat(adj_heads, ways, axis=0)
    adj_all = lax.all_to_all(adj_heads, "ctx", 0, 0, tiled=True).reshape(-1, QUERY_COLS)
    grad_output_first = tn(grad_inner_out, attended)
    grad_output_second = LOW_FACTORED * tn(inner_out, grad_branch)

    grad_heads, grad_inner, grad_own_seconds = attend_back(
        order, qkv, adj_all, lse, own_seconds, inner, seg_col, seg_row, cohort, ways
    )
    grad_tokens = to_tokens(grad_heads)
    grad_own_firsts = first_grad(order, x_blocks, grad_inner)

    def flat(array):
        return jnp.transpose(array, (1, 0, 2)).reshape(count, -1)

    half = ATTENTION_EXTENT
    grad_key = flat(grad_tokens[:, :, :half])
    grad_value = flat(grad_tokens[:, :, half:LANES])
    grad_query = flat(grad_tokens[:, :, LANES : LANES + QUERY_COLS])
    grad_normed_in = nt(jnp.concatenate([grad_query, grad_key, grad_value], axis=1), full_in)
    for grad, first, second in (
        (grad_query, query_first, query_second),
        (grad_key, key_first, lock_final_matrices),
        (grad_value, value_first, content_final_matrices),
    ):
        grad_inner_in = (LOW_FACTORED * nt(grad, elected(second))).astype(bf16)
        grad_normed_in = grad_normed_in + nn(grad_inner_in, elected(first))
    tokens_grad = (
        grad_mid + norm_back(rows_in, factor_in, attn_gain, grad_normed_in)
    ).astype(bf16)[None]

    wide = width // cohort
    own = jnp.concatenate(
        [grad_own_firsts[: 3 * RANK], grad_output_first, grad_output_second], axis=0
    ).astype(bf16)
    pieces = jnp.transpose(own.reshape(5 * RANK, cohort, wide), (1, 0, 2))
    summed = lax.all_to_all(pieces, "ctx", 0, 0, tiled=True).astype(f32).sum(0).astype(bf16)
    span = max(wide, QUERY_COLS)
    seconds_in = grad_own_seconds.astype(bf16)
    query_part = seconds_in[:RANK, LANES : LANES + QUERY_COLS]
    key_part = seconds_in[RANK : 2 * RANK, :half]
    value_part = seconds_in[2 * RANK : 3 * RANK, half:LANES]

    def fit(array):
        return jnp.pad(array, ((0, 0), (0, span - array.shape[1])))

    slip = jnp.concatenate(
        [fit(summed), fit(query_part), fit(key_part), fit(value_part)],
        axis=0,
    )
    groups = jnp.stack(gather_shifted(slip, "exp", sources))
    gathered, spot = gather_cohort(groups.reshape(-1, span), cohort)
    gathered = gathered[spot].reshape(cohort, sources, 8 * RANK, span)
    choice = (
        source_adapters[:, None] == jnp.arange(NUM_CHOICES_X, dtype=jnp.int32)[None, :]
    ).astype(f32)

    def to_adapters(array):
        total = 0.0
        for source in range(sources):
            factor = choice[source].reshape((NUM_CHOICES_X,) + (1,) * (array.ndim - 1))
            total = total + factor * array[source][None].astype(f32)
        return total

    def wide_table(index):
        part = gathered[:, :, index * RANK : (index + 1) * RANK, :wide]
        return to_adapters(jnp.transpose(part, (1, 2, 0, 3)).reshape(sources, RANK, width))

    def slim_table(row, start, size):
        part = gathered[:, :, row : row + RANK, start : start + size].astype(f32)
        part = part.reshape(PAIRED_ATTENDERS, ways, sources, RANK, size).sum(1)
        return to_adapters(jnp.transpose(part, (1, 2, 0, 3)).reshape(sources, RANK, -1))

    query_table = slim_table(5 * RANK, 0, QUERY_COLS)
    key_table = slim_table(6 * RANK, 0, half)
    value_table = slim_table(7 * RANK, 0, half)

    inner_size = sigmoid_matrices.shape[2]
    slim = inner_size // cohort
    table_rows = jnp.transpose(
        table_rows.reshape(experts, sources, RANK, -1), (1, 0, 2, 3)
    )

    def expert_table(start, size):
        return to_adapters(table_rows[..., start : start + size])

    return (
        block_out,
        tokens_grad,
        wide_table(0),
        query_table,
        wide_table(1),
        key_table,
        wide_table(2),
        value_table,
        wide_table(3),
        wide_table(4),
        expert_table(0, wide),
        expert_table(3 * wide, slim),
        expert_table(wide, wide),
        expert_table(3 * wide + slim, slim),
        expert_table(3 * wide + 2 * slim, slim),
        expert_table(2 * wide, wide),
    )


def solution(mesh):
    sharded = P("exp", "ctx", None)
    rows = P(("ctx", "exp"), None)
    table = P(None, "exp", None, None)
    expert = P("exp", None, None)
    in_specs = (
        (sharded, sharded, P(), P())
        + (rows,) * 4
        + (expert,) * 3
        + (P("exp", "ctx"), sharded, sharded, P())
        + (P(),) * 8
        + (table,) * 6
    )
    out_specs = (sharded, sharded) + (P(),) * 8 + (P(None, "exp", None, "ctx"),) * 6
    return jax.shard_map(body, mesh=mesh, in_specs=in_specs, out_specs=out_specs, check_vma=False)
```

```python
import functools

import jax
import jax.numpy as jnp
from jax import lax
from jax.experimental import pallas as pl
from jax.experimental.pallas import tpu as pltpu
from jax.sharding import PartitionSpec as P

ASKING_ATTENDERS = 24
PAIRED_ATTENDERS = 8
ATTENTION_EXTENT = 64
HEADS_PER_PAIR = ASKING_ATTENDERS // PAIRED_ATTENDERS
QUERY_COLS = HEADS_PER_PAIR * ATTENTION_EXTENT
EXPERTS = 40
TOPK = 8
NUM_CHOICES_X = 8
CAP = 48
RANK = 16
LANES = 128

EPS = 1e-06
LOW_FACTORED = 2.0
MASKED_FLOOR = -1e30
SCALE = 0.125
VMEM_LIMIT = 56 * 1024 * 1024

bf16 = jnp.bfloat16
f32 = jnp.float32

HEAD_COLS = 384


def nn(left, right):
    return jnp.dot(left, right, preferred_element_type=f32)


def nt(left, right):
    return lax.dot_general(left, right, (((1,), (1,)), ((), ())), preferred_element_type=f32)


def tn(left, right):
    return lax.dot_general(left, right, (((0,), (0,)), ((), ())), preferred_element_type=f32)


def normed(rows, gain):
    factor = lax.rsqrt(jnp.mean(rows * rows, axis=-1, keepdims=True) + EPS)
    return rows * factor * gain, factor


def norm_back(rows, factor, gain, adjoint):
    weighted = adjoint * gain
    central = jnp.mean(weighted * rows, axis=-1, keepdims=True)
    return factor * (weighted - rows * factor * factor * central)


def whole_block(shape):
    return pl.BlockSpec(shape, lambda *ids: (0,) * len(shape))


def call_params(axes=1):
    return pltpu.CompilerParams(
        dimension_semantics=("arbitrary",) * axes, vmem_limit_bytes=VMEM_LIMIT
    )


def key_mask(seg_col, seg_row, tile, start, kmax):
    key_place = lax.broadcasted_iota(jnp.int32, (kmax, tile), 0)
    query_place = start + lax.broadcasted_iota(jnp.int32, (kmax, tile), 1)
    key_seg = seg_col[pl.ds(0, kmax), :]
    query_seg = seg_row[0:1, pl.ds(start, tile)]
    same = (key_seg == query_seg) | (key_seg == 0.0)
    return (key_place <= query_place) & same


def block_rows(spot, rows):
    return pl.ds(pl.multiple_of(spot * rows, rows), rows)


def whole_call(kernel, scalars, arrays, out_shape, scratch=(), flops=0, exps=0, name=None):
    size = sum(v.size * v.dtype.itemsize for v in (*arrays, *out_shape))
    return pl.pallas_call(
        kernel,
        grid_spec=pltpu.PrefetchScalarGridSpec(
            num_scalar_prefetch=len(scalars),
            grid=(1,),
            in_specs=[whole_block(v.shape) for v in arrays],
            out_specs=[whole_block(v.shape) for v in out_shape],
            scratch_shapes=list(scratch),
        ),
        out_shape=list(out_shape),
        compiler_params=call_params(),
        cost_estimate=pl.CostEstimate(flops=flops, bytes_accessed=size, transcendentals=exps),
        name=name,
    )(*scalars, *arrays)


def struct(*shape, dtype=bf16):
    return jax.ShapeDtypeStruct(shape, dtype)


def project_attend_kernel(ways, sides, spots_ref, *refs):
    side_refs = refs[:sides]
    (
        w_ref, first_ref, second_ref, qkv_ref, inner_ref, att_ref, lse_ref, seg_col, seg_row, turned
    ) = refs[sides:]
    rows = side_refs[0].shape[1]
    width = first_ref.shape[1]
    slot = 0
    for side in side_refs:
        count = side.shape[0]
        x = side[...].reshape(count * rows, side.shape[2])
        inner = nt(x[:, :width], first_ref[...]).astype(bf16)
        qkv = nn(x[:, :width], w_ref[...]) + LOW_FACTORED * nn(inner, second_ref[...])
        qkv = qkv.astype(bf16)
        for index in range(count):
            own = slice(index * rows, (index + 1) * rows)
            here = block_rows(spots_ref[slot], rows)
            qkv_ref[here, :] = qkv[own]
            inner_ref[here, :] = inner[own]
            turned[:, here] = qkv[own].astype(f32).T.astype(bf16)
            segments = x[own, width:].astype(f32)
            seg_col[here, :] = segments[:, 0:1]
            seg_row[:, here] = segments.T[0:8, :]
            slot += 1
    part = spots_ref[slot]
    if ways > 1:
        att_ref[...] = jnp.zeros_like(att_ref)
        lse_ref[...] = jnp.zeros_like(lse_ref)
    per_tile = 2 if ways == 1 else 1
    tile = per_tile * rows
    for index in range(slot // ways // per_tile):
        kmax = (index + 1) * per_tile * ways * rows
        first_block = index * per_tile * ways + part if ways > 1 else index * per_tile
        start = pl.multiple_of(first_block * rows, rows) if ways > 1 else first_block * rows
        allowed = key_mask(seg_col, seg_row, tile, start, kmax)
        keys = qkv_ref[pl.ds(0, kmax), 0:LANES]
        values_t = turned[ATTENTION_EXTENT:LANES, pl.ds(0, kmax)]
        outs = []
        sums = []
        for head in range(HEADS_PER_PAIR):
            base = LANES + head * ATTENTION_EXTENT
            q_t = turned[base : base + ATTENTION_EXTENT, pl.ds(start, tile)] * SCALE
            q_pad = jnp.concatenate([q_t, jnp.zeros_like(q_t)], axis=0)
            score = jnp.where(allowed, nn(keys, q_pad), MASKED_FLOOR)
            top = jnp.max(score, axis=0, keepdims=True)
            weight = jnp.exp(score - top)
            total = jnp.sum(weight, axis=0, keepdims=True)
            prob = (weight * (1.0 / total)).astype(bf16)
            outs.append(nn(values_t, prob))
            sums.append(top + jnp.log(total))
        packed = jnp.concatenate(outs, axis=0).astype(bf16)
        for block in range(per_tile):
            att_ref[first_block + block] = packed[:, block * rows : (block + 1) * rows]
        lse_ref[:, pl.ds(start, tile)] = jnp.concatenate(
            sums + [jnp.zeros((8 - HEADS_PER_PAIR, tile), f32)], axis=0
        )


def project_attend(spots, x_sides, weights, first, second, ways):
    blocks, rows = sum(v.shape[0] for v in x_sides), x_sides[0].shape[1]
    total = blocks * rows
    return whole_call(
        functools.partial(project_attend_kernel, ways, len(x_sides)),
        (spots,),
        (*x_sides, weights, first, second),
        (
            struct(total, HEAD_COLS), struct(total, first.shape[0]),
            struct(blocks, QUERY_COLS, rows), struct(8, total, dtype=f32),
            struct(total, 1, dtype=f32), struct(8, total, dtype=f32),
        ),
        scratch=(pltpu.VMEM((HEAD_COLS, total), bf16),),
        flops=2 * total * first.shape[1] * 512 + 8 * total * total * 256,
        exps=HEADS_PER_PAIR * total * total,
        name="project_attend",
    )


def attend_back_kernel(ways, sides, spots_ref, *refs):
    (
        qkv_ref, adj_ref, lse_ref, second_ref, inner_ref, seg_col, seg_row, w_ref, first_ref
    ) = refs[:9]
    side_refs, rows_refs = refs[9 : 9 + sides], refs[9 + sides : 9 + 2 * sides]
    firsts_ref, seconds_ref, grad_ref, turned, adj_turned, grad_kv = refs[9 + 2 * sides :]
    blocks, rows = adj_ref.shape[0], adj_ref.shape[2]
    half = ATTENTION_EXTENT
    width = first_ref.shape[1]
    part = spots_ref[blocks]
    for index in range(blocks):
        here = pl.ds(index * rows, rows)
        turned[:, here] = qkv_ref[here, :].astype(f32).T.astype(bf16)
        adj_turned[:, here] = adj_ref[index]
    grad_kv[...] = jnp.zeros_like(grad_kv)
    if ways > 1:
        grad_ref[...] = jnp.zeros_like(grad_ref)
    per_tile = 2 if ways == 1 else 1
    tile = per_tile * rows
    zero = jnp.zeros((half, tile), bf16)
    for index in range(blocks // ways // per_tile):
        kmax = (index + 1) * per_tile * ways * rows
        start = index * tile
        if ways > 1:
            start = pl.multiple_of((index * per_tile * ways + part) * rows, rows)
        allowed = key_mask(seg_col, seg_row, tile, start, kmax)
        keys = qkv_ref[pl.ds(0, kmax), 0:LANES]
        keys_t = turned[0:half, pl.ds(0, kmax)]
        grads_q = []
        update = jnp.zeros((kmax, LANES), f32)
        for head in range(HEADS_PER_PAIR):
            base = LANES + head * half
            q_t = turned[base : base + half, pl.ds(start, tile)] * SCALE
            q_pad = jnp.concatenate([q_t, zero], axis=0)
            a_t = adj_turned[head * half : (head + 1) * half, pl.ds(start, tile)]
            a_pad = jnp.concatenate([zero, a_t], axis=0)
            score = nn(keys, q_pad) - lse_ref[head : head + 1, pl.ds(start, tile)]
            prob = jnp.where(allowed, jnp.exp(jnp.where(allowed, score, 0.0)), 0.0)
            grad_prob = nn(keys, a_pad)
            both = prob * grad_prob
            delta = jnp.sum(both, axis=0, keepdims=True)
            grad_score = (both - prob * delta).astype(bf16)
            update = update + nt(grad_score, q_pad) + nt(prob.astype(bf16), a_pad)
            grads_q.append(nn(keys_t, grad_score) * SCALE)
        grad_kv[pl.ds(0, kmax), :] += update
        packed = jnp.concatenate(grads_q + [jnp.zeros((half, tile), f32)], axis=0)
        grad_ref[pl.ds(start, tile), LANES:] = packed.T.astype(bf16)
    grad_ref[:, 0:LANES] = grad_kv[...].astype(bf16)

    slot = 0
    grad_first = None
    for side, rows_ref in zip(side_refs, rows_refs):
        count = side.shape[0]
        grad = jnp.concatenate(
            [grad_ref[block_rows(spots_ref[slot + i], rows), :] for i in range(count)], axis=0
        )
        grad_inner = (LOW_FACTORED * nt(grad, second_ref[...])).astype(bf16)
        out = nt(grad, w_ref[...]) + nn(grad_inner, first_ref[...])
        rows_ref[...] = out.astype(bf16).reshape(count, rows, width)
        x = side[...].reshape(count * rows, side.shape[2])[:, :width]
        term = tn(grad_inner, x)
        grad_first = term if grad_first is None else grad_first + term
        slot += count
    wide, span = width // blocks, firsts_ref.shape[2]
    for place in range(blocks):
        firsts_ref[place] = padded(grad_first[:, place * wide : (place + 1) * wide], span)
    seconds = LOW_FACTORED * tn(inner_ref[...], grad_ref[...])
    for index, low, size in ((0, LANES, QUERY_COLS), (1, 0, half), (2, half, half)):
        own = slice(index * RANK, (index + 1) * RANK)
        seconds_ref[own, :] = padded(seconds[own, low : low + size], span)


def padded(piece, span):
    rows, size = piece.shape
    if size < span:
        piece = jnp.concatenate([piece, jnp.zeros((rows, span - size), piece.dtype)], axis=1)
    return piece.astype(bf16)


def attend_back(
    spots, qkv, adj, lse, second, inner, seg_col, seg_row, weights, first, x_sides, span, ways
):
    blocks, rows = adj.shape[0], adj.shape[2]
    total, width = qkv.shape[0], first.shape[1]
    return whole_call(
        functools.partial(attend_back_kernel, ways, len(x_sides)),
        (spots,),
        (qkv, adj, lse, second, inner, seg_col, seg_row, weights, first, *x_sides),
        [struct(v.shape[0], rows, width) for v in x_sides]
        + [struct(blocks, 3 * RANK, span), struct(3 * RANK, span)],
        scratch=(
            pltpu.VMEM((total, HEAD_COLS), bf16),
            pltpu.VMEM((HEAD_COLS, total), bf16),
            pltpu.VMEM((QUERY_COLS, total), bf16),
            pltpu.VMEM((total, LANES), f32),
        ),
        flops=20 * total * total * 256 + 2 * total * width * 512,
        exps=HEADS_PER_PAIR * total * total,
        name="attend_back",
    )


def side_blocks(side_refs):
    slot = 0
    for side in side_refs:
        for index in range(side.shape[0]):
            yield slot, side[index]
            slot += 1


def output_project_kernel(sides, spots_ref, *refs):
    side_refs = refs[:sides]
    att_ref, first_ref, second_ref, rows_ref, gain_ref, mid_ref, normed_ref, inner_ref = refs[sides:]
    total = rows_ref[...].astype(f32)
    inner = None
    for slot, weights in side_blocks(side_refs):
        att = att_ref[spots_ref[slot]]
        total = total + tn(att, weights)
    for index in range(att_ref.shape[0]):
        term = tn(att_ref[index], first_ref[index])
        inner = term if inner is None else inner + term
    inner = inner.astype(bf16)
    mid = total + LOW_FACTORED * nn(inner, second_ref[...])
    mid_ref[...] = mid
    inner_ref[...] = inner
    low = normed(mid, gain_ref[...])[0].astype(bf16)
    for index in range(normed_ref.shape[0]):
        normed_ref[index] = low


def output_project(spots, w_sides, att, first, second, rows, gain, sources):
    count, width = rows.shape
    return whole_call(
        functools.partial(output_project_kernel, len(w_sides)),
        (spots,),
        (*w_sides, att, first, second, rows, gain),
        (struct(count, width, dtype=f32), struct(sources, count, width), struct(count, LANES)),
        flops=2 * count * width * width,
        name="output_project",
    )


def output_back_kernel(sides, spots_ref, *refs):
    side_refs = refs[:sides]
    (
        parts_ref, mid_ref, gain_ref, out_grad_ref, att_ref, first_ref, second_ref, inner_ref,
        adj_ref, tables_ref, grad_mid_ref,
    ) = refs[sides:]
    grad = parts_ref[0].astype(f32)
    for index in range(1, parts_ref.shape[0]):
        grad = grad + parts_ref[index].astype(f32)
    mid = mid_ref[...]
    factor = lax.rsqrt(jnp.mean(mid * mid, axis=-1, keepdims=True) + EPS)
    grad_mid = out_grad_ref[...].astype(f32) + norm_back(mid, factor, gain_ref[...], grad)
    grad_mid_ref[...] = grad_mid
    branch = grad_mid.astype(bf16)
    grad_inner = (LOW_FACTORED * nt(branch, second_ref[...])).astype(bf16)
    for slot, weights in side_blocks(side_refs):
        spot = spots_ref[slot]
        adj_ref[spot] = (nt(weights, branch) + nt(first_ref[spot], grad_inner)).astype(bf16)
    seconds = LOW_FACTORED * tn(inner_ref[...], branch)
    wide, span = att_ref.shape[1], tables_ref.shape[2]
    for place in range(att_ref.shape[0]):
        firsts = nn(att_ref[place], grad_inner).T
        tables_ref[place, 0:RANK, :] = padded(firsts[0:RANK], span)
        piece = seconds[0:RANK, place * wide : (place + 1) * wide]
        tables_ref[place, RANK:, :] = padded(piece, span)


def output_back(spots, w_sides, parts, mid, gain, out_grad, att, first, second, inner, span):
    count, width = mid.shape
    return whole_call(
        functools.partial(output_back_kernel, len(w_sides)),
        (spots,),
        (*w_sides, parts, mid, gain, out_grad, att, first, second, inner),
        (
            struct(*att.shape), struct(att.shape[0], 2 * RANK, span),
            struct(count, width, dtype=f32),
        ),
        flops=2 * count * width * width,
        name="output_back",
    )


def attend_tables_kernel(ways, sides, place_ref, adapter_ref, *refs):
    side_refs, out_refs = refs[:sides], refs[sides:]
    per_side, sources = side_refs[0].shape[0], side_refs[0].shape[1] // (8 * RANK)
    blocks = per_side * sides
    wide = out_refs[0].shape[2] // blocks
    half = ATTENTION_EXTENT

    def read(place, rows):
        slot = place_ref[place]
        value = side_refs[0][lax.rem(slot, per_side), rows, :]
        if sides > 1:
            value = jnp.where(slot < per_side, value, side_refs[1][lax.rem(slot, per_side), rows, :])
        return value.astype(f32)

    for out_ref in out_refs:
        out_ref[...] = jnp.zeros_like(out_ref)
    for source in range(sources):
        adapter = adapter_ref[source]
        for index, out_ref in enumerate(out_refs):
            rows = pl.ds((source * 8 + index) * RANK, RANK)
            pieces = [read(c, rows) for c in range(blocks)]
            if index < 5:
                size = wide
            else:
                size = QUERY_COLS if index == 5 else half
                pieces = [
                    sum(pieces[h * ways + 1 : (h + 1) * ways], pieces[h * ways])
                    for h in range(PAIRED_ATTENDERS)
                ]
            joined = jnp.concatenate([piece[:, :size] for piece in pieces], axis=1)
            out_ref[adapter] = out_ref[adapter] + joined


def attend_tables(place, adapters, sides, width, ways):
    key_cols = PAIRED_ATTENDERS * ATTENTION_EXTENT
    cols = (width,) * 5 + (ASKING_ATTENDERS * ATTENTION_EXTENT, key_cols, key_cols)
    return whole_call(
        functools.partial(attend_tables_kernel, ways, len(sides)),
        (place, adapters),
        sides,
        [struct(NUM_CHOICES_X, RANK, size, dtype=f32) for size in cols],
        name="attend_tables",
    )


def expert_tables_kernel(sizes, sources, adapter_ref, rows_ref, *out_refs):
    adapter = pl.program_id(0)
    for out_ref in out_refs:
        out_ref[...] = jnp.zeros_like(out_ref)
    for source in range(sources):

        @pl.when(adapter_ref[source] == adapter)
        def _():
            for expert in range(rows_ref.shape[0]):
                own = rows_ref[expert, source * RANK : (source + 1) * RANK, :].astype(f32)
                start = 0
                for size, out_ref in zip(sizes, out_refs):
                    out_ref[0, expert] += own[:, start : start + size]
                    start += size


def expert_tables(adapters, rows, wide, slim):
    experts, sources = rows.shape[0], adapters.shape[0]
    sizes = (wide,) * 3 + (slim,) * 3
    return pl.pallas_call(
        functools.partial(expert_tables_kernel, sizes, sources),
        grid_spec=pltpu.PrefetchScalarGridSpec(
            num_scalar_prefetch=1,
            grid=(NUM_CHOICES_X,),
            in_specs=[whole_block(rows.shape)],
            out_specs=[
                pl.BlockSpec((1, experts, RANK, size), lambda a, adapters: (a, 0, 0, 0))
                for size in sizes
            ],
        ),
        out_shape=[
            jax.ShapeDtypeStruct((NUM_CHOICES_X, experts, RANK, size), f32) for size in sizes
        ],
        compiler_params=call_params(),
        name="expert_tables",
    )(adapters, rows)


def source_mask(shape, sources):
    row = lax.broadcasted_iota(jnp.int32, shape, 0)
    col = lax.broadcasted_iota(jnp.int32, shape, 1)
    keep = None
    for source in range(sources):
        inside = (row >= source * CAP) & (row < (source + 1) * CAP)
        inside &= (lax.rem(col, sources * RANK) >= source * RANK) & (
            lax.rem(col, sources * RANK) < (source + 1) * RANK
        )
        keep = inside if keep is None else keep | inside
    return keep


def masked(values, sources):
    return jnp.where(source_mask(values.shape, sources), values, 0.0)


def picks(slot_ref, pair, tokens):
    slots = slot_ref[0, :, pair * 2 * tokens : (pair + 1) * 2 * tokens]
    place = lax.broadcasted_iota(jnp.int32, (2 * CAP, 2 * tokens), 0)
    return place == slots


def picked_rows(slot_ref, rows_ref, sources):
    tokens = rows_ref.shape[0] // sources
    parts = []
    for pair in range(sources // 2):
        pick = picks(slot_ref, pair, tokens).astype(f32).astype(bf16)
        rows = rows_ref[pair * 2 * tokens : (pair + 1) * 2 * tokens, :]
        parts.append(nn(pick, rows))
    return jnp.concatenate(parts, axis=0)


def picked_gates(slot_ref, gate_ref, sources):
    tokens = gate_ref.shape[2] // sources
    parts = []
    for pair in range(sources // 2):
        gate = gate_ref[0, :, pair * 2 * tokens : (pair + 1) * 2 * tokens]
        kept = jnp.where(picks(slot_ref, pair, tokens), gate, 0.0)
        parts.append(jnp.sum(kept, axis=1, keepdims=True))
    return jnp.concatenate(parts, axis=0)


def combine(target_ref, values, out_ref, sources):
    tokens = target_ref.shape[0] // sources
    slots = values.shape[1]
    for source in range(sources):
        target = target_ref[source * tokens : (source + 1) * tokens, :]
        place = lax.broadcasted_iota(jnp.int32, (tokens, slots), 1)
        hit = place == target[:, 0:1]
        for choice in range(1, TOPK):
            hit |= place == target[:, choice : choice + 1]
        out_ref[source] = nn(hit.astype(f32).astype(bf16), values[source]).astype(bf16)


def combine_ring(place, target_ref, values, out_refs):
    sources = len(out_refs)
    tokens = target_ref.shape[0] // sources
    slots = values.shape[1]
    for shift, out_ref in enumerate(out_refs):
        source = lax.rem(place + shift, sources)
        target = target_ref[pl.ds(pl.multiple_of(source * tokens, tokens), tokens), :]
        column = lax.broadcasted_iota(jnp.int32, (tokens, slots), 1)
        hit = column == target[:, 0:1]
        for choice in range(1, TOPK):
            hit |= column == target[:, choice : choice + 1]
        out_ref[...] = nn(hit.astype(f32).astype(bf16), values[source]).astype(bf16)


def keep_rows(values, rows, expert, sources):
    for source in range(sources):
        values[source, pl.ds(pl.multiple_of(expert * CAP, CAP), CAP), :] = rows[
            source * CAP : (source + 1) * CAP
        ]


def joined(refs):
    return jnp.concatenate([ref[0, 0] for ref in refs], axis=0)


def experts_pre_kernel(sources, adapter_ref, slot_ref, gate_ref, grads_ref, down_ref, *refs):
    down_first, down_second = joined(refs[:sources]), joined(refs[sources : 2 * sources])
    picked_ref, hidden_ref, inner_ref = refs[2 * sources :]
    grads = picked_rows(slot_ref, grads_ref, sources)
    grads = (grads * picked_gates(slot_ref, gate_ref, sources)).astype(bf16)
    picked_ref[0] = grads
    inner = LOW_FACTORED * nt(grads, down_second)
    inner = masked(inner, sources).astype(bf16)
    inner_ref[0] = inner
    hidden_ref[0] = nt(grads, down_ref[0]) + nn(inner, down_first)


def experts_main_kernel(
    sources, adapter_ref, slot_ref, x_ref, gate_w, up_w, grad_hidden, target_ref, *refs
):
    groups = [refs[i * sources : (i + 1) * sources] for i in range(4)]
    picked_ref, hidden_ref, adj_ref, inner_ref, out_ref, values = refs[4 * sources :]
    firsts = jnp.concatenate([joined(groups[0]), joined(groups[1])], axis=0)
    gate_second, up_second = joined(groups[2]), joined(groups[3])
    blank = jnp.zeros_like(gate_second)
    seconds = jnp.concatenate(
        [
            jnp.concatenate([gate_second, blank], axis=1),
            jnp.concatenate([blank, up_second], axis=1),
        ],
        axis=0,
    )
    expert = pl.program_id(0)
    inner_size = gate_w.shape[2]
    x = picked_rows(slot_ref, x_ref, sources).astype(bf16)
    picked_ref[0] = x
    inner = masked(nt(x, firsts), sources).astype(bf16)
    added = LOW_FACTORED * nn(inner, seconds)
    gate = nn(x, gate_w[0]) + added[:, :inner_size]
    up = nn(x, up_w[0]) + added[:, inner_size:]
    sigma = 1.0 / (1.0 + jnp.exp(-gate))
    active = gate * sigma
    hidden_ref[0] = (active * up).astype(bf16)
    adj = grad_hidden[0]
    grad_gate = (adj * up * sigma * (1.0 + gate * (1.0 - sigma))).astype(bf16)
    grad_up = (adj * active).astype(bf16)
    both = jnp.concatenate([grad_gate, grad_up], axis=1)
    adj_ref[0] = both
    grad_inner = masked(LOW_FACTORED * nt(both, seconds), sources).astype(bf16)
    inner_ref[0] = jnp.concatenate([inner, grad_inner], axis=1)
    rows = nt(grad_gate, gate_w[0]) + nt(grad_up, up_w[0]) + nn(grad_inner, firsts)
    keep_rows(values, rows.astype(bf16), expert, sources)

    @pl.when(expert == pl.num_programs(0) - 1)
    def _():
        combine(target_ref, values, out_ref, sources)


def experts_post_kernel(
    sources, cohort, adapter_ref, slot_ref, gate_ref, down_ref, picked_ref, hidden_ref, adj_ref,
    inner_ref, picked_grads, grad_inner_down, target_ref, *refs
):
    down_first, down_second = joined(refs[:sources]), joined(refs[sources : 2 * sources])
    table_ref, *out_refs, values = refs[2 * sources :]
    expert = pl.program_id(0)
    span = sources * RANK
    hidden = hidden_ref[0]
    inner_down = masked(nt(hidden, down_first), sources).astype(bf16)
    answer = nn(hidden, down_ref[0]) + LOW_FACTORED * nn(inner_down, down_second)
    answer = answer.astype(bf16).astype(f32) * picked_gates(slot_ref, gate_ref, sources)
    keep_rows(values, answer.astype(bf16), expert, sources)
    width = picked_ref.shape[2]
    inner_size = hidden.shape[1]
    inner = inner_ref[0, :, : 2 * span]
    grad_inner = inner_ref[0, :, 2 * span :]
    firsts = tn(grad_inner, picked_ref[0])
    seconds = LOW_FACTORED * tn(inner, adj_ref[0])
    down_firsts = tn(grad_inner_down[0], hidden)
    down_seconds = LOW_FACTORED * tn(inner_down, picked_grads[0])
    wide, slim = width // cohort, inner_size // cohort
    wide_parts = (firsts[:span], firsts[span:], down_seconds)
    slim_parts = (seconds[:span, :inner_size], seconds[span:, inner_size:], down_firsts)
    for place in range(cohort):
        pieces = [v[:, place * wide : (place + 1) * wide] for v in wide_parts]
        pieces += [v[:, place * slim : (place + 1) * slim] for v in slim_parts]
        table_ref[place, 0] = jnp.concatenate(pieces, axis=1).astype(bf16)

    @pl.when(expert == pl.num_programs(0) - 1)
    def _():
        combine_ring(adapter_ref[sources], target_ref, values, out_refs)


def per_expert(array):
    rest = array.shape[1:]
    return pl.BlockSpec((1,) + rest, lambda e, *_: (e,) + (0,) * len(rest))


def expert_rows(rows, width):
    return pl.BlockSpec((1, rows, width), lambda e, *_: (e, 0, 0))


def adapter_blocks(table, sources):
    shape = (1, 1) + table.shape[2:]
    return [
        pl.BlockSpec(shape, lambda e, adapters, s=s: (adapters[s], e, 0, 0))
        for s in range(sources)
    ]


def expert_call(
    kernel, sources, adapters, arrays, specs, tables, out_shape, out_specs, scratch, flops, name
):
    size = sum(v.size * v.dtype.itemsize for v in (*arrays, *out_shape))
    return pl.pallas_call(
        kernel,
        grid_spec=pltpu.PrefetchScalarGridSpec(
            num_scalar_prefetch=1,
            grid=(out_shape[0].shape[0 if len(out_shape[0].shape) == 3 else 1],),
            in_specs=specs + [spec for t in tables for spec in adapter_blocks(t, sources)],
            out_specs=out_specs,
            scratch_shapes=scratch,
        ),
        out_shape=out_shape,
        compiler_params=call_params(),
        cost_estimate=pl.CostEstimate(flops=flops, bytes_accessed=size, transcendentals=0),
        name=name,
    )(adapters, *arrays, *[t for t in tables for _ in range(sources)])


def experts_pre(adapters, slots, gates, grads, down, down_first, down_second):
    experts, inner_size, width = down.shape
    sources = adapters.shape[0]
    rows = sources * CAP
    return expert_call(
        functools.partial(experts_pre_kernel, sources),
        sources,
        adapters,
        (slots, gates, grads, down),
        [
            per_expert(slots), per_expert(gates), whole_block((grads.shape[0], width)),
            per_expert(down),
        ],
        (down_first, down_second),
        [
            struct(experts, rows, width), struct(experts, rows, inner_size, dtype=f32),
            struct(experts, rows, sources * RANK),
        ],
        [expert_rows(rows, v) for v in (width, inner_size, sources * RANK)],
        [],
        2 * experts * rows * width * inner_size * 2,
        "experts_pre",
    )


def experts_main(
    adapters, slots, x, gate_w, up_w, grad_hidden, target, gate_first, up_first, gate_second,
    up_second,
):
    experts, width, inner_size = gate_w.shape
    sources = adapters.shape[0]
    rows = sources * CAP
    tokens = x.shape[0] // sources
    outs = (width, inner_size, 2 * inner_size, 4 * sources * RANK)
    return expert_call(
        functools.partial(experts_main_kernel, sources),
        sources,
        adapters,
        (slots, x, gate_w, up_w, grad_hidden, target),
        [
            per_expert(slots), whole_block(x.shape), per_expert(gate_w), per_expert(up_w),
            per_expert(grad_hidden), whole_block(target.shape),
        ],
        (gate_first, up_first, gate_second, up_second),
        [struct(experts, rows, v) for v in outs] + [struct(sources, tokens, width)],
        [expert_rows(rows, v) for v in outs] + [whole_block((sources, tokens, width))],
        [pltpu.VMEM((sources, experts * CAP, width), bf16)],
        2 * experts * rows * width * inner_size * 5,
        "experts_main",
    )


def experts_post(
    adapters, slots, gates, down, picked, hidden, adj, inner, picked_grads, grad_inner_down,
    target, down_first, down_second, cohort,
):
    experts, inner_size, width = down.shape
    sources = adapters.shape[0] - 1
    tokens = target.shape[0] // sources
    lanes = 3 * (width + inner_size) // cohort
    arrays = (
        slots, gates, down, picked, hidden, adj, inner, picked_grads, grad_inner_down
    )
    return expert_call(
        functools.partial(experts_post_kernel, sources, cohort),
        sources,
        adapters,
        arrays + (target,),
        [per_expert(v) for v in arrays] + [whole_block(target.shape)],
        (down_first, down_second),
        [struct(cohort, experts, sources * RANK, lanes)] + [struct(tokens, width)] * sources,
        [
            pl.BlockSpec((cohort, 1, sources * RANK, lanes), lambda e, *_: (0, e, 0, 0)),
        ]
        + [whole_block((tokens, width))] * sources,
        [pltpu.VMEM((sources, experts * CAP, width), bf16)],
        2 * experts * sources * CAP * width * inner_size * 2,
        "experts_post",
    )


def flipped(array, axis, size, mask):
    return lax.ppermute(array, axis, [(i, i ^ mask) for i in range(size)])


def ring_blocks(array, axis, size):
    return [array] + [
        lax.ppermute(array, axis, [(i, (i + shift) % size) for i in range(size)])
        for shift in range(1, size)
    ]


def to_every(array, axis, size):
    return lax.all_to_all(
        jnp.broadcast_to(array[None], (size,) + array.shape), axis, 0, 0, tiled=True
    )


def cohort_spots(size):
    place = jnp.arange(size, dtype=jnp.int32)
    if size != 8:
        return place, place
    me = lax.axis_index("ctx")
    mask = place ^ me
    return (place % 4 * 2 + place // 4) ^ me, (mask & 1) * 4 + mask // 2


def gather_cohort(array, size, stage=lambda blocks: blocks):
    if size != 8:
        return (lax.all_gather(array, "ctx", axis=0, tiled=False),)
    blocks = stage([flipped(array, "ctx", size, mask) for mask in (2, 4, 6)])
    mine = jnp.stack([array] + blocks)
    return mine, flipped(mine, "ctx", size, 1)


class scatter_cohort:
    def __init__(self, sides, size):
        self.steps = self.run(sides, size)
        self.waiting = next(self.steps)

    def stage(self, beside):
        self.waiting, beside = lax.optimization_barrier((self.waiting, beside))
        self.waiting = self.steps.send(self.waiting)
        return beside

    def result(self):
        return self.waiting

    @staticmethod
    def run(sides, size):
        if size != 8:
            total = lax.psum_scatter(sides[0], "ctx", scatter_dimension=0, tiled=False)
            while True:
                total = yield total.astype(f32)
        half = sides[0].shape[1] // 2

        def plus(left, right):
            return (left.astype(f32) + right.astype(f32)).astype(bf16)

        other = yield flipped(sides[1], "ctx", size, 1)
        mine = plus(sides[0], other)
        low, high = mine[:, :half], mine[:, half:]
        near, far = yield (
            flipped(jnp.stack([low[1], low[3]]), "ctx", size, 2),
            flipped(jnp.stack([high[2], high[3]]), "ctx", size, 4),
        )
        low_last, high_last = yield (
            flipped(plus(low[2], near[1]), "ctx", size, 4),
            flipped(plus(high[1], far[1]), "ctx", size, 2),
        )
        low_sum = low[0].astype(f32) + near[0].astype(f32) + low_last.astype(f32)
        high_sum = high[0].astype(f32) + far[0].astype(f32) + high_last.astype(f32)
        yield jnp.concatenate([low_sum, high_sum], axis=0)


def head_columns(query, key, value):
    rows = query.shape[0]

    def split(array):
        return jnp.transpose(array.reshape(rows, PAIRED_ATTENDERS, -1), (1, 0, 2))

    parts = [split(key), split(value), split(query)]
    pad = HEAD_COLS - sum(p.shape[2] for p in parts)
    parts.append(jnp.zeros((PAIRED_ATTENDERS, rows, pad), query.dtype))
    return jnp.concatenate(parts, axis=2)


def body(
    tokens, out_grad, attn_gain, moe_gain, w_query, lock_projection, content_projection, w_out,
    sigmoid_matrices, widener_matrices, reducer_matrices, segment_ids, expert_routes,
    route_weights, adapter_index, query_first, query_second, key_first, lock_final_matrices,
    value_first, content_final_matrices, output_first, output_second, gate_first, gate_second,
    upward_first, upward_second, down_first, down_second,
):
    rows_in = tokens[0].astype(f32)
    count, width = rows_in.shape
    cohort = lax.axis_size("ctx")
    sources = lax.axis_size("exp")
    experts = sigmoid_matrices.shape[0]
    ctx = lax.axis_index("ctx")
    exp = lax.axis_index("exp")
    ways = cohort // PAIRED_ATTENDERS
    head = ctx // ways
    adapter = adapter_index[exp]

    def elected(table):
        return lax.dynamic_index_in_dim(table, adapter, 0, keepdims=False)

    attended_cols = ASKING_ATTENDERS * ATTENTION_EXTENT
    wide = width // cohort
    span = -(-max(wide, QUERY_COLS) // LANES) * LANES
    spots, place = cohort_spots(cohort)
    order = jnp.concatenate([spots, (ctx % ways)[None].astype(jnp.int32)])

    normed_in, factor_in = normed(rows_in, attn_gain)
    labels = jnp.pad(segment_ids[0].astype(bf16)[:, None], ((0, 0), (0, LANES - 1)))
    shared = [ring_blocks(w_out, "exp", sources)]

    def beside_out(blocks):
        blocks, shared[0] = lax.optimization_barrier((blocks, shared[0]))
        return blocks

    x_sides = gather_cohort(
        jnp.concatenate([normed_in.astype(bf16), labels], axis=1), cohort, beside_out
    )
    head_w = head_columns(w_query, lock_projection, content_projection)
    to_all = jnp.broadcast_to(
        head_w[:, None], (PAIRED_ATTENDERS, ways * sources) + head_w.shape[1:]
    ).reshape((cohort * sources,) + head_w.shape[1:])
    own_w = lax.all_to_all(to_all, ("ctx", "exp"), 0, 0, tiled=True).reshape(width, HEAD_COLS)
    relative = (exp - jnp.arange(sources, dtype=jnp.int32) + sources) % sources
    out_rows = jnp.stack(shared[0])[relative]

    routes = expert_routes[0].astype(bf16)
    weight_high = route_weights[0].astype(bf16)
    weight_low = (route_weights[0] - weight_high.astype(f32)).astype(bf16)
    parcel = jnp.concatenate(
        [
            out_grad[0], routes, weight_high, weight_low,
            jnp.zeros((count, LANES - 3 * TOPK), bf16),
        ],
        axis=1,
    )
    parcel, own_w = lax.optimization_barrier((parcel, own_w))
    parcels = ring_blocks(parcel, "exp", sources)

    own_firsts = jnp.concatenate(
        [elected(query_first), elected(key_first), elected(value_first)], axis=0
    )

    def head_part(table):
        part = elected(table)
        size = part.shape[1] // PAIRED_ATTENDERS
        return lax.dynamic_slice_in_dim(part, head * size, size, 1)

    def placed(part, row, col):
        return jnp.pad(
            part, ((row, 2 * RANK - row), (col, HEAD_COLS - col - part.shape[1]))
        )

    own_seconds = (
        placed(head_part(query_second), 0, LANES)
        + placed(head_part(lock_final_matrices), RANK, 0)
        + placed(head_part(content_final_matrices), 2 * RANK, ATTENTION_EXTENT)
    )
    qkv, inner, attended, lse, seg_col, seg_row = project_attend(
        order, x_sides, own_w, own_firsts, own_seconds, ways
    )
    shared[0] = lax.all_to_all(attended, "ctx", 0, 0, tiled=True)

    def beside_attention(blocks):
        blocks, shared[0], parcels[:] = lax.optimization_barrier((blocks, shared[0], parcels))
        return blocks

    out_sides = gather_cohort(out_rows.reshape(-1, width), cohort, beside_attention)
    attended = shared[0]
    if ways > 1:
        attended = attended.reshape(PAIRED_ATTENDERS, ways, QUERY_COLS, count)
        attended = attended.astype(f32).sum(1).astype(bf16).reshape(cohort, wide, count)
    out_first = jnp.pad(elected(output_first), ((0, LANES - RANK), (0, 0)))
    out_first = out_first.T.reshape(cohort, wide, LANES)
    out_second = jnp.pad(elected(output_second), ((0, LANES - RANK), (0, 0)))
    mid, normed_mid, inner_out = output_project(
        spots, out_sides, attended, out_first, out_second, tokens[0], moe_gain[None], sources
    )
    x_all = lax.all_to_all(normed_mid, "exp", 0, 0, tiled=True).reshape(sources * count, width)

    parcels, normed_mid = lax.optimization_barrier((parcels, normed_mid))
    parcels = jnp.stack(parcels)[relative].reshape(sources * count, -1)
    extra = parcels[:, width:].astype(f32).reshape(sources, count, -1)
    all_routes = extra[:, :, :TOPK].astype(jnp.int32) - exp * experts
    all_gates = extra[:, :, TOPK : 2 * TOPK] + extra[:, :, 2 * TOPK : 3 * TOPK]
    hits = all_routes[None] == jnp.arange(experts, dtype=jnp.int32)[:, None, None, None]
    named = jnp.any(hits, axis=3)
    gates = jnp.sum(jnp.where(hits, all_gates[None], 0.0), axis=3).reshape(experts, 1, -1)
    earlier = jnp.tril(jnp.ones((count, count), bf16), -1)
    rank = lax.dot_general(
        named.astype(bf16), earlier, (((2,), (1,)), ((), ())), preferred_element_type=f32
    ).astype(jnp.int32)
    side = (jnp.arange(sources, dtype=jnp.int32) % 2 * CAP)[None, :, None]
    slots = jnp.where(named, rank + side, -1).reshape(experts, 1, -1)
    places = jnp.arange(experts, dtype=jnp.int32)[:, None, None] * CAP + rank + 1
    target = jnp.sum(jnp.where(hits, places[..., None], 0), axis=0) - 1
    target = target.reshape(sources * count, TOPK)

    picked_grads, grad_hidden, grad_inner_down = experts_pre(
        adapter_index, slots, gates, parcels, reducer_matrices, down_first, down_second
    )
    picked, hidden, adj, inner_rows, grad_parts = experts_main(
        adapter_index, slots, x_all, sigmoid_matrices, widener_matrices, grad_hidden, target,
        gate_first, upward_first, gate_second, upward_second,
    )
    grad_parts = lax.all_to_all(grad_parts, "exp", 0, 0, tiled=True)
    tables, *answers = experts_post(
        jnp.concatenate([adapter_index, exp[None].astype(jnp.int32)]), slots, gates, reducer_matrices, picked, hidden, adj, inner_rows,
        picked_grads, grad_inner_down, target, down_first, down_second, cohort,
    )
    tables, answers, grad_parts = lax.optimization_barrier((tables, answers, grad_parts))
    answers = answers[:1] + [
        lax.ppermute(answers[shift], "exp", [(i, (i + shift) % sources) for i in range(sources)])
        for shift in range(1, sources)
    ]
    early, middle, last = answers[:2], answers[3:], answers[2:3]
    table_rows = lax.psum_scatter(tables, "ctx", scatter_dimension=0, tiled=False)

    adj_blocks, out_tables, grad_mid = output_back(
        spots, out_sides, grad_parts, mid, moe_gain[None], out_grad[0], attended, out_first,
        out_second, inner_out, span,
    )
    if ways > 1:
        adj_blocks = jnp.repeat(adj_blocks.reshape(-1, QUERY_COLS, count), ways, axis=0)
    adj_all = lax.all_to_all(adj_blocks, "ctx", 0, 0, tiled=True)
    adj_all, early = lax.optimization_barrier((adj_all, early))
    *row_sides, in_tables, grad_seconds = attend_back(
        order, qkv, adj_all, lse, own_seconds, inner, seg_col, seg_row, own_w, own_firsts,
        x_sides, span, ways,
    )
    row_sides, in_tables, middle = lax.optimization_barrier((row_sides, in_tables, middle))

    pieces = jnp.concatenate([in_tables, out_tables], axis=1)
    pieces = lax.all_to_all(pieces, "ctx", 0, 0, tiled=True)
    rows = scatter_cohort(row_sides, cohort)
    pieces = rows.stage(pieces)
    summed = pieces.astype(f32).sum(0).astype(bf16)
    groups = to_every(jnp.concatenate([summed, grad_seconds], axis=0), "exp", sources)
    groups = rows.stage(groups)
    expert_grads = list(
        expert_tables(adapter_index, table_rows, wide, sigmoid_matrices.shape[2] // cohort)
    )

    def last_stage(blocks):
        blocks, *given = rows.stage([blocks, last, *expert_grads])
        last[:], expert_grads[:] = given[0], given[1:]
        return blocks

    group_sides = gather_cohort(groups.reshape(-1, span), cohort, last_stage)
    answers = early + middle + last
    block_out = (mid + sum(v.astype(f32) for v in answers)).astype(bf16)[None]
    grad_normed_in = rows.result()
    tokens_grad = (
        grad_mid + norm_back(rows_in, factor_in, attn_gain, grad_normed_in)
    ).astype(bf16)[None]

    gate_f, up_f, down_s, gate_s, up_s, down_f = expert_grads
    attention_tables = attend_tables(place, adapter_index, group_sides, width, ways)
    query_f, key_f, value_f, out_f, out_s, query_s, key_s, value_s = attention_tables
    return (
        block_out, tokens_grad, query_f, query_s, key_f, key_s, value_f, value_s, out_f, out_s,
        gate_f, gate_s, up_f, up_s, down_f, down_s,
    )


def solution(mesh):
    sharded = P("exp", "ctx", None)
    rows = P(("ctx", "exp"), None)
    table = P(None, "exp", None, None)
    expert = P("exp", None, None)
    in_specs = (
        (sharded, sharded, P(), P())
        + (rows,) * 4
        + (expert,) * 3
        + (P("exp", "ctx"), sharded, sharded, P())
        + (P(),) * 8
        + (table,) * 6
    )
    out_specs = (sharded, sharded) + (P(),) * 8 + (P(None, "exp", None, "ctx"),) * 6
    return jax.shard_map(body, mesh=mesh, in_specs=in_specs, out_specs=out_specs, check_vma=False)
```

```python
import functools

import jax
import jax.numpy as jnp
from jax import lax
from jax.experimental import pallas as pl
from jax.experimental.pallas import tpu as pltpu
from jax.sharding import PartitionSpec as P

ASKING_ATTENDERS = 24
PAIRED_ATTENDERS = 8
ATTENTION_EXTENT = 64
HEADS_PER_PAIR = ASKING_ATTENDERS // PAIRED_ATTENDERS
QUERY_COLS = HEADS_PER_PAIR * ATTENTION_EXTENT
EXPERTS = 40
TOPK = 8
NUM_CHOICES_X = 8
CAP = 48
RANK = 16
LANES = 128

EPS = 1e-06
LOW_FACTORED = 2.0
MASKED_FLOOR = -1e30
SCALE = 0.125
VMEM_LIMIT = 56 * 1024 * 1024

bf16 = jnp.bfloat16
f32 = jnp.float32

HEAD_COLS = 384


def nn(left, right):
    return jnp.dot(left, right, preferred_element_type=f32)


def nt(left, right):
    return lax.dot_general(left, right, (((1,), (1,)), ((), ())), preferred_element_type=f32)


def tn(left, right):
    return lax.dot_general(left, right, (((0,), (0,)), ((), ())), preferred_element_type=f32)


def normed(rows, gain):
    factor = lax.rsqrt(jnp.mean(rows * rows, axis=-1, keepdims=True) + EPS)
    return rows * factor * gain, factor


def norm_back(rows, factor, gain, adjoint):
    weighted = adjoint * gain
    central = jnp.mean(weighted * rows, axis=-1, keepdims=True)
    return factor * (weighted - rows * factor * factor * central)


def whole_block(shape):
    return pl.BlockSpec(shape, lambda *ids: (0,) * len(shape))


def call_params(axes=1):
    return pltpu.CompilerParams(
        dimension_semantics=("arbitrary",) * axes, vmem_limit_bytes=VMEM_LIMIT
    )


def key_mask(seg_col, seg_row, tile, start, kmax):
    key_place = lax.broadcasted_iota(jnp.int32, (kmax, tile), 0)
    query_place = start + lax.broadcasted_iota(jnp.int32, (kmax, tile), 1)
    key_seg = seg_col[pl.ds(0, kmax), :]
    query_seg = seg_row[0:1, pl.ds(start, tile)]
    same = (key_seg == query_seg) | (key_seg == 0.0)
    return (key_place <= query_place) & same


def block_rows(spot, rows):
    return pl.ds(pl.multiple_of(spot * rows, rows), rows)


def whole_call(kernel, scalars, arrays, out_shape, scratch=(), flops=0, exps=0, name=None):
    size = sum(v.size * v.dtype.itemsize for v in (*arrays, *out_shape))
    return pl.pallas_call(
        kernel,
        grid_spec=pltpu.PrefetchScalarGridSpec(
            num_scalar_prefetch=len(scalars),
            grid=(1,),
            in_specs=[whole_block(v.shape) for v in arrays],
            out_specs=[whole_block(v.shape) for v in out_shape],
            scratch_shapes=list(scratch),
        ),
        out_shape=list(out_shape),
        compiler_params=call_params(),
        cost_estimate=pl.CostEstimate(flops=flops, bytes_accessed=size, transcendentals=exps),
        name=name,
    )(*scalars, *arrays)


def struct(*shape, dtype=bf16):
    return jax.ShapeDtypeStruct(shape, dtype)


def project_attend_kernel(ways, sides, spots_ref, *refs):
    side_refs = refs[:sides]
    (
        w_ref, first_ref, second_ref, qkv_ref, inner_ref, att_ref, lse_ref, seg_col, seg_row, turned
    ) = refs[sides:]
    rows = side_refs[0].shape[1]
    width = first_ref.shape[1]
    slot = 0
    for side in side_refs:
        count = side.shape[0]
        x = side[...].reshape(count * rows, side.shape[2])
        inner = nt(x[:, :width], first_ref[...]).astype(bf16)
        qkv = nn(x[:, :width], w_ref[...]) + LOW_FACTORED * nn(inner, second_ref[...])
        qkv = qkv.astype(bf16)
        for index in range(count):
            own = slice(index * rows, (index + 1) * rows)
            here = block_rows(spots_ref[slot], rows)
            qkv_ref[here, :] = qkv[own]
            inner_ref[here, :] = inner[own]
            turned[:, here] = qkv[own].astype(f32).T.astype(bf16)
            segments = x[own, width:].astype(f32)
            seg_col[here, :] = segments[:, 0:1]
            seg_row[:, here] = segments.T[0:8, :]
            slot += 1
    part = spots_ref[slot]
    if ways > 1:
        att_ref[...] = jnp.zeros_like(att_ref)
        lse_ref[...] = jnp.zeros_like(lse_ref)
    per_tile = 2 if ways == 1 else 1
    tile = per_tile * rows
    for index in range(slot // ways // per_tile):
        kmax = (index + 1) * per_tile * ways * rows
        first_block = index * per_tile * ways + part if ways > 1 else index * per_tile
        start = pl.multiple_of(first_block * rows, rows) if ways > 1 else first_block * rows
        allowed = key_mask(seg_col, seg_row, tile, start, kmax)
        keys = qkv_ref[pl.ds(0, kmax), 0:LANES]
        values_t = turned[ATTENTION_EXTENT:LANES, pl.ds(0, kmax)]
        outs = []
        sums = []
        for head in range(HEADS_PER_PAIR):
            base = LANES + head * ATTENTION_EXTENT
            q_t = turned[base : base + ATTENTION_EXTENT, pl.ds(start, tile)] * SCALE
            q_pad = jnp.concatenate([q_t, jnp.zeros_like(q_t)], axis=0)
            score = jnp.where(allowed, nn(keys, q_pad), MASKED_FLOOR)
            top = jnp.max(score, axis=0, keepdims=True)
            weight = jnp.exp(score - top)
            total = jnp.sum(weight, axis=0, keepdims=True)
            prob = (weight * (1.0 / total)).astype(bf16)
            outs.append(nn(values_t, prob))
            sums.append(top + jnp.log(total))
        packed = jnp.concatenate(outs, axis=0).astype(bf16)
        for block in range(per_tile):
            att_ref[first_block + block] = packed[:, block * rows : (block + 1) * rows]
        lse_ref[:, pl.ds(start, tile)] = jnp.concatenate(
            sums + [jnp.zeros((8 - HEADS_PER_PAIR, tile), f32)], axis=0
        )


def project_attend(spots, x_sides, weights, first, second, ways):
    blocks, rows = sum(v.shape[0] for v in x_sides), x_sides[0].shape[1]
    total = blocks * rows
    return whole_call(
        functools.partial(project_attend_kernel, ways, len(x_sides)),
        (spots,),
        (*x_sides, weights, first, second),
        (
            struct(total, HEAD_COLS), struct(total, first.shape[0]),
            struct(blocks, QUERY_COLS, rows), struct(8, total, dtype=f32),
            struct(total, 1, dtype=f32), struct(8, total, dtype=f32),
        ),
        scratch=(pltpu.VMEM((HEAD_COLS, total), bf16),),
        flops=2 * total * first.shape[1] * 512 + 8 * total * total * 256,
        exps=HEADS_PER_PAIR * total * total,
        name="project_attend",
    )


def attend_back_kernel(ways, sides, width, spots_ref, *refs):
    qkv_ref, adj_ref, lse_ref, second_ref, inner_ref, seg_col, seg_row = refs[:7]
    side_refs = refs[7 : 7 + sides]
    (
        out_tables, grad_ref, inner_grad_ref, pieces_ref, own_ref, turned, adj_turned, grad_kv
    ) = refs[7 + sides :]
    blocks, rows = adj_ref.shape[0], adj_ref.shape[2]
    half = ATTENTION_EXTENT
    wide, span = width // blocks, pieces_ref.shape[2]
    part = spots_ref[blocks]
    for index in range(blocks):
        here = pl.ds(index * rows, rows)
        turned[:, here] = qkv_ref[here, :].astype(f32).T.astype(bf16)
        adj_turned[:, here] = adj_ref[index]
    grad_kv[...] = jnp.zeros_like(grad_kv)
    if ways > 1:
        grad_ref[...] = jnp.zeros_like(grad_ref)
    per_tile = 2 if ways == 1 else 1
    tile = per_tile * rows
    zero = jnp.zeros((half, tile), bf16)
    for index in range(blocks // ways // per_tile):
        kmax = (index + 1) * per_tile * ways * rows
        start = index * tile
        if ways > 1:
            start = pl.multiple_of((index * per_tile * ways + part) * rows, rows)
        allowed = key_mask(seg_col, seg_row, tile, start, kmax)
        keys = qkv_ref[pl.ds(0, kmax), 0:LANES]
        keys_t = turned[0:half, pl.ds(0, kmax)]
        grads_q = []
        update = jnp.zeros((kmax, LANES), f32)
        for head in range(HEADS_PER_PAIR):
            base = LANES + head * half
            q_t = turned[base : base + half, pl.ds(start, tile)] * SCALE
            q_pad = jnp.concatenate([q_t, zero], axis=0)
            a_t = adj_turned[head * half : (head + 1) * half, pl.ds(start, tile)]
            a_pad = jnp.concatenate([zero, a_t], axis=0)
            score = nn(keys, q_pad) - lse_ref[head : head + 1, pl.ds(start, tile)]
            prob = jnp.where(allowed, jnp.exp(jnp.where(allowed, score, 0.0)), 0.0)
            grad_prob = nn(keys, a_pad)
            both = prob * grad_prob
            delta = jnp.sum(both, axis=0, keepdims=True)
            grad_score = (both - prob * delta).astype(bf16)
            update = update + nt(grad_score, q_pad) + nt(prob.astype(bf16), a_pad)
            grads_q.append(nn(keys_t, grad_score) * SCALE)
        grad_kv[pl.ds(0, kmax), :] += update
        packed = jnp.concatenate(grads_q + [jnp.zeros((half, tile), f32)], axis=0)
        grad_ref[pl.ds(start, tile), LANES:] = packed.T.astype(bf16)
    grad_ref[:, 0:LANES] = grad_kv[...].astype(bf16)

    inner_grad_ref[...] = (LOW_FACTORED * nt(grad_ref[...], second_ref[...])).astype(bf16)
    slot = 0
    grad_first = None
    for side in side_refs:
        count = side.shape[0]
        inner_grad = jnp.concatenate(
            [inner_grad_ref[block_rows(spots_ref[slot + i], rows), :] for i in range(count)],
            axis=0,
        )
        x = side[...].reshape(count * rows, side.shape[2])[:, :width]
        term = tn(inner_grad, x)
        grad_first = term if grad_first is None else grad_first + term
        slot += count
    third = wide // 3
    gap = jnp.zeros((RANK, QUERY_COLS - wide), f32)
    for place in range(blocks):
        second = out_tables[place, RANK:, :].astype(f32)
        for index in range(3):
            piece = grad_first[index * RANK : (index + 1) * RANK, place * wide : (place + 1) * wide]
            chunk = second[:, index * third : (index + 1) * third]
            parts = [piece, gap, chunk] if wide < QUERY_COLS else [piece, chunk]
            pieces_ref[place, index * RANK : (index + 1) * RANK, :] = padded(
                jnp.concatenate(parts, axis=1), span
            )
        pieces_ref[place, 3 * RANK :, :] = out_tables[place, 0:RANK, :]
    seconds = LOW_FACTORED * tn(inner_ref[...], grad_ref[...])
    own_ref[0 : 3 * RANK, :] = jnp.zeros((3 * RANK, span), bf16)
    value = seconds[2 * RANK : 3 * RANK, half : 2 * half]
    own_ref[3 * RANK : 4 * RANK, :] = padded(
        jnp.concatenate([jnp.zeros((RANK, QUERY_COLS), f32), value], axis=1), span
    )
    query, key = seconds[0:RANK, LANES : LANES + QUERY_COLS], seconds[RANK : 2 * RANK, 0:half]
    own_ref[4 * RANK :, :] = padded(jnp.concatenate([query, key], axis=1), span)


def padded(piece, span):
    rows, size = piece.shape
    if size < span:
        piece = jnp.concatenate([piece, jnp.zeros((rows, span - size), piece.dtype)], axis=1)
    return piece.astype(bf16)


def attend_back(
    spots, qkv, adj, lse, second, inner, seg_col, seg_row, x_sides, out_tables, width, ways
):
    blocks, rows = adj.shape[0], adj.shape[2]
    total, span = qkv.shape[0], out_tables.shape[2]
    return whole_call(
        functools.partial(attend_back_kernel, ways, len(x_sides), width),
        (spots,),
        (qkv, adj, lse, second, inner, seg_col, seg_row, *x_sides, out_tables),
        (
            struct(total, HEAD_COLS), struct(total, 3 * RANK),
            struct(blocks, 4 * RANK, span), struct(PACKED * RANK, span),
        ),
        scratch=(
            pltpu.VMEM((HEAD_COLS, total), bf16),
            pltpu.VMEM((QUERY_COLS, total), bf16),
            pltpu.VMEM((total, LANES), f32),
        ),
        flops=20 * total * total * 256,
        exps=HEADS_PER_PAIR * total * total,
        name="attend_back",
    )


def rows_back_kernel(first_slot, spots_ref, grad_ref, inner_ref, w_ref, first_ref, rows_ref):
    count, rows, width = rows_ref.shape
    spots = [block_rows(spots_ref[first_slot + i], rows) for i in range(count)]
    grad = jnp.concatenate([grad_ref[spot, :] for spot in spots], axis=0)
    inner = jnp.concatenate([inner_ref[spot, :] for spot in spots], axis=0)
    out = nt(grad, w_ref[...]) + nn(inner, first_ref[...])
    rows_ref[...] = out.astype(bf16).reshape(count, rows, width)


def rows_back(spots, grad, inner, weights, first, x_sides, side):
    count, rows, _ = x_sides[side].shape
    width, cols = weights.shape
    first_slot = sum(v.shape[0] for v in x_sides[:side])
    return whole_call(
        functools.partial(rows_back_kernel, first_slot),
        (spots,),
        (grad, inner, weights, first),
        [struct(count, rows, width)],
        flops=4 * count * rows * width * cols,
        name="rows_back",
    )[0]


OUT_STEPS = 4


def row_block(array):
    rest = array.shape[1:]
    return pl.BlockSpec((array.shape[0] // OUT_STEPS,) + rest, lambda i: (i,) + (0,) * len(rest))


def output_project_kernel(
    w_ref, att_ref, first_ref, second_ref, rows_ref, gain_ref, mid_ref, normed_ref, inner_ref,
    total, inner_total,
):
    step = pl.program_id(0)

    @pl.when(step == 0)
    def _():
        total[...] = rows_ref[...].astype(f32)
        inner_total[...] = jnp.zeros_like(inner_total)

    total[...] += tn(att_ref[...], w_ref[...])
    inner_total[...] += tn(att_ref[...], first_ref[...])

    @pl.when(step == OUT_STEPS - 1)
    def _():
        inner = inner_total[...].astype(bf16)
        mid = total[...] + LOW_FACTORED * nn(inner, second_ref[...])
        mid_ref[...] = mid
        inner_ref[...] = inner
        low = normed(mid, gain_ref[...])[0].astype(bf16)
        for index in range(normed_ref.shape[0]):
            normed_ref[index] = low


def output_project(weights, att, first, second, rows, gain, sources):
    count, width = rows.shape
    outs = (struct(count, width, dtype=f32), struct(sources, count, width), struct(count, LANES))
    return pl.pallas_call(
        output_project_kernel,
        grid=(OUT_STEPS,),
        in_specs=[row_block(v) for v in (weights, att, first)]
        + [whole_block(v.shape) for v in (second, rows, gain)],
        out_specs=[whole_block(v.shape) for v in outs],
        out_shape=outs,
        scratch_shapes=[pltpu.VMEM((count, width), f32), pltpu.VMEM((count, LANES), f32)],
        compiler_params=call_params(),
        cost_estimate=pl.CostEstimate(
            flops=2 * count * width * width, bytes_accessed=2 * width * width, transcendentals=0
        ),
        name="output_project",
    )(weights, att, first, second, rows, gain)


def output_back_kernel(
    w_ref, att_ref, first_ref, parts_ref, mid_ref, gain_ref, out_grad_ref, second_ref, inner_ref,
    adj_ref, tables_ref, grad_mid_ref, branch, grad_inner,
):
    step = pl.program_id(0)
    places, _, span = tables_ref.shape
    wide = w_ref.shape[1] // places

    @pl.when(step == 0)
    def _():
        grad = parts_ref[0].astype(f32)
        for index in range(1, parts_ref.shape[0]):
            grad = grad + parts_ref[index].astype(f32)
        mid = mid_ref[...]
        factor = lax.rsqrt(jnp.mean(mid * mid, axis=-1, keepdims=True) + EPS)
        grad_mid = out_grad_ref[...].astype(f32) + norm_back(mid, factor, gain_ref[...], grad)
        grad_mid_ref[...] = grad_mid
        low = grad_mid.astype(bf16)
        branch[...] = low
        grad_inner[...] = (LOW_FACTORED * nt(low, second_ref[...])).astype(bf16)
        seconds = LOW_FACTORED * tn(inner_ref[...], low)
        for place in range(places):
            piece = seconds[0:RANK, place * wide : (place + 1) * wide]
            tables_ref[place, RANK:, :] = padded(piece, span)

    adj_ref[...] = (
        nt(w_ref[...], branch[...]) + nt(first_ref[...], grad_inner[...])
    ).astype(bf16)
    firsts = nn(att_ref[...], grad_inner[...])
    for index in range(places // OUT_STEPS):
        piece = firsts[index * wide : (index + 1) * wide].T
        tables_ref[step * (places // OUT_STEPS) + index, 0:RANK, :] = padded(piece[0:RANK], span)


def output_back(weights, att, first, parts, mid, gain, out_grad, second, inner, places, span):
    count, width = mid.shape
    outs = (
        struct(*att.shape), struct(places, 2 * RANK, span), struct(count, width, dtype=f32)
    )
    rest = (parts, mid, gain, out_grad, second, inner)
    return pl.pallas_call(
        output_back_kernel,
        grid=(OUT_STEPS,),
        in_specs=[row_block(v) for v in (weights, att, first)]
        + [whole_block(v.shape) for v in rest],
        out_specs=[row_block(outs[0])] + [whole_block(v.shape) for v in outs[1:]],
        out_shape=outs,
        scratch_shapes=[pltpu.VMEM((count, width), bf16), pltpu.VMEM((count, LANES), bf16)],
        compiler_params=call_params(),
        cost_estimate=pl.CostEstimate(
            flops=2 * count * width * width, bytes_accessed=2 * width * width, transcendentals=0
        ),
        name="output_back",
    )(weights, att, first, *rest)


PACKED = 5


def attend_tables_kernel(ways, sides, place_ref, adapter_ref, *refs):
    side_refs, out_refs = refs[:sides], refs[sides:]
    per_side, sources = side_refs[0].shape[0], side_refs[0].shape[1] // (PACKED * RANK)
    blocks = per_side * sides
    wide = out_refs[0].shape[2] // blocks
    third = wide // 3
    half = ATTENTION_EXTENT

    def read(place, source, index):
        slot = place_ref[place]
        rows = pl.ds((source * PACKED + index) * RANK, RANK)
        value = side_refs[0][lax.rem(slot, per_side), rows, :]
        if sides > 1:
            value = jnp.where(slot < per_side, value, side_refs[1][lax.rem(slot, per_side), rows, :])
        return value.astype(f32)

    def by_head(pieces):
        return [
            sum(pieces[h * ways + 1 : (h + 1) * ways], pieces[h * ways])
            for h in range(PAIRED_ATTENDERS)
        ]

    for out_ref in out_refs:
        out_ref[...] = jnp.zeros_like(out_ref)
    for source in range(sources):
        adapter = adapter_ref[source]
        got = [[read(c, source, index) for c in range(blocks)] for index in range(PACKED)]
        pieces = [[v[:, :wide] for v in got[index]] for index in range(4)]
        pieces.append([
            got[index][c][:, QUERY_COLS : QUERY_COLS + third]
            for c in range(blocks) for index in range(3)
        ])
        pieces.append(by_head([v[:, :QUERY_COLS] for v in got[4]]))
        pieces.append(by_head([v[:, QUERY_COLS : QUERY_COLS + half] for v in got[4]]))
        pieces.append(by_head([v[:, QUERY_COLS : QUERY_COLS + half] for v in got[3]]))
        for parts, out_ref in zip(pieces, out_refs):
            out_ref[adapter] = out_ref[adapter] + jnp.concatenate(parts, axis=1)


def attend_tables(place, adapters, sides, width, ways):
    key_cols = PAIRED_ATTENDERS * ATTENTION_EXTENT
    cols = (width,) * 5 + (ASKING_ATTENDERS * ATTENTION_EXTENT, key_cols, key_cols)
    return whole_call(
        functools.partial(attend_tables_kernel, ways, len(sides)),
        (place, adapters),
        sides,
        [struct(NUM_CHOICES_X, RANK, size, dtype=f32) for size in cols],
        name="attend_tables",
    )


def expert_tables_kernel(sizes, sources, adapter_ref, rows_ref, *out_refs):
    adapter = pl.program_id(0)
    for out_ref in out_refs:
        out_ref[...] = jnp.zeros_like(out_ref)
    for source in range(sources):

        @pl.when(adapter_ref[source] == adapter)
        def _():
            for expert in range(rows_ref.shape[0]):
                own = rows_ref[expert, source * RANK : (source + 1) * RANK, :].astype(f32)
                start = 0
                for size, out_ref in zip(sizes, out_refs):
                    out_ref[0, expert] += own[:, start : start + size]
                    start += size


def expert_tables(adapters, rows, wide, slim):
    experts, sources = rows.shape[0], adapters.shape[0]
    sizes = (wide,) * 3 + (slim,) * 3
    return pl.pallas_call(
        functools.partial(expert_tables_kernel, sizes, sources),
        grid_spec=pltpu.PrefetchScalarGridSpec(
            num_scalar_prefetch=1,
            grid=(NUM_CHOICES_X,),
            in_specs=[whole_block(rows.shape)],
            out_specs=[
                pl.BlockSpec((1, experts, RANK, size), lambda a, adapters: (a, 0, 0, 0))
                for size in sizes
            ],
        ),
        out_shape=[
            jax.ShapeDtypeStruct((NUM_CHOICES_X, experts, RANK, size), f32) for size in sizes
        ],
        compiler_params=call_params(),
        name="expert_tables",
    )(adapters, rows)


def source_mask(shape, sources):
    row = lax.broadcasted_iota(jnp.int32, shape, 0)
    col = lax.broadcasted_iota(jnp.int32, shape, 1)
    keep = None
    for source in range(sources):
        inside = (row >= source * CAP) & (row < (source + 1) * CAP)
        inside &= (lax.rem(col, sources * RANK) >= source * RANK) & (
            lax.rem(col, sources * RANK) < (source + 1) * RANK
        )
        keep = inside if keep is None else keep | inside
    return keep


def masked(values, sources):
    return jnp.where(source_mask(values.shape, sources), values, 0.0)


def picks(slot_ref, pair, tokens, unit=0):
    slots = slot_ref[unit, :, pair * 2 * tokens : (pair + 1) * 2 * tokens]
    place = lax.broadcasted_iota(jnp.int32, (2 * CAP, 2 * tokens), 0)
    return place == slots


def picked_rows(slot_ref, rows_ref, sources, unit=0):
    tokens = rows_ref.shape[0] // sources
    parts = []
    for pair in range(sources // 2):
        pick = picks(slot_ref, pair, tokens, unit).astype(f32).astype(bf16)
        rows = rows_ref[pair * 2 * tokens : (pair + 1) * 2 * tokens, :]
        parts.append(nn(pick, rows))
    return jnp.concatenate(parts, axis=0)


def picked_gates(slot_ref, gate_ref, sources):
    tokens = gate_ref.shape[2] // sources
    parts = []
    for pair in range(sources // 2):
        gate = gate_ref[0, :, pair * 2 * tokens : (pair + 1) * 2 * tokens]
        kept = jnp.where(picks(slot_ref, pair, tokens), gate, 0.0)
        parts.append(jnp.sum(kept, axis=1, keepdims=True))
    return jnp.concatenate(parts, axis=0)


def combine(target_ref, values, out_ref, sources):
    tokens = target_ref.shape[0] // sources
    slots = values.shape[1]
    for source in range(sources):
        target = target_ref[source * tokens : (source + 1) * tokens, :]
        place = lax.broadcasted_iota(jnp.int32, (tokens, slots), 1)
        hit = place == target[:, 0:1]
        for choice in range(1, TOPK):
            hit |= place == target[:, choice : choice + 1]
        out_ref[source] = nn(hit.astype(f32).astype(bf16), values[source]).astype(bf16)


def combine_ring(place, target_ref, values, out_refs):
    sources = len(out_refs)
    tokens = target_ref.shape[0] // sources
    slots = values.shape[1]
    for shift, out_ref in enumerate(out_refs):
        source = lax.rem(place + shift, sources)
        target = target_ref[pl.ds(pl.multiple_of(source * tokens, tokens), tokens), :]
        column = lax.broadcasted_iota(jnp.int32, (tokens, slots), 1)
        hit = column == target[:, 0:1]
        for choice in range(1, TOPK):
            hit |= column == target[:, choice : choice + 1]
        out_ref[...] = nn(hit.astype(f32).astype(bf16), values[source]).astype(bf16)


def keep_rows(values, rows, expert, sources):
    for source in range(sources):
        values[source, pl.ds(pl.multiple_of(expert * CAP, CAP), CAP), :] = rows[
            source * CAP : (source + 1) * CAP
        ]


def joined(refs, unit=0):
    return jnp.concatenate([ref[0, unit] for ref in refs], axis=0)


def experts_pre_kernel(sources, adapter_ref, slot_ref, gate_ref, grads_ref, down_ref, *refs):
    down_first, down_second = joined(refs[:sources]), joined(refs[sources : 2 * sources])
    picked_ref, hidden_ref, inner_ref = refs[2 * sources :]
    grads = picked_rows(slot_ref, grads_ref, sources)
    grads = (grads * picked_gates(slot_ref, gate_ref, sources)).astype(bf16)
    picked_ref[0] = grads
    inner = LOW_FACTORED * nt(grads, down_second)
    inner = masked(inner, sources).astype(bf16)
    inner_ref[0] = inner
    hidden_ref[0] = nt(grads, down_ref[0]) + nn(inner, down_first)


def experts_main_kernel(
    sources, adapter_ref, slot_ref, x_ref, gate_w, up_w, grad_hidden, target_ref, *refs
):
    groups = [refs[i * sources : (i + 1) * sources] for i in range(4)]
    picked_ref, hidden_ref, adj_ref, inner_ref, out_ref, values = refs[4 * sources :]
    per_step, width, inner_size = gate_w.shape
    span = 2 * sources * RANK
    firsts, seconds = [], []
    for unit in range(per_step):
        firsts.append(
            jnp.concatenate([joined(groups[0], unit), joined(groups[1], unit)], axis=0)
        )
        gate_second, up_second = joined(groups[2], unit), joined(groups[3], unit)
        blank = jnp.zeros_like(gate_second)
        seconds.append(
            jnp.concatenate(
                [
                    jnp.concatenate([gate_second, blank], axis=1),
                    jnp.concatenate([blank, up_second], axis=1),
                ],
                axis=0,
            )
        )
        picked_ref[unit] = picked_rows(slot_ref, x_ref, sources, unit).astype(bf16)
        inner = masked(LOW_FACTORED * nt(picked_ref[unit], firsts[unit]), sources)
        inner_ref[unit, :, :span] = inner.astype(bf16)
    for unit in range(per_step):
        x = picked_ref[unit]
        inner = inner_ref[unit, :, :span]
        for start in range(0, inner_size, 2 * LANES):
            cols = slice(start, start + 2 * LANES)
            ups = slice(inner_size + start, inner_size + start + 2 * LANES)
            gate = nn(x, gate_w[unit, :, cols]) + nn(inner, seconds[unit][:, cols])
            up = nn(x, up_w[unit, :, cols]) + nn(inner, seconds[unit][:, ups])
            sigma = 1.0 / (1.0 + jnp.exp(-gate))
            active = gate * sigma
            hidden_ref[unit, :, cols] = (active * up).astype(bf16)
            adj = grad_hidden[unit, :, cols]
            grad_gate = adj * up * sigma * (1.0 + gate * (1.0 - sigma))
            adj_ref[unit, :, cols] = grad_gate.astype(bf16)
            adj_ref[unit, :, ups] = (adj * active).astype(bf16)
    for unit in range(per_step):
        grad_inner = masked(LOW_FACTORED * nt(adj_ref[unit], seconds[unit]), sources)
        inner_ref[unit, :, span:] = grad_inner.astype(bf16)
    for unit in range(per_step):
        rows = nt(adj_ref[unit, :, :inner_size], gate_w[unit])
        rows = rows + nt(adj_ref[unit, :, inner_size:], up_w[unit])
        rows = rows + nn(inner_ref[unit, :, span:], firsts[unit])
        expert = pl.program_id(0) * per_step + unit
        keep_rows(values, rows.astype(bf16), expert, sources)

    @pl.when(pl.program_id(0) == pl.num_programs(0) - 1)
    def _():
        combine(target_ref, values, out_ref, sources)


def experts_post_kernel(
    sources, cohort, adapter_ref, slot_ref, gate_ref, down_ref, picked_ref, hidden_ref, adj_ref,
    inner_ref, picked_grads, grad_inner_down, target_ref, *refs
):
    down_first, down_second = joined(refs[:sources]), joined(refs[sources : 2 * sources])
    table_ref, *out_refs, values = refs[2 * sources :]
    expert = pl.program_id(0)
    span = sources * RANK
    hidden = hidden_ref[0]
    inner_down = masked(nt(hidden, down_first), sources).astype(bf16)
    answer = nn(hidden, down_ref[0]) + LOW_FACTORED * nn(inner_down, down_second)
    answer = answer.astype(bf16).astype(f32) * picked_gates(slot_ref, gate_ref, sources)
    keep_rows(values, answer.astype(bf16), expert, sources)
    width = picked_ref.shape[2]
    inner_size = hidden.shape[1]
    inner = inner_ref[0, :, : 2 * span]
    grad_inner = inner_ref[0, :, 2 * span :]
    firsts = tn(grad_inner, picked_ref[0])
    seconds = tn(inner, adj_ref[0])
    down_firsts = tn(grad_inner_down[0], hidden)
    down_seconds = LOW_FACTORED * tn(inner_down, picked_grads[0])
    wide, slim = width // cohort, inner_size // cohort
    wide_parts = (firsts[:span], firsts[span:], down_seconds)
    slim_parts = (seconds[:span, :inner_size], seconds[span:, inner_size:], down_firsts)
    for place in range(cohort):
        pieces = [v[:, place * wide : (place + 1) * wide] for v in wide_parts]
        pieces += [v[:, place * slim : (place + 1) * slim] for v in slim_parts]
        table_ref[place, 0] = jnp.concatenate(pieces, axis=1).astype(bf16)

    @pl.when(expert == pl.num_programs(0) - 1)
    def _():
        combine_ring(adapter_ref[sources], target_ref, values, out_refs)


def per_expert(array, per_step=1):
    rest = array.shape[1:]
    return pl.BlockSpec((per_step,) + rest, lambda e, *_: (e,) + (0,) * len(rest))


def expert_rows(rows, width, per_step=1):
    return pl.BlockSpec((per_step, rows, width), lambda e, *_: (e, 0, 0))


def adapter_blocks(table, sources, per_step):
    shape = (1, per_step) + table.shape[2:]
    return [
        pl.BlockSpec(shape, lambda e, adapters, s=s: (adapters[s], e, 0, 0))
        for s in range(sources)
    ]


def expert_call(
    kernel, sources, adapters, arrays, specs, tables, out_shape, out_specs, scratch, flops, name,
    per_step=1,
):
    experts = tables[0].shape[1]
    size = sum(v.size * v.dtype.itemsize for v in (*arrays, *out_shape))
    return pl.pallas_call(
        kernel,
        grid_spec=pltpu.PrefetchScalarGridSpec(
            num_scalar_prefetch=1,
            grid=(experts // per_step,),
            in_specs=specs
            + [spec for t in tables for spec in adapter_blocks(t, sources, per_step)],
            out_specs=out_specs,
            scratch_shapes=scratch,
        ),
        out_shape=out_shape,
        compiler_params=call_params(),
        cost_estimate=pl.CostEstimate(flops=flops, bytes_accessed=size, transcendentals=0),
        name=name,
    )(adapters, *arrays, *[t for t in tables for _ in range(sources)])


def experts_pre(adapters, slots, gates, grads, down, down_first, down_second):
    experts, inner_size, width = down.shape
    sources = adapters.shape[0]
    rows = sources * CAP
    return expert_call(
        functools.partial(experts_pre_kernel, sources),
        sources,
        adapters,
        (slots, gates, grads, down),
        [
            per_expert(slots), per_expert(gates), whole_block((grads.shape[0], width)),
            per_expert(down),
        ],
        (down_first, down_second),
        [
            struct(experts, rows, width), struct(experts, rows, inner_size, dtype=f32),
            struct(experts, rows, sources * RANK),
        ],
        [expert_rows(rows, v) for v in (width, inner_size, sources * RANK)],
        [],
        2 * experts * rows * width * inner_size * 2,
        "experts_pre",
    )


def experts_main(
    adapters, slots, x, gate_w, up_w, grad_hidden, target, gate_first, up_first, gate_second,
    up_second,
):
    experts, width, inner_size = gate_w.shape
    sources = adapters.shape[0]
    rows = sources * CAP
    tokens = x.shape[0] // sources
    per_step = 2 if experts % 2 == 0 else 1
    outs = (width, inner_size, 2 * inner_size, 4 * sources * RANK)
    return expert_call(
        functools.partial(experts_main_kernel, sources),
        sources,
        adapters,
        (slots, x, gate_w, up_w, grad_hidden, target),
        [
            per_expert(slots, per_step), whole_block(x.shape), per_expert(gate_w, per_step),
            per_expert(up_w, per_step), per_expert(grad_hidden, per_step),
            whole_block(target.shape),
        ],
        (gate_first, up_first, gate_second, up_second),
        [struct(experts, rows, v) for v in outs] + [struct(sources, tokens, width)],
        [expert_rows(rows, v, per_step) for v in outs] + [whole_block((sources, tokens, width))],
        [pltpu.VMEM((sources, experts * CAP, width), bf16)],
        2 * experts * rows * width * inner_size * 5,
        "experts_main",
        per_step,
    )


def experts_post(
    adapters, slots, gates, down, picked, hidden, adj, inner, picked_grads, grad_inner_down,
    target, down_first, down_second, cohort,
):
    experts, inner_size, width = down.shape
    sources = adapters.shape[0] - 1
    tokens = target.shape[0] // sources
    lanes = 3 * (width + inner_size) // cohort
    arrays = (
        slots, gates, down, picked, hidden, adj, inner, picked_grads, grad_inner_down
    )
    return expert_call(
        functools.partial(experts_post_kernel, sources, cohort),
        sources,
        adapters,
        arrays + (target,),
        [per_expert(v) for v in arrays] + [whole_block(target.shape)],
        (down_first, down_second),
        [struct(cohort, experts, sources * RANK, lanes)] + [struct(tokens, width)] * sources,
        [
            pl.BlockSpec((cohort, 1, sources * RANK, lanes), lambda e, *_: (0, e, 0, 0)),
        ]
        + [whole_block((tokens, width))] * sources,
        [pltpu.VMEM((sources, experts * CAP, width), bf16)],
        2 * experts * sources * CAP * width * inner_size * 2,
        "experts_post",
    )


def flipped(array, axis, size, mask):
    return lax.ppermute(array, axis, [(i, i ^ mask) for i in range(size)])


def ring_blocks(array, axis, size):
    return [array] + [
        lax.ppermute(array, axis, [(i, (i + shift) % size) for i in range(size)])
        for shift in range(1, size)
    ]


def to_every(array, axis, size):
    return lax.all_to_all(
        jnp.broadcast_to(array[None], (size,) + array.shape), axis, 0, 0, tiled=True
    )


def cohort_spots(size):
    place = jnp.arange(size, dtype=jnp.int32)
    if size != 8:
        return place, place
    me = lax.axis_index("ctx")
    mask = place ^ me
    return (place % 4 * 2 + place // 4) ^ me, (mask & 1) * 4 + mask // 2


def gather_cohort(array, size):
    if size != 8:
        return (lax.all_gather(array, "ctx", axis=0, tiled=False),)
    mine = jnp.stack([array] + [flipped(array, "ctx", size, mask) for mask in (2, 4, 6)])
    return mine, flipped(mine, "ctx", size, 1)


def staged_sums(pieces, row_sides, summed, beside, size, sources):
    tie = lax.optimization_barrier

    def plus(left, right):
        return (left.astype(f32) + right.astype(f32)).astype(bf16)

    other, row_side, pieces = tie((flipped(row_sides[1], "ctx", size, 1), row_sides[0], pieces))
    mine = plus(row_side, other)
    half = mine.shape[1] // 2
    low, high = mine[:, :half], mine[:, half:]
    near, far, slip = tie(
        (jnp.stack([low[1], low[3]]), jnp.stack([high[2], high[3]]), summed(pieces))
    )
    near, far, groups = tie(
        (
            flipped(near, "ctx", size, 2), flipped(far, "ctx", size, 4),
            to_every(slip, "exp", sources),
        )
    )
    low_last, high_last, groups = tie(
        (plus(low[2], near[1]), plus(high[1], far[1]), groups.reshape(-1, slip.shape[1]))
    )
    low_last, high_last, blocks, beside = tie(
        (
            flipped(low_last, "ctx", size, 4), flipped(high_last, "ctx", size, 2),
            [flipped(groups, "ctx", size, mask) for mask in (2, 4, 6)], beside,
        )
    )
    mine = jnp.stack([groups] + blocks)
    low_sum = low[0].astype(f32) + near[0].astype(f32) + low_last.astype(f32)
    high_sum = high[0].astype(f32) + far[0].astype(f32) + high_last.astype(f32)
    rows = jnp.concatenate([low_sum, high_sum], axis=0)
    return (mine, flipped(mine, "ctx", size, 1)), rows, beside


def head_columns(query, key, value):
    rows = query.shape[0]

    def split(array):
        return jnp.transpose(array.reshape(rows, PAIRED_ATTENDERS, -1), (1, 0, 2))

    parts = [split(key), split(value), split(query)]
    pad = HEAD_COLS - sum(p.shape[2] for p in parts)
    parts.append(jnp.zeros((PAIRED_ATTENDERS, rows, pad), query.dtype))
    return jnp.concatenate(parts, axis=2)


def body(
    tokens, out_grad, attn_gain, moe_gain, w_query, lock_projection, content_projection, w_out,
    sigmoid_matrices, widener_matrices, reducer_matrices, segment_ids, expert_routes,
    route_weights, adapter_index, query_first, query_second, key_first, lock_final_matrices,
    value_first, content_final_matrices, output_first, output_second, gate_first, gate_second,
    upward_first, upward_second, down_first, down_second,
):
    rows_in = tokens[0].astype(f32)
    count, width = rows_in.shape
    cohort = lax.axis_size("ctx")
    sources = lax.axis_size("exp")
    experts = sigmoid_matrices.shape[0]
    ctx = lax.axis_index("ctx")
    exp = lax.axis_index("exp")
    ways = cohort // PAIRED_ATTENDERS
    head = ctx // ways
    adapter = adapter_index[exp]

    def elected(table):
        return lax.dynamic_index_in_dim(table, adapter, 0, keepdims=False)

    attended_cols = ASKING_ATTENDERS * ATTENTION_EXTENT
    wide = width // cohort
    span = -(-max(wide, QUERY_COLS) // LANES) * LANES
    spots, place = cohort_spots(cohort)
    order = jnp.concatenate([spots, (ctx % ways)[None].astype(jnp.int32)])

    normed_in, factor_in = normed(rows_in, attn_gain)
    labels = jnp.pad(segment_ids[0].astype(bf16)[:, None], ((0, 0), (0, LANES - 1)))
    x_sides = gather_cohort(jnp.concatenate([normed_in.astype(bf16), labels], axis=1), cohort)
    full_out = lax.all_gather(w_out, ("ctx", "exp"), axis=0, tiled=True)
    head_w = head_columns(w_query, lock_projection, content_projection)
    to_all = jnp.broadcast_to(
        head_w[:, None], (PAIRED_ATTENDERS, ways * sources) + head_w.shape[1:]
    ).reshape((cohort * sources,) + head_w.shape[1:])
    own_w = lax.all_to_all(to_all, ("ctx", "exp"), 0, 0, tiled=True).reshape(width, HEAD_COLS)
    relative = (exp - jnp.arange(sources, dtype=jnp.int32) + sources) % sources

    routes = expert_routes[0].astype(bf16)
    weight_high = route_weights[0].astype(bf16)
    weight_low = (route_weights[0] - weight_high.astype(f32)).astype(bf16)
    parcel = jnp.concatenate(
        [
            out_grad[0], routes, weight_high, weight_low,
            jnp.zeros((count, LANES - 3 * TOPK), bf16),
        ],
        axis=1,
    )
    parcel, own_w = lax.optimization_barrier((parcel, own_w))
    parcels = ring_blocks(parcel, "exp", sources)

    own_firsts = jnp.concatenate(
        [elected(query_first), elected(key_first), elected(value_first)], axis=0
    )

    def head_part(table):
        part = elected(table)
        size = part.shape[1] // PAIRED_ATTENDERS
        return lax.dynamic_slice_in_dim(part, head * size, size, 1)

    def placed(part, row, col):
        return jnp.pad(
            part, ((row, 2 * RANK - row), (col, HEAD_COLS - col - part.shape[1]))
        )

    own_seconds = (
        placed(head_part(query_second), 0, LANES)
        + placed(head_part(lock_final_matrices), RANK, 0)
        + placed(head_part(content_final_matrices), 2 * RANK, ATTENTION_EXTENT)
    )
    qkv, inner, attended, lse, seg_col, seg_row = project_attend(
        order, x_sides, own_w, own_firsts, own_seconds, ways
    )
    attended = lax.all_to_all(attended, "ctx", 0, 0, tiled=True)
    attended, parcels = lax.optimization_barrier((attended, parcels))
    if ways > 1:
        attended = attended.reshape(PAIRED_ATTENDERS, ways, QUERY_COLS, count)
        attended = attended.astype(f32).sum(1).astype(bf16)
    attended = attended.reshape(attended_cols, count)
    out_first = jnp.pad(elected(output_first), ((0, LANES - RANK), (0, 0)))
    out_first = out_first.T
    out_second = jnp.pad(elected(output_second), ((0, LANES - RANK), (0, 0)))
    mid, normed_mid, inner_out = output_project(
        full_out, attended, out_first, out_second, tokens[0], moe_gain[None], sources
    )
    x_all = lax.all_to_all(normed_mid, "exp", 0, 0, tiled=True).reshape(sources * count, width)

    parcels, normed_mid = lax.optimization_barrier((parcels, normed_mid))
    parcels = jnp.stack(parcels)[relative].reshape(sources * count, -1)
    extra = parcels[:, width:].astype(f32).reshape(sources, count, -1)
    all_routes = extra[:, :, :TOPK].astype(jnp.int32) - exp * experts
    all_gates = extra[:, :, TOPK : 2 * TOPK] + extra[:, :, 2 * TOPK : 3 * TOPK]
    hits = all_routes[None] == jnp.arange(experts, dtype=jnp.int32)[:, None, None, None]
    named = jnp.any(hits, axis=3)
    gates = jnp.sum(jnp.where(hits, all_gates[None], 0.0), axis=3).reshape(experts, 1, -1)
    earlier = jnp.tril(jnp.ones((count, count), bf16), -1)
    rank = lax.dot_general(
        named.astype(bf16), earlier, (((2,), (1,)), ((), ())), preferred_element_type=f32
    ).astype(jnp.int32)
    side = (jnp.arange(sources, dtype=jnp.int32) % 2 * CAP)[None, :, None]
    slots = jnp.where(named, rank + side, -1).reshape(experts, 1, -1)
    places = jnp.arange(experts, dtype=jnp.int32)[:, None, None] * CAP + rank + 1
    target = jnp.sum(jnp.where(hits, places[..., None], 0), axis=0) - 1
    target = target.reshape(sources * count, TOPK)

    picked_grads, grad_hidden, grad_inner_down = experts_pre(
        adapter_index, slots, gates, parcels, reducer_matrices, down_first, down_second
    )
    picked, hidden, adj, inner_rows, grad_parts = experts_main(
        adapter_index, slots, x_all, sigmoid_matrices, widener_matrices, grad_hidden, target,
        gate_first, upward_first, gate_second, upward_second,
    )
    grad_parts = lax.all_to_all(grad_parts, "exp", 0, 0, tiled=True)
    tables, *answers = experts_post(
        jnp.concatenate([adapter_index, exp[None].astype(jnp.int32)]), slots, gates, reducer_matrices, picked, hidden, adj, inner_rows,
        picked_grads, grad_inner_down, target, down_first, down_second, cohort,
    )
    tables, answers, grad_parts = lax.optimization_barrier((tables, answers, grad_parts))
    answers = answers[:1] + [
        lax.ppermute(answers[shift], "exp", [(i, (i + shift) % sources) for i in range(sources)])
        for shift in range(1, sources)
    ]
    early, middle = answers[:2] + answers[3:], answers[2:3]
    table_rows = lax.psum_scatter(tables, "ctx", scatter_dimension=0, tiled=False)

    adj_blocks, out_tables, grad_mid = output_back(
        full_out, attended, out_first, grad_parts, mid, moe_gain[None], out_grad[0], out_second,
        inner_out, cohort, span,
    )
    adj_blocks = jnp.repeat(adj_blocks.reshape(-1, QUERY_COLS, count), ways, axis=0)
    adj_all = lax.all_to_all(adj_blocks, "ctx", 0, 0, tiled=True)
    adj_all, early = lax.optimization_barrier((adj_all, early))
    grad_heads, grad_inner, pieces, own_seconds_grad = attend_back(
        order, qkv, adj_all, lse, own_seconds, inner, seg_col, seg_row, x_sides, out_tables,
        width, ways,
    )
    grad_heads, pieces, middle = lax.optimization_barrier((grad_heads, pieces, middle))
    answers = early + middle
    block_out = (mid + sum(v.astype(f32) for v in answers)).astype(bf16)[None]
    expert_grads = expert_tables(
        adapter_index, table_rows, wide, sigmoid_matrices.shape[2] // cohort
    )

    pieces = lax.all_to_all(pieces, "ctx", 0, 0, tiled=True)
    row_sides = [
        rows_back(order, grad_heads, grad_inner, own_w, own_firsts, x_sides, side)
        for side in reversed(range(len(x_sides)))
    ][::-1]

    def summed(pieces):
        total = jnp.pad(pieces.astype(f32).sum(0), ((0, RANK), (0, 0)))
        return (total + own_seconds_grad.astype(f32)).astype(bf16)

    if cohort != 8:
        groups = to_every(summed(pieces), "exp", sources)
        group_sides = gather_cohort(groups.reshape(-1, span), cohort)
        grad_normed_in = lax.psum_scatter(row_sides[0], "ctx", scatter_dimension=0).astype(f32)
    else:
        group_sides, grad_normed_in, expert_grads = staged_sums(
            pieces, row_sides, summed, expert_grads, cohort, sources
        )
    attention_tables = attend_tables(place, adapter_index, group_sides, width, ways)
    tokens_grad = (
        grad_mid + norm_back(rows_in, factor_in, attn_gain, grad_normed_in)
    ).astype(bf16)[None]
    gate_f, up_f, down_s, gate_s, up_s, down_f = expert_grads
    attention_tables = attend_tables(place, adapter_index, group_sides, width, ways)
    query_f, key_f, value_f, out_f, out_s, query_s, key_s, value_s = attention_tables
    return (
        block_out, tokens_grad, query_f, query_s, key_f, key_s, value_f, value_s, out_f, out_s,
        gate_f, gate_s, up_f, up_s, down_f, down_s,
    )


def solution(mesh):
    sharded = P("exp", "ctx", None)
    rows = P(("ctx", "exp"), None)
    table = P(None, "exp", None, None)
    expert = P("exp", None, None)
    in_specs = (
        (sharded, sharded, P(), P())
        + (rows,) * 4
        + (expert,) * 3
        + (P("exp", "ctx"), sharded, sharded, P())
        + (P(),) * 8
        + (table,) * 6
    )
    out_specs = (sharded, sharded) + (P(),) * 8 + (P(None, "exp", None, "ctx"),) * 6
    return jax.shard_map(body, mesh=mesh, in_specs=in_specs, out_specs=out_specs, check_vma=False)
```

```python
import functools

import jax
import jax.numpy as jnp
from jax import lax
from jax.experimental import pallas as pl
from jax.experimental.pallas import tpu as pltpu
from jax.sharding import PartitionSpec as P

ASKING_ATTENDERS = 24
PAIRED_ATTENDERS = 8
ATTENTION_EXTENT = 64
HEADS_PER_PAIR = ASKING_ATTENDERS // PAIRED_ATTENDERS
QUERY_COLS = HEADS_PER_PAIR * ATTENTION_EXTENT
EXPERTS = 40
TOPK = 8
NUM_CHOICES_X = 8
CAP = 48
RANK = 16
LANES = 128

EPS = 1e-06
LOW_FACTORED = 2.0
MASKED_FLOOR = -1e30
SCALE = 0.125
VMEM_LIMIT = 56 * 1024 * 1024

bf16 = jnp.bfloat16
f32 = jnp.float32

NO_COST = pl.CostEstimate(flops=0, bytes_accessed=0, transcendentals=0)

HEAD_COLS = 384


def nn(left, right):
    return jnp.dot(left, right, preferred_element_type=f32)


def nt(left, right):
    return lax.dot_general(left, right, (((1,), (1,)), ((), ())), preferred_element_type=f32)


def tn(left, right):
    return lax.dot_general(left, right, (((0,), (0,)), ((), ())), preferred_element_type=f32)


def normed(rows, gain):
    factor = lax.rsqrt(jnp.mean(rows * rows, axis=-1, keepdims=True) + EPS)
    return rows * factor * gain, factor


def norm_back(rows, factor, gain, adjoint):
    weighted = adjoint * gain
    central = jnp.mean(weighted * rows, axis=-1, keepdims=True)
    return factor * (weighted - rows * factor * factor * central)


def whole_block(shape):
    return pl.BlockSpec(shape, lambda *ids: (0,) * len(shape))


def call_params(axes=1):
    return pltpu.CompilerParams(
        dimension_semantics=("arbitrary",) * axes, vmem_limit_bytes=VMEM_LIMIT
    )


def key_mask(seg_col, seg_row, tile, start, kmax):
    key_place = lax.broadcasted_iota(jnp.int32, (kmax, tile), 0)
    query_place = start + lax.broadcasted_iota(jnp.int32, (kmax, tile), 1)
    key_seg = seg_col[pl.ds(0, kmax), :]
    query_seg = seg_row[0:1, pl.ds(start, tile)]
    same = (key_seg == query_seg) | (key_seg == 0.0)
    return (key_place <= query_place) & same


def block_rows(spot, rows):
    return pl.ds(pl.multiple_of(spot * rows, rows), rows)


def whole_call(kernel, scalars, arrays, out_shape, scratch=(), flops=0, exps=0, name=None):
    size = sum(v.size * v.dtype.itemsize for v in (*arrays, *out_shape))
    return pl.pallas_call(
        kernel,
        grid_spec=pltpu.PrefetchScalarGridSpec(
            num_scalar_prefetch=len(scalars),
            grid=(1,),
            in_specs=[whole_block(v.shape) for v in arrays],
            out_specs=[whole_block(v.shape) for v in out_shape],
            scratch_shapes=list(scratch),
        ),
        out_shape=list(out_shape),
        compiler_params=call_params(),
        cost_estimate=NO_COST,
        name=name,
    )(*scalars, *arrays)


def struct(*shape, dtype=bf16):
    return jax.ShapeDtypeStruct(shape, dtype)


def project_attend_kernel(ways, sides, spots_ref, *refs):
    side_refs = refs[:sides]
    (
        w_ref, first_ref, second_ref, qkv_ref, inner_ref, att_ref, lse_ref, seg_col, seg_row, turned
    ) = refs[sides:]
    rows = side_refs[0].shape[1]
    width = first_ref.shape[1]
    slot = 0
    for side in side_refs:
        count = side.shape[0]
        x = side[...].reshape(count * rows, side.shape[2])
        inner = nt(x[:, :width], first_ref[...]).astype(bf16)
        qkv = nn(x[:, :width], w_ref[...]) + LOW_FACTORED * nn(inner, second_ref[...])
        qkv = qkv.astype(bf16)
        for index in range(count):
            own = slice(index * rows, (index + 1) * rows)
            here = block_rows(spots_ref[slot], rows)
            qkv_ref[here, :] = qkv[own]
            inner_ref[here, :] = inner[own]
            turned[:, here] = qkv[own].astype(f32).T.astype(bf16)
            segments = x[own, width:].astype(f32)
            seg_col[here, :] = segments[:, 0:1]
            seg_row[:, here] = segments.T[0:8, :]
            slot += 1
    part = spots_ref[slot]
    if ways > 1:
        att_ref[...] = jnp.zeros_like(att_ref)
        lse_ref[...] = jnp.zeros_like(lse_ref)
    per_tile = 2 if ways == 1 else 1
    tile = per_tile * rows
    for index in range(slot // ways // per_tile):
        kmax = (index + 1) * per_tile * ways * rows
        first_block = index * per_tile * ways + part if ways > 1 else index * per_tile
        start = pl.multiple_of(first_block * rows, rows) if ways > 1 else first_block * rows
        allowed = key_mask(seg_col, seg_row, tile, start, kmax)
        keys = qkv_ref[pl.ds(0, kmax), 0:LANES]
        values_t = turned[ATTENTION_EXTENT:LANES, pl.ds(0, kmax)]
        outs = []
        sums = []
        for head in range(HEADS_PER_PAIR):
            base = LANES + head * ATTENTION_EXTENT
            q_t = turned[base : base + ATTENTION_EXTENT, pl.ds(start, tile)] * SCALE
            q_pad = jnp.concatenate([q_t, jnp.zeros_like(q_t)], axis=0)
            score = jnp.where(allowed, nn(keys, q_pad), MASKED_FLOOR)
            top = jnp.max(score, axis=0, keepdims=True)
            weight = jnp.exp(score - top)
            total = jnp.sum(weight, axis=0, keepdims=True)
            prob = (weight * (1.0 / total)).astype(bf16)
            outs.append(nn(values_t, prob))
            sums.append(top + jnp.log(total))
        packed = jnp.concatenate(outs, axis=0).astype(bf16)
        for block in range(per_tile):
            att_ref[first_block + block] = packed[:, block * rows : (block + 1) * rows]
        lse_ref[:, pl.ds(start, tile)] = jnp.concatenate(
            sums + [jnp.zeros((8 - HEADS_PER_PAIR, tile), f32)], axis=0
        )


def project_attend(spots, x_sides, weights, first, second, ways):
    blocks, rows = sum(v.shape[0] for v in x_sides), x_sides[0].shape[1]
    total = blocks * rows
    return whole_call(
        functools.partial(project_attend_kernel, ways, len(x_sides)),
        (spots,),
        (*x_sides, weights, first, second),
        (
            struct(total, HEAD_COLS), struct(total, first.shape[0]),
            struct(blocks, QUERY_COLS, rows), struct(8, total, dtype=f32),
            struct(total, 1, dtype=f32), struct(8, total, dtype=f32),
        ),
        scratch=(pltpu.VMEM((HEAD_COLS, total), bf16),),
        flops=2 * total * first.shape[1] * 512 + 8 * total * total * 256,
        exps=HEADS_PER_PAIR * total * total,
        name="project_attend",
    )


def attend_back_kernel(ways, sides, width, spots_ref, *refs):
    qkv_ref, adj_ref, lse_ref, second_ref, inner_ref, seg_col, seg_row = refs[:7]
    side_refs = refs[7 : 7 + sides]
    (
        out_tables, grad_ref, inner_grad_ref, pieces_ref, own_ref, turned, adj_turned, grad_kv
    ) = refs[7 + sides :]
    blocks, rows = adj_ref.shape[0], adj_ref.shape[2]
    half = ATTENTION_EXTENT
    wide, span = width // blocks, pieces_ref.shape[2]
    part = spots_ref[blocks]
    for index in range(blocks):
        here = pl.ds(index * rows, rows)
        turned[:, here] = qkv_ref[here, :].astype(f32).T.astype(bf16)
        adj_turned[:, here] = adj_ref[index]
    grad_kv[...] = jnp.zeros_like(grad_kv)
    if ways > 1:
        grad_ref[...] = jnp.zeros_like(grad_ref)
    per_tile = 2 if ways == 1 else 1
    tile = per_tile * rows
    zero = jnp.zeros((half, tile), bf16)
    for index in range(blocks // ways // per_tile):
        kmax = (index + 1) * per_tile * ways * rows
        start = index * tile
        if ways > 1:
            start = pl.multiple_of((index * per_tile * ways + part) * rows, rows)
        allowed = key_mask(seg_col, seg_row, tile, start, kmax)
        keys = qkv_ref[pl.ds(0, kmax), 0:LANES]
        keys_t = turned[0:half, pl.ds(0, kmax)]
        grads_q = []
        update = jnp.zeros((kmax, LANES), f32)
        for head in range(HEADS_PER_PAIR):
            base = LANES + head * half
            q_t = turned[base : base + half, pl.ds(start, tile)] * SCALE
            q_pad = jnp.concatenate([q_t, zero], axis=0)
            a_t = adj_turned[head * half : (head + 1) * half, pl.ds(start, tile)]
            a_pad = jnp.concatenate([zero, a_t], axis=0)
            score = nn(keys, q_pad) - lse_ref[head : head + 1, pl.ds(start, tile)]
            prob = jnp.where(allowed, jnp.exp(jnp.where(allowed, score, 0.0)), 0.0)
            grad_prob = nn(keys, a_pad)
            both = prob * grad_prob
            delta = jnp.sum(both, axis=0, keepdims=True)
            grad_score = (both - prob * delta).astype(bf16)
            update = update + nt(grad_score, q_pad) + nt(prob.astype(bf16), a_pad)
            grads_q.append(nn(keys_t, grad_score) * SCALE)
        grad_kv[pl.ds(0, kmax), :] += update
        packed = jnp.concatenate(grads_q + [jnp.zeros((half, tile), f32)], axis=0)
        grad_ref[pl.ds(start, tile), LANES:] = packed.T.astype(bf16)
    grad_ref[:, 0:LANES] = grad_kv[...].astype(bf16)

    inner_grad_ref[...] = (LOW_FACTORED * nt(grad_ref[...], second_ref[...])).astype(bf16)
    slot = 0
    grad_first = None
    for side in side_refs:
        count = side.shape[0]
        inner_grad = jnp.concatenate(
            [inner_grad_ref[block_rows(spots_ref[slot + i], rows), :] for i in range(count)],
            axis=0,
        )
        x = side[...].reshape(count * rows, side.shape[2])[:, :width]
        term = tn(inner_grad, x)
        grad_first = term if grad_first is None else grad_first + term
        slot += count
    third = wide // 3
    gap = jnp.zeros((RANK, QUERY_COLS - wide), f32)
    for place in range(blocks):
        second = out_tables[place, RANK:, :].astype(f32)
        for index in range(3):
            piece = grad_first[index * RANK : (index + 1) * RANK, place * wide : (place + 1) * wide]
            chunk = second[:, index * third : (index + 1) * third]
            parts = [piece, gap, chunk] if wide < QUERY_COLS else [piece, chunk]
            pieces_ref[place, index * RANK : (index + 1) * RANK, :] = padded(
                jnp.concatenate(parts, axis=1), span
            )
        pieces_ref[place, 3 * RANK :, :] = out_tables[place, 0:RANK, :]
    seconds = LOW_FACTORED * tn(inner_ref[...], grad_ref[...])
    own_ref[0 : 3 * RANK, :] = jnp.zeros((3 * RANK, span), bf16)
    value = seconds[2 * RANK : 3 * RANK, half : 2 * half]
    own_ref[3 * RANK : 4 * RANK, :] = padded(
        jnp.concatenate([jnp.zeros((RANK, QUERY_COLS), f32), value], axis=1), span
    )
    query, key = seconds[0:RANK, LANES : LANES + QUERY_COLS], seconds[RANK : 2 * RANK, 0:half]
    own_ref[4 * RANK :, :] = padded(jnp.concatenate([query, key], axis=1), span)


def padded(piece, span):
    rows, size = piece.shape
    if size < span:
        piece = jnp.concatenate([piece, jnp.zeros((rows, span - size), piece.dtype)], axis=1)
    return piece.astype(bf16)


def attend_back(
    spots, qkv, adj, lse, second, inner, seg_col, seg_row, x_sides, out_tables, width, ways
):
    blocks, rows = adj.shape[0], adj.shape[2]
    total, span = qkv.shape[0], out_tables.shape[2]
    return whole_call(
        functools.partial(attend_back_kernel, ways, len(x_sides), width),
        (spots,),
        (qkv, adj, lse, second, inner, seg_col, seg_row, *x_sides, out_tables),
        (
            struct(total, HEAD_COLS), struct(total, 3 * RANK),
            struct(blocks, 4 * RANK, span), struct(PACKED * RANK, span),
        ),
        scratch=(
            pltpu.VMEM((HEAD_COLS, total), bf16),
            pltpu.VMEM((QUERY_COLS, total), bf16),
            pltpu.VMEM((total, LANES), f32),
        ),
        flops=20 * total * total * 256,
        exps=HEADS_PER_PAIR * total * total,
        name="attend_back",
    )


def rows_back_kernel(first_slot, spots_ref, grad_ref, inner_ref, w_ref, first_ref, rows_ref):
    count, rows, width = rows_ref.shape
    spots = [block_rows(spots_ref[first_slot + i], rows) for i in range(count)]
    grad = jnp.concatenate([grad_ref[spot, :] for spot in spots], axis=0)
    inner = jnp.concatenate([inner_ref[spot, :] for spot in spots], axis=0)
    out = nt(grad, w_ref[...]) + nn(inner, first_ref[...])
    rows_ref[...] = out.astype(bf16).reshape(count, rows, width)


def rows_back(spots, grad, inner, weights, first, x_sides, side):
    count, rows, _ = x_sides[side].shape
    width, cols = weights.shape
    first_slot = sum(v.shape[0] for v in x_sides[:side])
    return whole_call(
        functools.partial(rows_back_kernel, first_slot),
        (spots,),
        (grad, inner, weights, first),
        [struct(count, rows, width)],
        flops=4 * count * rows * width * cols,
        name="rows_back",
    )[0]


OUT_STEPS = 4


def side_specs(sides):
    steps = OUT_STEPS // len(sides)
    specs = []
    for index, side in enumerate(sides):
        shape = (side.shape[0] // steps,) + side.shape[1:]
        specs.append(
            pl.BlockSpec(
                shape,
                lambda i, *_, base=index * steps, last=steps - 1: (
                    jnp.clip(i - base, 0, last), 0, 0
                ),
            )
        )
    return specs


def each_step(side_refs, spots_ref, visit):
    step = pl.program_id(0)
    steps = OUT_STEPS // len(side_refs)
    per_step, wide, width = side_refs[0].shape
    for index, side in enumerate(side_refs):

        @pl.when((step >= index * steps) & (step < (index + 1) * steps))
        def _():
            spots = [
                block_rows(spots_ref[step * per_step + block], wide) for block in range(per_step)
            ]
            visit(spots, side[...].reshape(per_step * wide, width))


def output_project_kernel(sides, spots_ref, *refs):
    side_refs = refs[:sides]
    (
        att_ref, first_ref, second_ref, rows_ref, gain_ref, mid_ref, normed_ref, inner_ref, total
    ) = refs[sides:]
    step = pl.program_id(0)

    @pl.when(step == 0)
    def _():
        total[...] = rows_ref[...].astype(f32)

    def visit(spots, weights):
        att = jnp.concatenate([att_ref[rows, :] for rows in spots], axis=0)
        total[...] += tn(att, weights)

    each_step(side_refs, spots_ref, visit)

    @pl.when(step == OUT_STEPS - 1)
    def _():
        inner = tn(att_ref[...], first_ref[...]).astype(bf16)
        mid = total[...] + LOW_FACTORED * nn(inner, second_ref[...])
        mid_ref[...] = mid
        inner_ref[...] = inner
        normed_ref[...] = normed(mid, gain_ref[...])[0].astype(bf16)


def output_project(spots, w_sides, att, first, second, rows, gain):
    count, width = rows.shape
    outs = (struct(count, width, dtype=f32), struct(count, width), struct(count, LANES))
    rest = (att, first, second, rows, gain)
    return pl.pallas_call(
        functools.partial(output_project_kernel, len(w_sides)),
        grid_spec=pltpu.PrefetchScalarGridSpec(
            num_scalar_prefetch=1,
            grid=(OUT_STEPS,),
            in_specs=side_specs(w_sides) + [whole_block(v.shape) for v in rest],
            out_specs=[whole_block(v.shape) for v in outs],
            scratch_shapes=[pltpu.VMEM((count, width), f32)],
        ),
        out_shape=outs,
        compiler_params=call_params(),
        cost_estimate=NO_COST,
        name="output_project",
    )(spots, *w_sides, *rest)


def output_back_kernel(sides, parts, spots_ref, *refs):
    side_refs, part_refs = refs[:sides], refs[sides : sides + parts]
    (
        att_ref, first_ref, mid_ref, gain_ref, out_grad_ref, second_ref, inner_ref,
        adj_ref, tables_ref, grad_mid_ref, branch, grad_inner,
    ) = refs[sides + parts :]
    step = pl.program_id(0)
    places, _, span = tables_ref.shape
    wide = mid_ref.shape[1] // places

    @pl.when(step == 0)
    def _():
        grad = sum([v[...].astype(f32) for v in part_refs[1:]], part_refs[0][...].astype(f32))
        mid = mid_ref[...]
        factor = lax.rsqrt(jnp.mean(mid * mid, axis=-1, keepdims=True) + EPS)
        grad_mid = out_grad_ref[...].astype(f32) + norm_back(mid, factor, gain_ref[...], grad)
        grad_mid_ref[...] = grad_mid
        low = grad_mid.astype(bf16)
        branch[...] = low
        grad_inner[...] = (LOW_FACTORED * nt(low, second_ref[...])).astype(bf16)

    def visit(spots, weights):
        first = jnp.concatenate([first_ref[rows, :] for rows in spots], axis=0)
        adj = (nt(weights, branch[...]) + nt(first, grad_inner[...])).astype(bf16)
        wide = adj.shape[0] // len(spots)
        for index, rows in enumerate(spots):
            adj_ref[rows, :] = adj[index * wide : (index + 1) * wide]

    each_step(side_refs, spots_ref, visit)

    @pl.when(step == OUT_STEPS - 1)
    def _():
        firsts = tn(grad_inner[...], att_ref[...].T)
        seconds = LOW_FACTORED * tn(inner_ref[...], branch[...])
        for place in range(places):
            own = slice(place * wide, (place + 1) * wide)
            tables_ref[place, 0:RANK, :] = padded(firsts[0:RANK, own], span)
            tables_ref[place, RANK:, :] = padded(seconds[0:RANK, own], span)


def output_back(
    spots, w_sides, att, first, parts, mid, gain, out_grad, second, inner, places, span
):
    count, width = mid.shape
    outs = (
        struct(*att.shape), struct(places, 2 * RANK, span), struct(count, width, dtype=f32)
    )
    rest = (*parts, att, first, mid, gain, out_grad, second, inner)
    return pl.pallas_call(
        functools.partial(output_back_kernel, len(w_sides), len(parts)),
        grid_spec=pltpu.PrefetchScalarGridSpec(
            num_scalar_prefetch=1,
            grid=(OUT_STEPS,),
            in_specs=side_specs(w_sides) + [whole_block(v.shape) for v in rest],
            out_specs=[whole_block(v.shape) for v in outs],
            scratch_shapes=[
                pltpu.VMEM((count, width), bf16), pltpu.VMEM((count, LANES), bf16)
            ],
        ),
        out_shape=outs,
        compiler_params=call_params(),
        cost_estimate=NO_COST,
        name="output_back",
    )(spots, *w_sides, *rest)


PACKED = 5


def attend_tables_kernel(ways, sides, place_ref, adapter_ref, *refs):
    side_refs, out_refs = refs[:sides], refs[sides:]
    per_side, sources = side_refs[0].shape[0], side_refs[0].shape[1] // (PACKED * RANK)
    blocks = per_side * sides
    wide = out_refs[0].shape[2] // blocks
    third = wide // 3
    half = ATTENTION_EXTENT

    def read(place, source, index):
        slot = place_ref[place]
        rows = pl.ds((source * PACKED + index) * RANK, RANK)
        value = side_refs[0][lax.rem(slot, per_side), rows, :]
        if sides > 1:
            value = jnp.where(slot < per_side, value, side_refs[1][lax.rem(slot, per_side), rows, :])
        return value.astype(f32)

    def by_head(pieces):
        return [
            sum(pieces[h * ways + 1 : (h + 1) * ways], pieces[h * ways])
            for h in range(PAIRED_ATTENDERS)
        ]

    for out_ref in out_refs:
        out_ref[...] = jnp.zeros_like(out_ref)
    for source in range(sources):
        adapter = adapter_ref[source]
        got = [[read(c, source, index) for c in range(blocks)] for index in range(PACKED)]
        pieces = [[v[:, :wide] for v in got[index]] for index in range(4)]
        pieces.append([
            got[index][c][:, QUERY_COLS : QUERY_COLS + third]
            for c in range(blocks) for index in range(3)
        ])
        pieces.append(by_head([v[:, :QUERY_COLS] for v in got[4]]))
        pieces.append(by_head([v[:, QUERY_COLS : QUERY_COLS + half] for v in got[4]]))
        pieces.append(by_head([v[:, QUERY_COLS : QUERY_COLS + half] for v in got[3]]))
        for parts, out_ref in zip(pieces, out_refs):
            out_ref[adapter] = out_ref[adapter] + jnp.concatenate(parts, axis=1)


def attend_tables(place, adapters, sides, width, ways):
    key_cols = PAIRED_ATTENDERS * ATTENTION_EXTENT
    cols = (width,) * 5 + (ASKING_ATTENDERS * ATTENTION_EXTENT, key_cols, key_cols)
    return whole_call(
        functools.partial(attend_tables_kernel, ways, len(sides)),
        (place, adapters),
        sides,
        [struct(NUM_CHOICES_X, RANK, size, dtype=f32) for size in cols],
        name="attend_tables",
    )


def expert_tables_kernel(sizes, sources, terms, adapter_ref, *refs):
    term_refs, out_refs = refs[:terms], refs[terms:]
    adapter = pl.program_id(0)
    for out_ref in out_refs:
        out_ref[...] = jnp.zeros_like(out_ref)
    for source in range(sources):

        @pl.when(adapter_ref[source] == adapter)
        def _():
            for expert in range(term_refs[0].shape[0]):
                own = None
                for term_ref in term_refs:
                    term = term_ref[expert, source * RANK : (source + 1) * RANK, :].astype(f32)
                    own = term if own is None else own + term
                start = 0
                for size, out_ref in zip(sizes, out_refs):
                    out_ref[0, expert] += own[:, start : start + size]
                    start += size


def expert_tables(adapters, terms, wide, slim):
    experts, sources = terms[0].shape[0], adapters.shape[0]
    sizes = (wide,) * 3 + (slim,) * 3
    return pl.pallas_call(
        functools.partial(expert_tables_kernel, sizes, sources, len(terms)),
        grid_spec=pltpu.PrefetchScalarGridSpec(
            num_scalar_prefetch=1,
            grid=(NUM_CHOICES_X,),
            in_specs=[whole_block(v.shape) for v in terms],
            out_specs=[
                pl.BlockSpec((1, experts, RANK, size), lambda a, adapters: (a, 0, 0, 0))
                for size in sizes
            ],
        ),
        out_shape=[
            jax.ShapeDtypeStruct((NUM_CHOICES_X, experts, RANK, size), f32) for size in sizes
        ],
        compiler_params=call_params(),
        cost_estimate=NO_COST,
        name="expert_tables",
    )(adapters, *terms)


def source_mask(shape, sources):
    row = lax.broadcasted_iota(jnp.int32, shape, 0)
    col = lax.broadcasted_iota(jnp.int32, shape, 1)
    keep = None
    for source in range(sources):
        inside = (row >= source * CAP) & (row < (source + 1) * CAP)
        inside &= (lax.rem(col, sources * RANK) >= source * RANK) & (
            lax.rem(col, sources * RANK) < (source + 1) * RANK
        )
        keep = inside if keep is None else keep | inside
    return keep


def masked(values, sources):
    return jnp.where(source_mask(values.shape, sources), values, 0.0)


def picks(slot_ref, pair, tokens, unit=0):
    slots = slot_ref[unit, :, pair * 2 * tokens : (pair + 1) * 2 * tokens]
    place = lax.broadcasted_iota(jnp.int32, (2 * CAP, 2 * tokens), 0)
    return place == slots


def picked_rows(slot_ref, rows_ref, sources, unit=0):
    tokens = rows_ref.shape[0] // sources
    parts = []
    for pair in range(sources // 2):
        pick = picks(slot_ref, pair, tokens, unit).astype(f32).astype(bf16)
        rows = rows_ref[pair * 2 * tokens : (pair + 1) * 2 * tokens, :]
        parts.append(nn(pick, rows))
    return jnp.concatenate(parts, axis=0)


def picked_gates(slot_ref, gate_ref, sources, unit=0):
    tokens = gate_ref.shape[2] // sources
    parts = []
    for pair in range(sources // 2):
        gate = gate_ref[unit, :, pair * 2 * tokens : (pair + 1) * 2 * tokens]
        kept = jnp.where(picks(slot_ref, pair, tokens, unit), gate, 0.0)
        parts.append(jnp.sum(kept, axis=1, keepdims=True))
    return jnp.concatenate(parts, axis=0)


def combine(target_ref, values, out_refs):
    sources = len(out_refs)
    tokens = target_ref.shape[0] // sources
    slots = values.shape[1]
    for source, out_ref in enumerate(out_refs):
        target = target_ref[source * tokens : (source + 1) * tokens, :]
        place = lax.broadcasted_iota(jnp.int32, (tokens, slots), 1)
        hit = place == target[:, 0:1]
        for choice in range(1, TOPK):
            hit |= place == target[:, choice : choice + 1]
        out_ref[...] = nn(hit.astype(f32).astype(bf16), values[source]).astype(bf16)


def keep_rows(values, rows, expert, sources):
    for source in range(sources):
        values[source, pl.ds(pl.multiple_of(expert * CAP, CAP), CAP), :] = rows[
            source * CAP : (source + 1) * CAP
        ]


def joined(refs, unit=0):
    return jnp.concatenate([ref[0, unit] for ref in refs], axis=0)


def experts_pre_kernel(sources, adapter_ref, slot_ref, gate_ref, grads_ref, down_ref, *refs):
    down_first, down_second = joined(refs[:sources]), joined(refs[sources : 2 * sources])
    picked_ref, hidden_ref, inner_ref = refs[2 * sources :]
    grads = picked_rows(slot_ref, grads_ref, sources)
    grads = (grads * picked_gates(slot_ref, gate_ref, sources)).astype(bf16)
    picked_ref[0] = grads
    inner = LOW_FACTORED * nt(grads, down_second)
    inner = masked(inner, sources).astype(bf16)
    inner_ref[0] = inner
    hidden_ref[0] = nt(grads, down_ref[0]) + nn(inner, down_first)


def experts_main_kernel(
    sources, adapter_ref, slot_ref, gate_w, up_w, grad_hidden, target_ref, *refs
):
    x_refs, refs = refs[:sources], refs[sources:]
    groups = [refs[i * sources : (i + 1) * sources] for i in range(4)]
    picked_ref, hidden_ref, adj_ref, inner_ref, *out_refs, values, x_ref = refs[4 * sources :]
    per_step, width, inner_size = gate_w.shape
    span = 2 * sources * RANK

    @pl.when(pl.program_id(0) == 0)
    def _():
        tokens = x_refs[0].shape[0]
        for source in range(sources):
            x_ref[source * tokens : (source + 1) * tokens, :] = x_refs[source][...]

    firsts, seconds = [], []
    for unit in range(per_step):
        firsts.append(
            jnp.concatenate([joined(groups[0], unit), joined(groups[1], unit)], axis=0)
        )
        gate_second, up_second = joined(groups[2], unit), joined(groups[3], unit)
        blank = jnp.zeros_like(gate_second)
        seconds.append(
            jnp.concatenate(
                [
                    jnp.concatenate([gate_second, blank], axis=1),
                    jnp.concatenate([blank, up_second], axis=1),
                ],
                axis=0,
            )
        )
        picked_ref[unit] = picked_rows(slot_ref, x_ref, sources, unit).astype(bf16)
        inner = masked(LOW_FACTORED * nt(picked_ref[unit], firsts[unit]), sources)
        inner_ref[unit, :, :span] = inner.astype(bf16)
    for unit in range(per_step):
        x = picked_ref[unit]
        inner = inner_ref[unit, :, :span]
        for start in range(0, inner_size, 2 * LANES):
            cols = slice(start, start + 2 * LANES)
            ups = slice(inner_size + start, inner_size + start + 2 * LANES)
            gate = nn(x, gate_w[unit, :, cols]) + nn(inner, seconds[unit][:, cols])
            up = nn(x, up_w[unit, :, cols]) + nn(inner, seconds[unit][:, ups])
            sigma = 1.0 / (1.0 + jnp.exp(-gate))
            active = gate * sigma
            hidden_ref[unit, :, cols] = (active * up).astype(bf16)
            adj = grad_hidden[unit, :, cols]
            grad_gate = adj * up * sigma * (1.0 + gate * (1.0 - sigma))
            adj_ref[unit, :, cols] = grad_gate.astype(bf16)
            adj_ref[unit, :, ups] = (adj * active).astype(bf16)
    for unit in range(per_step):
        grad_inner = masked(LOW_FACTORED * nt(adj_ref[unit], seconds[unit]), sources)
        inner_ref[unit, :, span:] = grad_inner.astype(bf16)
    for unit in range(per_step):
        rows = nt(adj_ref[unit, :, :inner_size], gate_w[unit])
        rows = rows + nt(adj_ref[unit, :, inner_size:], up_w[unit])
        rows = rows + nn(inner_ref[unit, :, span:], firsts[unit])
        expert = pl.program_id(0) * per_step + unit
        keep_rows(values, rows.astype(bf16), expert, sources)

    @pl.when(pl.program_id(0) == pl.num_programs(0) - 1)
    def _():
        combine(target_ref, values, out_refs)


def experts_post_kernel(
    sources, cohort, adapter_ref, slot_ref, gate_ref, down_ref, picked_ref, hidden_ref, adj_ref,
    inner_ref, picked_grads, grad_inner_down, target_ref, *refs
):
    groups = [refs[i * sources : (i + 1) * sources] for i in range(2)]
    table_ref, *out_refs, values = refs[2 * sources :]
    per_step = hidden_ref.shape[0]
    units = range(per_step)
    span = sources * RANK
    width, inner_size = picked_ref.shape[2], hidden_ref.shape[2]
    wide, slim = width // cohort, inner_size // cohort
    inner_down = [
        masked(nt(hidden_ref[u], joined(groups[0], u)), sources).astype(bf16) for u in units
    ]
    for unit in units:
        answer = nn(hidden_ref[unit], down_ref[unit])
        answer = answer + LOW_FACTORED * nn(inner_down[unit], joined(groups[1], unit))
        gates = picked_gates(slot_ref, gate_ref, sources, unit)
        answer = answer.astype(bf16).astype(f32) * gates
        expert = pl.program_id(0) * per_step + unit
        keep_rows(values, answer.astype(bf16), expert, sources)
    for unit in units:
        hidden = hidden_ref[unit]
        firsts = tn(inner_ref[unit, :, 2 * span :], picked_ref[unit])
        seconds = tn(inner_ref[unit, :, : 2 * span], adj_ref[unit])
        down_firsts = tn(grad_inner_down[unit], hidden)
        down_seconds = LOW_FACTORED * tn(inner_down[unit], picked_grads[unit])
        wide_parts = (firsts[:span], firsts[span:], down_seconds)
        slim_parts = (seconds[:span, :inner_size], seconds[span:, inner_size:], down_firsts)
        for place in range(cohort):
            pieces = [v[:, place * wide : (place + 1) * wide] for v in wide_parts]
            pieces += [v[:, place * slim : (place + 1) * slim] for v in slim_parts]
            table_ref[place, unit] = jnp.concatenate(pieces, axis=1).astype(bf16)

    @pl.when(pl.program_id(0) == pl.num_programs(0) - 1)
    def _():
        combine(target_ref, values, out_refs)


def per_expert(array, per_step=1):
    rest = array.shape[1:]
    return pl.BlockSpec((per_step,) + rest, lambda e, *_: (e,) + (0,) * len(rest))


def expert_rows(rows, width, per_step=1):
    return pl.BlockSpec((per_step, rows, width), lambda e, *_: (e, 0, 0))


def adapter_blocks(table, sources, per_step):
    shape = (1, per_step) + table.shape[2:]
    return [
        pl.BlockSpec(shape, lambda e, adapters, *_, s=s: (adapters[s], e, 0, 0))
        for s in range(sources)
    ]


def expert_call(
    kernel, sources, scalars, arrays, specs, tables, out_shape, out_specs, scratch, name,
    per_step=1,
):
    experts = tables[0].shape[1]
    return pl.pallas_call(
        kernel,
        grid_spec=pltpu.PrefetchScalarGridSpec(
            num_scalar_prefetch=len(scalars),
            grid=(experts // per_step,),
            in_specs=specs
            + [spec for t in tables for spec in adapter_blocks(t, sources, per_step)],
            out_specs=out_specs,
            scratch_shapes=scratch,
        ),
        out_shape=out_shape,
        compiler_params=call_params(),
        cost_estimate=NO_COST,
        name=name,
    )(*scalars, *arrays, *[t for t in tables for _ in range(sources)])


def experts_pre(adapters, slots, gates, grads, down, down_first, down_second):
    experts, inner_size, width = down.shape
    sources = adapters.shape[0]
    rows = sources * CAP
    return expert_call(
        functools.partial(experts_pre_kernel, sources),
        sources,
        (adapters,),
        (slots, gates, grads, down),
        [
            per_expert(slots), per_expert(gates), whole_block((grads.shape[0], width)),
            per_expert(down),
        ],
        (down_first, down_second),
        [
            struct(experts, rows, width), struct(experts, rows, inner_size, dtype=f32),
            struct(experts, rows, sources * RANK),
        ],
        [expert_rows(rows, v) for v in (width, inner_size, sources * RANK)],
        [],
        "experts_pre",
    )


def experts_main(
    adapters, slots, x_blocks, gate_w, up_w, grad_hidden, target, gate_first, up_first,
    gate_second, up_second,
):
    experts, width, inner_size = gate_w.shape
    sources = adapters.shape[0]
    rows = sources * CAP
    tokens = x_blocks[0].shape[0]
    per_step = 2 if experts % 2 == 0 else 1
    outs = (width, inner_size, 2 * inner_size, 4 * sources * RANK)
    return expert_call(
        functools.partial(experts_main_kernel, sources),
        sources,
        (adapters,),
        (slots, gate_w, up_w, grad_hidden, target, *x_blocks),
        [
            per_expert(slots, per_step), per_expert(gate_w, per_step), per_expert(up_w, per_step),
            per_expert(grad_hidden, per_step), whole_block(target.shape),
        ]
        + [whole_block(v.shape) for v in x_blocks],
        (gate_first, up_first, gate_second, up_second),
        [struct(experts, rows, v) for v in outs] + [struct(tokens, width)] * sources,
        [expert_rows(rows, v, per_step) for v in outs]
        + [whole_block((tokens, width))] * sources,
        [
            pltpu.VMEM((sources, experts * CAP, width), bf16),
            pltpu.VMEM((sources * tokens, width), bf16),
        ],
        "experts_main",
        per_step,
    )


def experts_post(
    adapters, slots, gates, down, picked, hidden, adj, inner, picked_grads, grad_inner_down,
    target, down_first, down_second, cohort,
):
    experts, inner_size, width = down.shape
    sources = adapters.shape[0]
    tokens = target.shape[0] // sources
    per_step = 2 if experts % 2 == 0 else 1
    lanes = 3 * (width + inner_size) // cohort
    arrays = (
        slots, gates, down, picked, hidden, adj, inner, picked_grads, grad_inner_down
    )
    return expert_call(
        functools.partial(experts_post_kernel, sources, cohort),
        sources,
        (adapters,),
        arrays + (target,),
        [per_expert(v, per_step) for v in arrays] + [whole_block(target.shape)],
        (down_first, down_second),
        [struct(cohort, experts, sources * RANK, lanes)] + [struct(tokens, width)] * sources,
        [
            pl.BlockSpec((cohort, per_step, sources * RANK, lanes), lambda e, *_: (0, e, 0, 0)),
        ]
        + [whole_block((tokens, width))] * sources,
        [pltpu.VMEM((sources, experts * CAP, width), bf16)],
        "experts_post",
        per_step,
    )


def flipped(array, axis, size, mask):
    return lax.ppermute(array, axis, [(i, i ^ mask) for i in range(size)])


def ring_blocks(array, axis, size):
    return [array] + [
        lax.ppermute(array, axis, [(i, (i + shift) % size) for i in range(size)])
        for shift in range(1, size)
    ]


def ring_return(blocks, axis, size):
    return [blocks[0]] + [
        lax.ppermute(blocks[shift], axis, [(i, (i - shift) % size) for i in range(size)])
        for shift in range(1, size)
    ]


def to_every(array, axis, size):
    return lax.all_to_all(
        jnp.broadcast_to(array[None], (size,) + array.shape), axis, 0, 0, tiled=True
    )


def cohort_spots(size):
    place = jnp.arange(size, dtype=jnp.int32)
    if size != 8:
        return place, place
    me = lax.axis_index("ctx")
    mask = place ^ me
    return (place % 4 * 2 + place // 4) ^ me, (mask & 1) * 4 + mask // 2


def gather_cohort(array, size, halves=False, stage=lambda blocks: blocks):
    if size != 8:
        return (lax.all_gather(array, "ctx", axis=0, tiled=False),)
    if halves:
        half = array.shape[0] // 2
        near, far = flipped(array, "ctx", size, 2), flipped(array, "ctx", size, 4)
        low, high = stage(
            [flipped(near[:half], "ctx", size, 4), flipped(far[half:], "ctx", size, 2)]
        )
        blocks = [near, far, jnp.concatenate([low, high], axis=0)]
    else:
        blocks = stage([flipped(array, "ctx", size, mask) for mask in (2, 4, 6)])
    mine = jnp.stack([array] + blocks)
    return mine, flipped(mine, "ctx", size, 1)


def staged_sums(pieces, row_sides, summed, terms, tables_of, size, sources):
    tie = lax.optimization_barrier

    def plus(left, right):
        return (left.astype(f32) + right.astype(f32)).astype(bf16)

    other, row_side, pieces = tie((flipped(row_sides[1], "ctx", size, 1), row_sides[0], pieces))
    mine = plus(row_side, other)
    half = mine.shape[1] // 2
    low, high = mine[:, :half], mine[:, half:]
    near, far, slip = tie(
        (jnp.stack([low[1], low[3]]), jnp.stack([high[2], high[3]]), summed(pieces))
    )
    beside = tables_of(terms)
    near, far, groups = tie(
        (
            flipped(near, "ctx", size, 2), flipped(far, "ctx", size, 4),
            to_every(slip, "exp", sources),
        )
    )
    low_last, high_last, groups = tie(
        (plus(low[2], near[1]), plus(high[1], far[1]), groups.reshape(-1, slip.shape[1]))
    )
    low_last, high_last, blocks, beside = tie(
        (
            flipped(low_last, "ctx", size, 4), flipped(high_last, "ctx", size, 2),
            [flipped(groups, "ctx", size, mask) for mask in (2, 4, 6)], beside,
        )
    )
    mine = jnp.stack([groups] + blocks)
    low_sum = low[0].astype(f32) + near[0].astype(f32) + low_last.astype(f32)
    high_sum = high[0].astype(f32) + far[0].astype(f32) + high_last.astype(f32)
    rows = jnp.concatenate([low_sum, high_sum], axis=0)
    return (mine, flipped(mine, "ctx", size, 1)), rows, beside


def head_columns(query, key, value):
    rows = query.shape[0]

    def split(array):
        return jnp.transpose(array.reshape(rows, PAIRED_ATTENDERS, -1), (1, 0, 2))

    parts = [split(key), split(value), split(query)]
    pad = HEAD_COLS - sum(p.shape[2] for p in parts)
    parts.append(jnp.zeros((PAIRED_ATTENDERS, rows, pad), query.dtype))
    return jnp.concatenate(parts, axis=2)


def body(
    tokens, out_grad, attn_gain, moe_gain, w_query, lock_projection, content_projection, w_out,
    sigmoid_matrices, widener_matrices, reducer_matrices, segment_ids, expert_routes,
    route_weights, adapter_index, query_first, query_second, key_first, lock_final_matrices,
    value_first, content_final_matrices, output_first, output_second, gate_first, gate_second,
    upward_first, upward_second, down_first, down_second,
):
    rows_in = tokens[0].astype(f32)
    count, width = rows_in.shape
    cohort = lax.axis_size("ctx")
    sources = lax.axis_size("exp")
    experts = sigmoid_matrices.shape[0]
    ctx = lax.axis_index("ctx")
    exp = lax.axis_index("exp")
    ways = cohort // PAIRED_ATTENDERS
    head = ctx // ways
    adapter = adapter_index[exp]

    def elected(table):
        return lax.dynamic_index_in_dim(table, adapter, 0, keepdims=False)

    attended_cols = ASKING_ATTENDERS * ATTENTION_EXTENT
    wide = width // cohort
    span = -(-max(wide, QUERY_COLS) // LANES) * LANES
    spots, place = cohort_spots(cohort)
    order = jnp.concatenate([spots, (ctx % ways)[None].astype(jnp.int32)])

    normed_in, factor_in = normed(rows_in, attn_gain)
    labels = jnp.pad(segment_ids[0].astype(bf16)[:, None], ((0, 0), (0, LANES - 1)))
    x_sides = gather_cohort(
        jnp.concatenate([normed_in.astype(bf16), labels], axis=1), cohort, True
    )
    relative = (exp - jnp.arange(sources, dtype=jnp.int32) + sources) % sources
    out_rows = jnp.stack(ring_blocks(w_out, "exp", sources))[relative].reshape(-1, width)
    head_w = head_columns(w_query, lock_projection, content_projection)
    to_all = jnp.broadcast_to(
        head_w[:, None], (PAIRED_ATTENDERS, ways * sources) + head_w.shape[1:]
    ).reshape((cohort * sources,) + head_w.shape[1:])
    own_w = lax.all_to_all(to_all, ("ctx", "exp"), 0, 0, tiled=True).reshape(width, HEAD_COLS)

    routes = expert_routes[0].astype(bf16)
    weight_high = route_weights[0].astype(bf16)
    weight_low = (route_weights[0] - weight_high.astype(f32)).astype(bf16)
    parcel = jnp.concatenate(
        [
            out_grad[0], routes, weight_high, weight_low,
            jnp.zeros((count, LANES - 3 * TOPK), bf16),
        ],
        axis=1,
    )
    parcel, own_w = lax.optimization_barrier((parcel, own_w))
    parcels = ring_blocks(parcel, "exp", sources)

    own_firsts = jnp.concatenate(
        [elected(query_first), elected(key_first), elected(value_first)], axis=0
    )

    def head_part(table):
        part = elected(table)
        size = part.shape[1] // PAIRED_ATTENDERS
        return lax.dynamic_slice_in_dim(part, head * size, size, 1)

    def placed(part, row, col):
        return jnp.pad(
            part, ((row, 2 * RANK - row), (col, HEAD_COLS - col - part.shape[1]))
        )

    own_seconds = (
        placed(head_part(query_second), 0, LANES)
        + placed(head_part(lock_final_matrices), RANK, 0)
        + placed(head_part(content_final_matrices), 2 * RANK, ATTENTION_EXTENT)
    )
    qkv, inner, attended, lse, seg_col, seg_row = project_attend(
        order, x_sides, own_w, own_firsts, own_seconds, ways
    )
    shared = [lax.all_to_all(attended, "ctx", 0, 0, tiled=True)]

    def beside_attention(blocks):
        blocks, shared[0], parcels[:] = lax.optimization_barrier((blocks, shared[0], parcels))
        return blocks

    out_sides = gather_cohort(out_rows, cohort, True, beside_attention)
    attended = shared[0]
    if ways > 1:
        attended = attended.reshape(PAIRED_ATTENDERS, ways, QUERY_COLS, count)
        attended = attended.astype(f32).sum(1).astype(bf16)
    attended = attended.reshape(attended_cols, count)
    out_first = jnp.pad(elected(output_first), ((0, LANES - RANK), (0, 0)))
    out_first = out_first.T
    out_second = jnp.pad(elected(output_second), ((0, LANES - RANK), (0, 0)))
    mid, normed_mid, inner_out = output_project(
        spots, out_sides, attended, out_first, out_second, tokens[0], moe_gain[None]
    )
    x_exp = ring_blocks(normed_mid, "exp", sources)

    parcels, normed_mid = lax.optimization_barrier((parcels, normed_mid))
    parcels = jnp.concatenate(parcels, axis=0)
    extra = parcels[:, width:].astype(f32).reshape(sources, count, -1)
    all_routes = extra[:, :, :TOPK].astype(jnp.int32) - exp * experts
    all_gates = extra[:, :, TOPK : 2 * TOPK] + extra[:, :, 2 * TOPK : 3 * TOPK]
    hits = all_routes[None] == jnp.arange(experts, dtype=jnp.int32)[:, None, None, None]
    named = jnp.any(hits, axis=3)
    gates = jnp.sum(jnp.where(hits, all_gates[None], 0.0), axis=3).reshape(experts, 1, -1)
    earlier = jnp.tril(jnp.ones((count, count), bf16), -1)
    rank = lax.dot_general(
        named.astype(bf16), earlier, (((2,), (1,)), ((), ())), preferred_element_type=f32
    ).astype(jnp.int32)
    side = (jnp.arange(sources, dtype=jnp.int32) % 2 * CAP)[None, :, None]
    slots = jnp.where(named, rank + side, -1).reshape(experts, 1, -1)
    places = jnp.arange(experts, dtype=jnp.int32)[:, None, None] * CAP + rank + 1
    target = jnp.sum(jnp.where(hits, places[..., None], 0), axis=0) - 1
    target = target.reshape(sources * count, TOPK)

    adapters = adapter_index[relative]
    picked_grads, grad_hidden, grad_inner_down = experts_pre(
        adapters, slots, gates, parcels, reducer_matrices, down_first, down_second
    )
    picked, hidden, adj, inner_rows, *grad_parts = experts_main(
        adapters, slots, x_exp, sigmoid_matrices, widener_matrices, grad_hidden, target,
        gate_first, upward_first, gate_second, upward_second,
    )
    grad_parts = ring_return(grad_parts, "exp", sources)
    tables, *answers = experts_post(
        adapters, slots, gates, reducer_matrices, picked, hidden, adj, inner_rows,
        picked_grads, grad_inner_down, target, down_first, down_second, cohort,
    )
    tables, answers, grad_parts = lax.optimization_barrier((tables, answers, grad_parts))
    answers = ring_return(answers, "exp", sources)
    early, middle = answers[:2] + answers[3:], answers[2:3]
    terms = [lax.psum_scatter(tables, "ctx", scatter_dimension=0, tiled=False)]

    adj_blocks, out_tables, grad_mid = output_back(
        spots, out_sides, attended, out_first, grad_parts, mid, moe_gain[None], out_grad[0], out_second,
        inner_out, cohort, span,
    )
    adj_blocks = jnp.repeat(adj_blocks.reshape(-1, QUERY_COLS, count), ways, axis=0)
    adj_all = lax.all_to_all(adj_blocks, "ctx", 0, 0, tiled=True)
    adj_all, early = lax.optimization_barrier((adj_all, early))
    grad_heads, grad_inner, pieces, own_seconds_grad = attend_back(
        order, qkv, adj_all, lse, own_seconds, inner, seg_col, seg_row, x_sides, out_tables,
        width, ways,
    )

    def tables_of(terms):
        return expert_tables(adapters, terms, wide, sigmoid_matrices.shape[2] // cohort)

    grad_heads, pieces, middle = lax.optimization_barrier((grad_heads, pieces, middle))

    pieces = lax.all_to_all(pieces, "ctx", 0, 0, tiled=True)
    row_sides = [
        rows_back(order, grad_heads, grad_inner, own_w, own_firsts, x_sides, side)
        for side in reversed(range(len(x_sides)))
    ][::-1]

    def summed(pieces):
        total = jnp.pad(pieces.astype(f32).sum(0), ((0, RANK), (0, 0)))
        return (total + own_seconds_grad.astype(f32)).astype(bf16)

    if cohort != 8:
        groups = to_every(summed(pieces), "exp", sources)
        group_sides = gather_cohort(groups.reshape(-1, span), cohort)
        grad_normed_in = lax.psum_scatter(row_sides[0], "ctx", scatter_dimension=0).astype(f32)
        expert_grads = tables_of(terms)
    else:
        group_sides, grad_normed_in, expert_grads = staged_sums(
            pieces, row_sides, summed, terms, tables_of, cohort, sources
        )
    block_out = (mid + sum(v.astype(f32) for v in early + middle)).astype(bf16)[None]
    attention_tables = attend_tables(place, adapter_index, group_sides, width, ways)
    tokens_grad = (
        grad_mid + norm_back(rows_in, factor_in, attn_gain, grad_normed_in)
    ).astype(bf16)[None]
    gate_f, up_f, down_s, gate_s, up_s, down_f = expert_grads
    attention_tables = attend_tables(place, adapter_index, group_sides, width, ways)
    query_f, key_f, value_f, out_f, out_s, query_s, key_s, value_s = attention_tables
    return (
        block_out, tokens_grad, query_f, query_s, key_f, key_s, value_f, value_s, out_f, out_s,
        gate_f, gate_s, up_f, up_s, down_f, down_s,
    )


def solution(mesh):
    sharded = P("exp", "ctx", None)
    rows = P(("ctx", "exp"), None)
    table = P(None, "exp", None, None)
    expert = P("exp", None, None)
    in_specs = (
        (sharded, sharded, P(), P())
        + (rows,) * 4
        + (expert,) * 3
        + (P("exp", "ctx"), sharded, sharded, P())
        + (P(),) * 8
        + (table,) * 6
    )
    out_specs = (sharded, sharded) + (P(),) * 8 + (P(None, "exp", None, "ctx"),) * 6
    return jax.shard_map(body, mesh=mesh, in_specs=in_specs, out_specs=out_specs, check_vma=False)
```

```python
import functools

import jax
import jax.numpy as jnp
from jax import lax
from jax.experimental import pallas as pl
from jax.experimental.pallas import tpu as pltpu
from jax.sharding import PartitionSpec as P

ASKING_ATTENDERS = 24
PAIRED_ATTENDERS = 8
ATTENTION_EXTENT = 64
HEADS_PER_PAIR = ASKING_ATTENDERS // PAIRED_ATTENDERS
QUERY_COLS = HEADS_PER_PAIR * ATTENTION_EXTENT
EXPERTS = 40
TOPK = 8
NUM_CHOICES_X = 8
CAP = 48
RANK = 16
LANES = 128

EPS = 1e-06
LOW_FACTORED = 2.0
MASKED_FLOOR = -1e30
SCALE = 0.125
VMEM_LIMIT = 56 * 1024 * 1024

bf16 = jnp.bfloat16
f32 = jnp.float32

NO_COST = pl.CostEstimate(flops=0, bytes_accessed=0, transcendentals=0)

HEAD_COLS = 384


def nn(left, right):
    return jnp.dot(left, right, preferred_element_type=f32)


def nt(left, right):
    return lax.dot_general(left, right, (((1,), (1,)), ((), ())), preferred_element_type=f32)


def tn(left, right):
    return lax.dot_general(left, right, (((0,), (0,)), ((), ())), preferred_element_type=f32)


def normed(rows, gain):
    factor = lax.rsqrt(jnp.mean(rows * rows, axis=-1, keepdims=True) + EPS)
    return rows * factor * gain, factor


def norm_back(rows, factor, gain, adjoint):
    weighted = adjoint * gain
    central = jnp.mean(weighted * rows, axis=-1, keepdims=True)
    return factor * (weighted - rows * factor * factor * central)


def whole_block(shape):
    return pl.BlockSpec(shape, lambda *ids: (0,) * len(shape))


def call_params(axes=1):
    return pltpu.CompilerParams(
        dimension_semantics=("arbitrary",) * axes, vmem_limit_bytes=VMEM_LIMIT
    )


def key_floor(seg_col, seg_row, tile, start, kmax):
    key_place = lax.broadcasted_iota(jnp.int32, (kmax, tile), 0)
    query_place = start + lax.broadcasted_iota(jnp.int32, (kmax, tile), 1)
    key_seg = seg_col[pl.ds(0, kmax), :]
    query_seg = seg_row[0:1, pl.ds(start, tile)]
    same = (key_seg == query_seg) | (key_seg == 0.0)
    floor = jnp.where((key_place <= query_place) & same, 0.0, MASKED_FLOOR)
    return jnp.concatenate([floor] * HEADS_PER_PAIR, axis=1)


def heads_beside(turned, first_row, start, tile):
    return jnp.concatenate(
        [
            turned[
                first_row + head * ATTENTION_EXTENT : first_row + (head + 1) * ATTENTION_EXTENT,
                pl.ds(start, tile),
            ]
            for head in range(HEADS_PER_PAIR)
        ],
        axis=1,
    )


def heads_below(beside, tile):
    return jnp.concatenate(
        [beside[:, head * tile : (head + 1) * tile] for head in range(HEADS_PER_PAIR)], axis=0
    )


def block_rows(spot, rows):
    return pl.ds(pl.multiple_of(spot * rows, rows), rows)


def whole_call(kernel, scalars, arrays, out_shape, scratch=(), flops=0, exps=0, name=None):
    size = sum(v.size * v.dtype.itemsize for v in (*arrays, *out_shape))
    return pl.pallas_call(
        kernel,
        grid_spec=pltpu.PrefetchScalarGridSpec(
            num_scalar_prefetch=len(scalars),
            grid=(1,),
            in_specs=[whole_block(v.shape) for v in arrays],
            out_specs=[whole_block(v.shape) for v in out_shape],
            scratch_shapes=list(scratch),
        ),
        out_shape=list(out_shape),
        compiler_params=call_params(),
        cost_estimate=NO_COST,
        name=name,
    )(*scalars, *arrays)


def struct(*shape, dtype=bf16):
    return jax.ShapeDtypeStruct(shape, dtype)


def project_attend_kernel(ways, sides, spots_ref, *refs):
    side_refs = refs[:sides]
    (
        w_ref, first_ref, second_ref, qkv_ref, inner_ref, att_ref, lse_ref, seg_col, seg_row, turned
    ) = refs[sides:]
    rows = side_refs[0].shape[1]
    width = first_ref.shape[1]
    slot = 0
    for side in side_refs:
        count = side.shape[0]
        x = side[...].reshape(count * rows, side.shape[2])
        inner = nt(x[:, :width], first_ref[...]).astype(bf16)
        qkv = nn(x[:, :width], w_ref[...]) + LOW_FACTORED * nn(inner, second_ref[...])
        qkv = qkv.astype(bf16)
        for index in range(count):
            own = slice(index * rows, (index + 1) * rows)
            here = block_rows(spots_ref[slot], rows)
            qkv_ref[here, :] = qkv[own]
            inner_ref[here, :] = inner[own]
            turned[:, here] = qkv[own].astype(f32).T.astype(bf16)
            segments = x[own, width:].astype(f32)
            seg_col[here, :] = segments[:, 0:1]
            seg_row[:, here] = segments.T[0:8, :]
            slot += 1
    part = spots_ref[slot]
    if ways > 1:
        att_ref[...] = jnp.zeros_like(att_ref)
        lse_ref[...] = jnp.zeros_like(lse_ref)
    per_tile = 2 if ways == 1 else 1
    tile = per_tile * rows
    for index in range(slot // ways // per_tile):
        kmax = (index + 1) * per_tile * ways * rows
        first_block = index * per_tile * ways + part if ways > 1 else index * per_tile
        start = pl.multiple_of(first_block * rows, rows) if ways > 1 else first_block * rows
        keys = qkv_ref[pl.ds(0, kmax), 0:LANES]
        values_t = turned[ATTENTION_EXTENT:LANES, pl.ds(0, kmax)]
        queries = heads_beside(turned, LANES, start, tile) * SCALE
        queries = jnp.concatenate([queries, jnp.zeros_like(queries)], axis=0)
        score = nn(keys, queries) + key_floor(seg_col, seg_row, tile, start, kmax)
        top = jnp.max(score, axis=0, keepdims=True)
        weight = jnp.exp(score - top)
        total = jnp.sum(weight, axis=0, keepdims=True)
        prob = (weight * (1.0 / total)).astype(bf16)
        packed = heads_below(nn(values_t, prob), tile).astype(bf16)
        for block in range(per_tile):
            att_ref[first_block + block] = packed[:, block * rows : (block + 1) * rows]
        lse_ref[:, pl.ds(start, tile)] = jnp.concatenate(
            [
                heads_below(top + jnp.log(total), tile),
                jnp.zeros((8 - HEADS_PER_PAIR, tile), f32),
            ],
            axis=0,
        )


def project_attend(spots, x_sides, weights, first, second, ways):
    blocks, rows = sum(v.shape[0] for v in x_sides), x_sides[0].shape[1]
    total = blocks * rows
    return whole_call(
        functools.partial(project_attend_kernel, ways, len(x_sides)),
        (spots,),
        (*x_sides, weights, first, second),
        (
            struct(total, HEAD_COLS), struct(total, first.shape[0]),
            struct(blocks, QUERY_COLS, rows), struct(8, total, dtype=f32),
            struct(total, 1, dtype=f32), struct(8, total, dtype=f32),
        ),
        scratch=(pltpu.VMEM((HEAD_COLS, total), bf16),),
        flops=2 * total * first.shape[1] * 512 + 8 * total * total * 256,
        exps=HEADS_PER_PAIR * total * total,
        name="project_attend",
    )


def rows_of(spots, grad_ref, inner_ref, w_ref, first_ref, rows_ref):
    grad = jnp.concatenate([grad_ref[spot, :] for spot in spots], axis=0)
    inner = jnp.concatenate([inner_ref[spot, :] for spot in spots], axis=0)
    out = nt(grad, w_ref[...]) + nn(inner, first_ref[...])
    rows_ref[...] = out.astype(bf16).reshape(rows_ref.shape)


def attend_back_kernel(ways, sides, spots_ref, *refs):
    qkv_ref, adj_ref, lse_ref, second_ref, inner_ref, seg_col, seg_row, w_ref, first_ref = refs[:9]
    side_refs = refs[9 : 9 + sides]
    (
        out_tables, rows_ref, grad_ref, inner_grad_ref, pieces_ref, own_ref, turned, adj_turned,
        grad_kv,
    ) = refs[9 + sides :]
    width = first_ref.shape[1]
    blocks, rows = adj_ref.shape[0], adj_ref.shape[2]
    half = ATTENTION_EXTENT
    wide, span = width // blocks, pieces_ref.shape[2]
    part = spots_ref[blocks]
    for index in range(blocks):
        here = pl.ds(index * rows, rows)
        turned[:, here] = qkv_ref[here, :].astype(f32).T.astype(bf16)
        adj_turned[:, here] = adj_ref[index]
    grad_kv[...] = jnp.zeros_like(grad_kv)
    if ways > 1:
        grad_ref[...] = jnp.zeros_like(grad_ref)
    per_tile = 2 if ways == 1 else 1
    tile = per_tile * rows
    for index in range(blocks // ways // per_tile):
        kmax = (index + 1) * per_tile * ways * rows
        start = index * tile
        if ways > 1:
            start = pl.multiple_of((index * per_tile * ways + part) * rows, rows)
        keys = qkv_ref[pl.ds(0, kmax), 0:LANES]
        keys_t = turned[0:half, pl.ds(0, kmax)]
        queries = heads_beside(turned, LANES, start, tile) * SCALE
        blank = jnp.zeros_like(queries)
        queries = jnp.concatenate([queries, blank], axis=0)
        adjoint = jnp.concatenate([blank, heads_beside(adj_turned, 0, start, tile)], axis=0)
        lse = jnp.concatenate(
            [lse_ref[h : h + 1, pl.ds(start, tile)] for h in range(HEADS_PER_PAIR)], axis=1
        )
        floor = key_floor(seg_col, seg_row, tile, start, kmax)
        prob = jnp.exp(nn(keys, queries) - lse + floor)
        both = prob * nn(keys, adjoint)
        delta = jnp.sum(both, axis=0, keepdims=True)
        grad_score = (both - prob * delta).astype(bf16)
        grad_kv[pl.ds(0, kmax), :] += nt(grad_score, queries) + nt(prob.astype(bf16), adjoint)
        packed = heads_below(nn(keys_t, grad_score), tile) * SCALE
        packed = jnp.concatenate([packed, jnp.zeros((half, tile), f32)], axis=0)
        grad_ref[pl.ds(start, tile), LANES:] = packed.T.astype(bf16)
    grad_ref[:, 0:LANES] = grad_kv[...].astype(bf16)

    inner_grad_ref[...] = (LOW_FACTORED * nt(grad_ref[...], second_ref[...])).astype(bf16)
    slot = 0
    grad_first = None
    for side in side_refs:
        count = side.shape[0]
        inner_grad = jnp.concatenate(
            [inner_grad_ref[block_rows(spots_ref[slot + i], rows), :] for i in range(count)],
            axis=0,
        )
        x = side[...].reshape(count * rows, side.shape[2])[:, :width]
        term = tn(inner_grad, x)
        grad_first = term if grad_first is None else grad_first + term
        slot += count
    third = wide // 3
    gap = jnp.zeros((RANK, QUERY_COLS - wide), f32)
    for place in range(blocks):
        second = out_tables[place, RANK:, :].astype(f32)
        for index in range(3):
            piece = grad_first[index * RANK : (index + 1) * RANK, place * wide : (place + 1) * wide]
            chunk = second[:, index * third : (index + 1) * third]
            parts = [piece, gap, chunk] if wide < QUERY_COLS else [piece, chunk]
            pieces_ref[place, index * RANK : (index + 1) * RANK, :] = padded(
                jnp.concatenate(parts, axis=1), span
            )
        pieces_ref[place, 3 * RANK :, :] = out_tables[place, 0:RANK, :]
    count = rows_ref.shape[0]
    last = [block_rows(spots_ref[blocks - count + i], rows) for i in range(count)]
    rows_of(last, grad_ref, inner_grad_ref, w_ref, first_ref, rows_ref)
    seconds = LOW_FACTORED * tn(inner_ref[...], grad_ref[...])
    own_ref[0 : 3 * RANK, :] = jnp.zeros((3 * RANK, span), bf16)
    value = seconds[2 * RANK : 3 * RANK, half : 2 * half]
    own_ref[3 * RANK : 4 * RANK, :] = padded(
        jnp.concatenate([jnp.zeros((RANK, QUERY_COLS), f32), value], axis=1), span
    )
    query, key = seconds[0:RANK, LANES : LANES + QUERY_COLS], seconds[RANK : 2 * RANK, 0:half]
    own_ref[4 * RANK :, :] = padded(jnp.concatenate([query, key], axis=1), span)


def padded(piece, span):
    rows, size = piece.shape
    if size < span:
        piece = jnp.concatenate([piece, jnp.zeros((rows, span - size), piece.dtype)], axis=1)
    return piece.astype(bf16)


def attend_back(
    spots, qkv, adj, lse, second, inner, seg_col, seg_row, weights, first, x_sides, out_tables,
    ways,
):
    blocks, rows = adj.shape[0], adj.shape[2]
    total, span = qkv.shape[0], out_tables.shape[2]
    return whole_call(
        functools.partial(attend_back_kernel, ways, len(x_sides)),
        (spots,),
        (qkv, adj, lse, second, inner, seg_col, seg_row, weights, first, *x_sides, out_tables),
        (
            struct(x_sides[-1].shape[0], rows, first.shape[1]), struct(total, HEAD_COLS), struct(total, 3 * RANK),
            struct(blocks, 4 * RANK, span), struct(PACKED * RANK, span),
        ),
        scratch=(
            pltpu.VMEM((HEAD_COLS, total), bf16),
            pltpu.VMEM((QUERY_COLS, total), bf16),
            pltpu.VMEM((total, LANES), f32),
        ),
        flops=20 * total * total * 256,
        exps=HEADS_PER_PAIR * total * total,
        name="attend_back",
    )


def rows_back_kernel(spots_ref, grad_ref, inner_ref, w_ref, first_ref, rows_ref):
    count, rows, _ = rows_ref.shape
    spots = [block_rows(spots_ref[i], rows) for i in range(count)]
    rows_of(spots, grad_ref, inner_ref, w_ref, first_ref, rows_ref)


def rows_back(spots, grad, inner, weights, first, side):
    count, rows, _ = side.shape
    width, cols = weights.shape
    return whole_call(
        rows_back_kernel,
        (spots,),
        (grad, inner, weights, first),
        [struct(count, rows, width)],
        flops=4 * count * rows * width * cols,
        name="rows_back",
    )[0]


OUT_STEPS = 4


def side_specs(sides):
    steps = OUT_STEPS // len(sides)
    specs = []
    for index, side in enumerate(sides):
        shape = (side.shape[0] // steps,) + side.shape[1:]
        specs.append(
            pl.BlockSpec(
                shape,
                lambda i, *_, base=index * steps, last=steps - 1: (
                    jnp.clip(i - base, 0, last), 0, 0
                ),
            )
        )
    return specs


def each_step(side_refs, spots_ref, visit):
    step = pl.program_id(0)
    steps = OUT_STEPS // len(side_refs)
    per_step, wide, width = side_refs[0].shape
    for index, side in enumerate(side_refs):

        @pl.when((step >= index * steps) & (step < (index + 1) * steps))
        def _():
            spots = [
                block_rows(spots_ref[step * per_step + block], wide) for block in range(per_step)
            ]
            visit(spots, side[...].reshape(per_step * wide, width))


def output_project_kernel(sides, spots_ref, *refs):
    side_refs = refs[:sides]
    (
        att_ref, first_ref, second_ref, rows_ref, gain_ref, mid_ref, normed_ref, inner_ref, total
    ) = refs[sides:]
    step = pl.program_id(0)

    @pl.when(step == 0)
    def _():
        total[...] = rows_ref[...].astype(f32)

    def visit(spots, weights):
        att = jnp.concatenate([att_ref[rows, :] for rows in spots], axis=0)
        total[...] += tn(att, weights)

    each_step(side_refs, spots_ref, visit)

    @pl.when(step == OUT_STEPS - 1)
    def _():
        inner = tn(att_ref[...], first_ref[...]).astype(bf16)
        mid = total[...] + LOW_FACTORED * nn(inner, second_ref[...])
        mid_ref[...] = mid
        inner_ref[...] = inner
        normed_ref[...] = normed(mid, gain_ref[...])[0].astype(bf16)


def output_project(spots, w_sides, att, first, second, rows, gain):
    count, width = rows.shape
    outs = (struct(count, width, dtype=f32), struct(count, width), struct(count, LANES))
    rest = (att, first, second, rows, gain)
    return pl.pallas_call(
        functools.partial(output_project_kernel, len(w_sides)),
        grid_spec=pltpu.PrefetchScalarGridSpec(
            num_scalar_prefetch=1,
            grid=(OUT_STEPS,),
            in_specs=side_specs(w_sides) + [whole_block(v.shape) for v in rest],
            out_specs=[whole_block(v.shape) for v in outs],
            scratch_shapes=[pltpu.VMEM((count, width), f32)],
        ),
        out_shape=outs,
        compiler_params=call_params(),
        cost_estimate=NO_COST,
        name="output_project",
    )(spots, *w_sides, *rest)


def output_back_kernel(sides, parts, spots_ref, *refs):
    side_refs, part_refs = refs[:sides], refs[sides : sides + parts]
    (
        att_ref, first_ref, mid_ref, gain_ref, out_grad_ref, second_ref, inner_ref,
        adj_ref, tables_ref, grad_mid_ref, branch, grad_inner,
    ) = refs[sides + parts :]
    step = pl.program_id(0)
    places, _, span = tables_ref.shape
    wide = mid_ref.shape[1] // places

    @pl.when(step == 0)
    def _():
        grad = sum([v[...].astype(f32) for v in part_refs[1:]], part_refs[0][...].astype(f32))
        mid = mid_ref[...]
        factor = lax.rsqrt(jnp.mean(mid * mid, axis=-1, keepdims=True) + EPS)
        grad_mid = out_grad_ref[...].astype(f32) + norm_back(mid, factor, gain_ref[...], grad)
        grad_mid_ref[...] = grad_mid
        low = grad_mid.astype(bf16)
        branch[...] = low
        grad_inner[...] = (LOW_FACTORED * nt(low, second_ref[...])).astype(bf16)

    def visit(spots, weights):
        first = jnp.concatenate([first_ref[rows, :] for rows in spots], axis=0)
        adj = (nt(weights, branch[...]) + nt(first, grad_inner[...])).astype(bf16)
        wide = adj.shape[0] // len(spots)
        for index, rows in enumerate(spots):
            adj_ref[rows, :] = adj[index * wide : (index + 1) * wide]

    each_step(side_refs, spots_ref, visit)

    @pl.when(step == OUT_STEPS - 1)
    def _():
        firsts = tn(grad_inner[...], att_ref[...].T)
        seconds = LOW_FACTORED * tn(inner_ref[...], branch[...])
        for place in range(places):
            own = slice(place * wide, (place + 1) * wide)
            tables_ref[place, 0:RANK, :] = padded(firsts[0:RANK, own], span)
            tables_ref[place, RANK:, :] = padded(seconds[0:RANK, own], span)


def output_back(
    spots, w_sides, att, first, parts, mid, gain, out_grad, second, inner, places, span
):
    count, width = mid.shape
    outs = (
        struct(*att.shape), struct(places, 2 * RANK, span), struct(count, width, dtype=f32)
    )
    rest = (*parts, att, first, mid, gain, out_grad, second, inner)
    return pl.pallas_call(
        functools.partial(output_back_kernel, len(w_sides), len(parts)),
        grid_spec=pltpu.PrefetchScalarGridSpec(
            num_scalar_prefetch=1,
            grid=(OUT_STEPS,),
            in_specs=side_specs(w_sides) + [whole_block(v.shape) for v in rest],
            out_specs=[whole_block(v.shape) for v in outs],
            scratch_shapes=[
                pltpu.VMEM((count, width), bf16), pltpu.VMEM((count, LANES), bf16)
            ],
        ),
        out_shape=outs,
        compiler_params=call_params(),
        cost_estimate=NO_COST,
        name="output_back",
    )(spots, *w_sides, *rest)


PACKED = 5


def attend_tables_kernel(ways, sides, place_ref, adapter_ref, *refs):
    side_refs, out_refs = refs[:sides], refs[sides:]
    per_side, sources = side_refs[0].shape[0], side_refs[0].shape[1] // (PACKED * RANK)
    blocks = per_side * sides
    wide = out_refs[0].shape[2] // blocks
    third = wide // 3
    half = ATTENTION_EXTENT

    def read(place, source, index):
        slot = place_ref[place]
        rows = pl.ds((source * PACKED + index) * RANK, RANK)
        value = side_refs[0][lax.rem(slot, per_side), rows, :]
        if sides > 1:
            value = jnp.where(slot < per_side, value, side_refs[1][lax.rem(slot, per_side), rows, :])
        return value.astype(f32)

    def by_head(pieces):
        return [
            sum(pieces[h * ways + 1 : (h + 1) * ways], pieces[h * ways])
            for h in range(PAIRED_ATTENDERS)
        ]

    for out_ref in out_refs:
        out_ref[...] = jnp.zeros_like(out_ref)
    for source in range(sources):
        adapter = adapter_ref[source]
        got = [[read(c, source, index) for c in range(blocks)] for index in range(PACKED)]
        pieces = [[v[:, :wide] for v in got[index]] for index in range(4)]
        pieces.append([
            got[index][c][:, QUERY_COLS : QUERY_COLS + third]
            for c in range(blocks) for index in range(3)
        ])
        pieces.append(by_head([v[:, :QUERY_COLS] for v in got[4]]))
        pieces.append(by_head([v[:, QUERY_COLS : QUERY_COLS + half] for v in got[4]]))
        pieces.append(by_head([v[:, QUERY_COLS : QUERY_COLS + half] for v in got[3]]))
        for parts, out_ref in zip(pieces, out_refs):
            out_ref[adapter] = out_ref[adapter] + jnp.concatenate(parts, axis=1)


def attend_tables(place, adapters, sides, width, ways):
    key_cols = PAIRED_ATTENDERS * ATTENTION_EXTENT
    cols = (width,) * 5 + (ASKING_ATTENDERS * ATTENTION_EXTENT, key_cols, key_cols)
    return whole_call(
        functools.partial(attend_tables_kernel, ways, len(sides)),
        (place, adapters),
        sides,
        [struct(NUM_CHOICES_X, RANK, size, dtype=f32) for size in cols],
        name="attend_tables",
    )


def expert_tables_kernel(sizes, sources, terms, adapter_ref, *refs):
    term_refs, out_refs = refs[:terms], refs[terms:]
    adapter = pl.program_id(0)
    for out_ref in out_refs:
        out_ref[...] = jnp.zeros_like(out_ref)
    for source in range(sources):

        @pl.when(adapter_ref[source] == adapter)
        def _():
            for expert in range(term_refs[0].shape[0]):
                own = None
                for term_ref in term_refs:
                    term = term_ref[expert, source * RANK : (source + 1) * RANK, :].astype(f32)
                    own = term if own is None else own + term
                start = 0
                for size, out_ref in zip(sizes, out_refs):
                    out_ref[0, expert] += own[:, start : start + size]
                    start += size


def expert_tables(adapters, terms, wide, slim):
    experts, sources = terms[0].shape[0], adapters.shape[0]
    sizes = (wide,) * 3 + (slim,) * 3
    return pl.pallas_call(
        functools.partial(expert_tables_kernel, sizes, sources, len(terms)),
        grid_spec=pltpu.PrefetchScalarGridSpec(
            num_scalar_prefetch=1,
            grid=(NUM_CHOICES_X,),
            in_specs=[whole_block(v.shape) for v in terms],
            out_specs=[
                pl.BlockSpec((1, experts, RANK, size), lambda a, adapters: (a, 0, 0, 0))
                for size in sizes
            ],
        ),
        out_shape=[
            jax.ShapeDtypeStruct((NUM_CHOICES_X, experts, RANK, size), f32) for size in sizes
        ],
        compiler_params=call_params(),
        cost_estimate=NO_COST,
        name="expert_tables",
    )(adapters, *terms)


def source_mask(shape, sources):
    row = lax.broadcasted_iota(jnp.int32, shape, 0)
    col = lax.broadcasted_iota(jnp.int32, shape, 1)
    keep = None
    for source in range(sources):
        inside = (row >= source * CAP) & (row < (source + 1) * CAP)
        inside &= (lax.rem(col, sources * RANK) >= source * RANK) & (
            lax.rem(col, sources * RANK) < (source + 1) * RANK
        )
        keep = inside if keep is None else keep | inside
    return keep


def masked(values, sources):
    return jnp.where(source_mask(values.shape, sources), values, 0.0)


def picks(slot_ref, pair, tokens, unit=0):
    slots = slot_ref[unit, :, pair * 2 * tokens : (pair + 1) * 2 * tokens]
    place = lax.broadcasted_iota(jnp.int32, (2 * CAP, 2 * tokens), 0)
    return place == slots


def picked_rows(slot_ref, rows_ref, sources, unit=0):
    tokens = rows_ref.shape[0] // sources
    parts = []
    for pair in range(sources // 2):
        pick = picks(slot_ref, pair, tokens, unit).astype(f32).astype(bf16)
        rows = rows_ref[pair * 2 * tokens : (pair + 1) * 2 * tokens, :]
        parts.append(nn(pick, rows))
    return jnp.concatenate(parts, axis=0)


def picked_gates(slot_ref, gate_ref, sources, unit=0):
    tokens = gate_ref.shape[2] // sources
    parts = []
    for pair in range(sources // 2):
        gate = gate_ref[unit, :, pair * 2 * tokens : (pair + 1) * 2 * tokens]
        kept = jnp.where(picks(slot_ref, pair, tokens, unit), gate, 0.0)
        parts.append(jnp.sum(kept, axis=1, keepdims=True))
    return jnp.concatenate(parts, axis=0)


def combine(target_ref, values, out_refs):
    sources = len(out_refs)
    tokens = target_ref.shape[0] // sources
    slots = values.shape[1]
    for source, out_ref in enumerate(out_refs):
        target = target_ref[source * tokens : (source + 1) * tokens, :]
        place = lax.broadcasted_iota(jnp.int32, (tokens, slots), 1)
        hit = place == target[:, 0:1]
        for choice in range(1, TOPK):
            hit |= place == target[:, choice : choice + 1]
        out_ref[...] = nn(hit.astype(f32).astype(bf16), values[source]).astype(bf16)


def keep_rows(values, rows, expert, sources):
    for source in range(sources):
        values[source, pl.ds(pl.multiple_of(expert * CAP, CAP), CAP), :] = rows[
            source * CAP : (source + 1) * CAP
        ]


def joined(refs, unit=0):
    return jnp.concatenate([ref[0, unit] for ref in refs], axis=0)


def experts_pre_kernel(sources, adapter_ref, slot_ref, gate_ref, grads_ref, down_ref, *refs):
    down_first, down_second = joined(refs[:sources]), joined(refs[sources : 2 * sources])
    picked_ref, hidden_ref, inner_ref = refs[2 * sources :]
    grads = picked_rows(slot_ref, grads_ref, sources)
    grads = (grads * picked_gates(slot_ref, gate_ref, sources)).astype(bf16)
    picked_ref[0] = grads
    inner = LOW_FACTORED * nt(grads, down_second)
    inner = masked(inner, sources).astype(bf16)
    inner_ref[0] = inner
    hidden_ref[0] = nt(grads, down_ref[0]) + nn(inner, down_first)


def experts_main_kernel(
    sources, adapter_ref, slot_ref, gate_w, up_w, grad_hidden, target_ref, *refs
):
    x_refs, refs = refs[:sources], refs[sources:]
    groups = [refs[i * sources : (i + 1) * sources] for i in range(4)]
    picked_ref, hidden_ref, adj_ref, inner_ref, *out_refs, values, x_ref = refs[4 * sources :]
    per_step, width, inner_size = gate_w.shape
    span = 2 * sources * RANK

    @pl.when(pl.program_id(0) == 0)
    def _():
        tokens = x_refs[0].shape[0]
        for source in range(sources):
            x_ref[source * tokens : (source + 1) * tokens, :] = x_refs[source][...]

    firsts, seconds = [], []
    for unit in range(per_step):
        firsts.append(
            jnp.concatenate([joined(groups[0], unit), joined(groups[1], unit)], axis=0)
        )
        gate_second, up_second = joined(groups[2], unit), joined(groups[3], unit)
        blank = jnp.zeros_like(gate_second)
        seconds.append(
            jnp.concatenate(
                [
                    jnp.concatenate([gate_second, blank], axis=1),
                    jnp.concatenate([blank, up_second], axis=1),
                ],
                axis=0,
            )
        )
        picked_ref[unit] = picked_rows(slot_ref, x_ref, sources, unit).astype(bf16)
        inner = masked(LOW_FACTORED * nt(picked_ref[unit], firsts[unit]), sources)
        inner_ref[unit, :, :span] = inner.astype(bf16)
    for unit in range(per_step):
        x = picked_ref[unit]
        inner = inner_ref[unit, :, :span]
        for start in range(0, inner_size, 2 * LANES):
            cols = slice(start, start + 2 * LANES)
            ups = slice(inner_size + start, inner_size + start + 2 * LANES)
            gate = nn(x, gate_w[unit, :, cols]) + nn(inner, seconds[unit][:, cols])
            up = nn(x, up_w[unit, :, cols]) + nn(inner, seconds[unit][:, ups])
            sigma = 1.0 / (1.0 + jnp.exp(-gate))
            active = gate * sigma
            hidden_ref[unit, :, cols] = (active * up).astype(bf16)
            adj = grad_hidden[unit, :, cols]
            grad_gate = adj * up * sigma * (1.0 + gate * (1.0 - sigma))
            adj_ref[unit, :, cols] = grad_gate.astype(bf16)
            adj_ref[unit, :, ups] = (adj * active).astype(bf16)
    for unit in range(per_step):
        grad_inner = masked(LOW_FACTORED * nt(adj_ref[unit], seconds[unit]), sources)
        inner_ref[unit, :, span:] = grad_inner.astype(bf16)
    for unit in range(per_step):
        rows = nt(adj_ref[unit, :, :inner_size], gate_w[unit])
        rows = rows + nt(adj_ref[unit, :, inner_size:], up_w[unit])
        rows = rows + nn(inner_ref[unit, :, span:], firsts[unit])
        expert = pl.program_id(0) * per_step + unit
        keep_rows(values, rows.astype(bf16), expert, sources)

    @pl.when(pl.program_id(0) == pl.num_programs(0) - 1)
    def _():
        combine(target_ref, values, out_refs)


def experts_post_kernel(
    sources, cohort, adapter_ref, slot_ref, gate_ref, down_ref, picked_ref, hidden_ref, adj_ref,
    inner_ref, picked_grads, grad_inner_down, target_ref, *refs
):
    groups = [refs[i * sources : (i + 1) * sources] for i in range(2)]
    table_ref, *out_refs, values = refs[2 * sources :]
    per_step = hidden_ref.shape[0]
    units = range(per_step)
    span = sources * RANK
    width, inner_size = picked_ref.shape[2], hidden_ref.shape[2]
    wide, slim = width // cohort, inner_size // cohort
    inner_down = [
        masked(nt(hidden_ref[u], joined(groups[0], u)), sources).astype(bf16) for u in units
    ]
    for unit in units:
        answer = nn(hidden_ref[unit], down_ref[unit])
        answer = answer + LOW_FACTORED * nn(inner_down[unit], joined(groups[1], unit))
        gates = picked_gates(slot_ref, gate_ref, sources, unit)
        answer = answer.astype(bf16).astype(f32) * gates
        expert = pl.program_id(0) * per_step + unit
        keep_rows(values, answer.astype(bf16), expert, sources)
    for unit in units:
        hidden = hidden_ref[unit]
        firsts = tn(inner_ref[unit, :, 2 * span :], picked_ref[unit])
        seconds = tn(inner_ref[unit, :, : 2 * span], adj_ref[unit])
        down_firsts = tn(grad_inner_down[unit], hidden)
        down_seconds = LOW_FACTORED * tn(inner_down[unit], picked_grads[unit])
        wide_parts = (firsts[:span], firsts[span:], down_seconds)
        slim_parts = (seconds[:span, :inner_size], seconds[span:, inner_size:], down_firsts)
        for place in range(cohort):
            pieces = [v[:, place * wide : (place + 1) * wide] for v in wide_parts]
            pieces += [v[:, place * slim : (place + 1) * slim] for v in slim_parts]
            table_ref[place, unit] = jnp.concatenate(pieces, axis=1).astype(bf16)

    @pl.when(pl.program_id(0) == pl.num_programs(0) - 1)
    def _():
        combine(target_ref, values, out_refs)


def per_expert(array, per_step=1):
    rest = array.shape[1:]
    return pl.BlockSpec((per_step,) + rest, lambda e, *_: (e,) + (0,) * len(rest))


def expert_rows(rows, width, per_step=1):
    return pl.BlockSpec((per_step, rows, width), lambda e, *_: (e, 0, 0))


def adapter_blocks(table, sources, per_step):
    shape = (1, per_step) + table.shape[2:]
    return [
        pl.BlockSpec(shape, lambda e, adapters, *_, s=s: (adapters[s], e, 0, 0))
        for s in range(sources)
    ]


def expert_call(
    kernel, sources, scalars, arrays, specs, tables, out_shape, out_specs, scratch, name,
    per_step=1,
):
    experts = tables[0].shape[1]
    return pl.pallas_call(
        kernel,
        grid_spec=pltpu.PrefetchScalarGridSpec(
            num_scalar_prefetch=len(scalars),
            grid=(experts // per_step,),
            in_specs=specs
            + [spec for t in tables for spec in adapter_blocks(t, sources, per_step)],
            out_specs=out_specs,
            scratch_shapes=scratch,
        ),
        out_shape=out_shape,
        compiler_params=call_params(),
        cost_estimate=NO_COST,
        name=name,
    )(*scalars, *arrays, *[t for t in tables for _ in range(sources)])


def experts_pre(adapters, slots, gates, grads, down, down_first, down_second):
    experts, inner_size, width = down.shape
    sources = adapters.shape[0]
    rows = sources * CAP
    return expert_call(
        functools.partial(experts_pre_kernel, sources),
        sources,
        (adapters,),
        (slots, gates, grads, down),
        [
            per_expert(slots), per_expert(gates), whole_block((grads.shape[0], width)),
            per_expert(down),
        ],
        (down_first, down_second),
        [
            struct(experts, rows, width), struct(experts, rows, inner_size, dtype=f32),
            struct(experts, rows, sources * RANK),
        ],
        [expert_rows(rows, v) for v in (width, inner_size, sources * RANK)],
        [],
        "experts_pre",
    )


def experts_main(
    adapters, slots, x_blocks, gate_w, up_w, grad_hidden, target, gate_first, up_first,
    gate_second, up_second,
):
    experts, width, inner_size = gate_w.shape
    sources = adapters.shape[0]
    rows = sources * CAP
    tokens = x_blocks[0].shape[0]
    per_step = 2 if experts % 2 == 0 else 1
    outs = (width, inner_size, 2 * inner_size, 4 * sources * RANK)
    return expert_call(
        functools.partial(experts_main_kernel, sources),
        sources,
        (adapters,),
        (slots, gate_w, up_w, grad_hidden, target, *x_blocks),
        [
            per_expert(slots, per_step), per_expert(gate_w, per_step), per_expert(up_w, per_step),
            per_expert(grad_hidden, per_step), whole_block(target.shape),
        ]
        + [whole_block(v.shape) for v in x_blocks],
        (gate_first, up_first, gate_second, up_second),
        [struct(experts, rows, v) for v in outs] + [struct(tokens, width)] * sources,
        [expert_rows(rows, v, per_step) for v in outs]
        + [whole_block((tokens, width))] * sources,
        [
            pltpu.VMEM((sources, experts * CAP, width), bf16),
            pltpu.VMEM((sources * tokens, width), bf16),
        ],
        "experts_main",
        per_step,
    )


def experts_post(
    adapters, slots, gates, down, picked, hidden, adj, inner, picked_grads, grad_inner_down,
    target, down_first, down_second, cohort,
):
    experts, inner_size, width = down.shape
    sources = adapters.shape[0]
    tokens = target.shape[0] // sources
    per_step = 2 if experts % 2 == 0 else 1
    lanes = 3 * (width + inner_size) // cohort
    arrays = (
        slots, gates, down, picked, hidden, adj, inner, picked_grads, grad_inner_down
    )
    return expert_call(
        functools.partial(experts_post_kernel, sources, cohort),
        sources,
        (adapters,),
        arrays + (target,),
        [per_expert(v, per_step) for v in arrays] + [whole_block(target.shape)],
        (down_first, down_second),
        [struct(cohort, experts, sources * RANK, lanes)] + [struct(tokens, width)] * sources,
        [
            pl.BlockSpec((cohort, per_step, sources * RANK, lanes), lambda e, *_: (0, e, 0, 0)),
        ]
        + [whole_block((tokens, width))] * sources,
        [pltpu.VMEM((sources, experts * CAP, width), bf16)],
        "experts_post",
        per_step,
    )


def flipped(array, axis, size, mask):
    return lax.ppermute(array, axis, [(i, i ^ mask) for i in range(size)])


def ring_blocks(array, axis, size):
    return [array] + [
        lax.ppermute(array, axis, [(i, (i + shift) % size) for i in range(size)])
        for shift in range(1, size)
    ]


def ring_return(blocks, axis, size):
    return [blocks[0]] + [
        lax.ppermute(blocks[shift], axis, [(i, (i - shift) % size) for i in range(size)])
        for shift in range(1, size)
    ]


def to_every(array, axis, size):
    return lax.all_to_all(
        jnp.broadcast_to(array[None], (size,) + array.shape), axis, 0, 0, tiled=True
    )


def cohort_spots(size):
    place = jnp.arange(size, dtype=jnp.int32)
    if size != 8:
        return place, place
    me = lax.axis_index("ctx")
    mask = place ^ me
    return (place % 4 * 2 + place // 4) ^ me, (mask & 1) * 4 + mask // 2


def gather_cohort(array, size, halves=False, stage=lambda blocks: blocks):
    if size != 8:
        return (lax.all_gather(array, "ctx", axis=0, tiled=False),)
    if halves:
        half = array.shape[0] // 2
        near, far = flipped(array, "ctx", size, 2), flipped(array, "ctx", size, 4)
        low, high = stage(
            [flipped(near[:half], "ctx", size, 4), flipped(far[half:], "ctx", size, 2)]
        )
        blocks = [near, far, jnp.concatenate([low, high], axis=0)]
    else:
        blocks = stage([flipped(array, "ctx", size, mask) for mask in (2, 4, 6)])
    mine = jnp.stack([array] + blocks)
    return mine, flipped(mine, "ctx", size, 1)


def staged_sums(pieces, row_sides, summed, terms, tables_of, size, sources):
    tie = lax.optimization_barrier

    def plus(left, right):
        return (left.astype(f32) + right.astype(f32)).astype(bf16)

    other, row_side, pieces = tie((flipped(row_sides[1], "ctx", size, 1), row_sides[0], pieces))
    mine = plus(row_side, other)
    half = mine.shape[1] // 2
    low, high = mine[:, :half], mine[:, half:]
    near, far, slip = tie(
        (jnp.stack([low[1], low[3]]), jnp.stack([high[2], high[3]]), summed(pieces))
    )
    beside = tables_of(terms)
    near, far, groups = tie(
        (
            flipped(near, "ctx", size, 2), flipped(far, "ctx", size, 4),
            to_every(slip, "exp", sources),
        )
    )
    low_last, high_last, groups = tie(
        (plus(low[2], near[1]), plus(high[1], far[1]), groups.reshape(-1, slip.shape[1]))
    )
    low_last, high_last, blocks, beside = tie(
        (
            flipped(low_last, "ctx", size, 4), flipped(high_last, "ctx", size, 2),
            [flipped(groups, "ctx", size, mask) for mask in (2, 4, 6)], beside,
        )
    )
    mine = jnp.stack([groups] + blocks)
    low_sum = low[0].astype(f32) + near[0].astype(f32) + low_last.astype(f32)
    high_sum = high[0].astype(f32) + far[0].astype(f32) + high_last.astype(f32)
    rows = jnp.concatenate([low_sum, high_sum], axis=0)
    return (mine, flipped(mine, "ctx", size, 1)), rows, beside


def head_columns(query, key, value):
    rows = query.shape[0]

    def split(array):
        return jnp.transpose(array.reshape(rows, PAIRED_ATTENDERS, -1), (1, 0, 2))

    parts = [split(key), split(value), split(query)]
    pad = HEAD_COLS - sum(p.shape[2] for p in parts)
    parts.append(jnp.zeros((PAIRED_ATTENDERS, rows, pad), query.dtype))
    return jnp.concatenate(parts, axis=2)


def body(
    tokens, out_grad, attn_gain, moe_gain, w_query, lock_projection, content_projection, w_out,
    sigmoid_matrices, widener_matrices, reducer_matrices, segment_ids, expert_routes,
    route_weights, adapter_index, query_first, query_second, key_first, lock_final_matrices,
    value_first, content_final_matrices, output_first, output_second, gate_first, gate_second,
    upward_first, upward_second, down_first, down_second,
):
    rows_in = tokens[0].astype(f32)
    count, width = rows_in.shape
    cohort = lax.axis_size("ctx")
    sources = lax.axis_size("exp")
    experts = sigmoid_matrices.shape[0]
    ctx = lax.axis_index("ctx")
    exp = lax.axis_index("exp")
    ways = cohort // PAIRED_ATTENDERS
    head = ctx // ways
    adapter = adapter_index[exp]

    def elected(table):
        return lax.dynamic_index_in_dim(table, adapter, 0, keepdims=False)

    attended_cols = ASKING_ATTENDERS * ATTENTION_EXTENT
    wide = width // cohort
    span = -(-max(wide, QUERY_COLS) // LANES) * LANES
    spots, place = cohort_spots(cohort)
    order = jnp.concatenate([spots, (ctx % ways)[None].astype(jnp.int32)])

    normed_in, factor_in = normed(rows_in, attn_gain)
    labels = jnp.pad(segment_ids[0].astype(bf16)[:, None], ((0, 0), (0, LANES - 1)))
    x_sides = gather_cohort(
        jnp.concatenate([normed_in.astype(bf16), labels], axis=1), cohort, True
    )
    relative = (exp - jnp.arange(sources, dtype=jnp.int32) + sources) % sources
    out_rows = jnp.stack(ring_blocks(w_out, "exp", sources))[relative].reshape(-1, width)
    head_w = head_columns(w_query, lock_projection, content_projection)
    to_all = jnp.broadcast_to(
        head_w[:, None], (PAIRED_ATTENDERS, ways * sources) + head_w.shape[1:]
    ).reshape((cohort * sources,) + head_w.shape[1:])
    own_w = lax.all_to_all(to_all, ("ctx", "exp"), 0, 0, tiled=True).reshape(width, HEAD_COLS)

    routes = expert_routes[0].astype(bf16)
    weight_high = route_weights[0].astype(bf16)
    weight_low = (route_weights[0] - weight_high.astype(f32)).astype(bf16)
    parcel = jnp.concatenate(
        [
            out_grad[0], routes, weight_high, weight_low,
            jnp.zeros((count, LANES - 3 * TOPK), bf16),
        ],
        axis=1,
    )
    parcel, own_w = lax.optimization_barrier((parcel, own_w))
    parcels = ring_blocks(parcel, "exp", sources)

    own_firsts = jnp.concatenate(
        [elected(query_first), elected(key_first), elected(value_first)], axis=0
    )

    def head_part(table):
        part = elected(table)
        size = part.shape[1] // PAIRED_ATTENDERS
        return lax.dynamic_slice_in_dim(part, head * size, size, 1)

    def placed(part, row, col):
        return jnp.pad(
            part, ((row, 2 * RANK - row), (col, HEAD_COLS - col - part.shape[1]))
        )

    own_seconds = (
        placed(head_part(query_second), 0, LANES)
        + placed(head_part(lock_final_matrices), RANK, 0)
        + placed(head_part(content_final_matrices), 2 * RANK, ATTENTION_EXTENT)
    )
    qkv, inner, attended, lse, seg_col, seg_row = project_attend(
        order, x_sides, own_w, own_firsts, own_seconds, ways
    )
    shared = [lax.all_to_all(attended, "ctx", 0, 0, tiled=True)]

    def beside_attention(blocks):
        blocks, shared[0], parcels[:] = lax.optimization_barrier((blocks, shared[0], parcels))
        return blocks

    out_sides = gather_cohort(out_rows, cohort, True, beside_attention)
    attended = shared[0]
    if ways > 1:
        attended = attended.reshape(PAIRED_ATTENDERS, ways, QUERY_COLS, count)
        attended = attended.astype(f32).sum(1).astype(bf16)
    attended = attended.reshape(attended_cols, count)
    out_first = jnp.pad(elected(output_first), ((0, LANES - RANK), (0, 0)))
    out_first = out_first.T
    out_second = jnp.pad(elected(output_second), ((0, LANES - RANK), (0, 0)))
    mid, normed_mid, inner_out = output_project(
        spots, out_sides, attended, out_first, out_second, tokens[0], moe_gain[None]
    )
    x_exp = ring_blocks(normed_mid, "exp", sources)

    parcels, normed_mid = lax.optimization_barrier((parcels, normed_mid))
    parcels = jnp.concatenate(parcels, axis=0)
    extra = parcels[:, width:].astype(f32).reshape(sources, count, -1)
    all_routes = extra[:, :, :TOPK].astype(jnp.int32) - exp * experts
    all_gates = extra[:, :, TOPK : 2 * TOPK] + extra[:, :, 2 * TOPK : 3 * TOPK]
    hits = all_routes[None] == jnp.arange(experts, dtype=jnp.int32)[:, None, None, None]
    named = jnp.any(hits, axis=3)
    gates = jnp.sum(jnp.where(hits, all_gates[None], 0.0), axis=3).reshape(experts, 1, -1)
    earlier = jnp.tril(jnp.ones((count, count), bf16), -1)
    rank = lax.dot_general(
        named.astype(bf16), earlier, (((2,), (1,)), ((), ())), preferred_element_type=f32
    ).astype(jnp.int32)
    side = (jnp.arange(sources, dtype=jnp.int32) % 2 * CAP)[None, :, None]
    slots = jnp.where(named, rank + side, -1).reshape(experts, 1, -1)
    places = jnp.arange(experts, dtype=jnp.int32)[:, None, None] * CAP + rank + 1
    target = jnp.sum(jnp.where(hits, places[..., None], 0), axis=0) - 1
    target = target.reshape(sources * count, TOPK)

    adapters = adapter_index[relative]
    picked_grads, grad_hidden, grad_inner_down = experts_pre(
        adapters, slots, gates, parcels, reducer_matrices, down_first, down_second
    )
    picked, hidden, adj, inner_rows, *grad_parts = experts_main(
        adapters, slots, x_exp, sigmoid_matrices, widener_matrices, grad_hidden, target,
        gate_first, upward_first, gate_second, upward_second,
    )
    grad_parts = ring_return(grad_parts, "exp", sources)
    tables, *answers = experts_post(
        adapters, slots, gates, reducer_matrices, picked, hidden, adj, inner_rows,
        picked_grads, grad_inner_down, target, down_first, down_second, cohort,
    )
    tables, answers, grad_parts = lax.optimization_barrier((tables, answers, grad_parts))
    answers = ring_return(answers, "exp", sources)
    early, middle = answers[:2] + answers[3:], answers[2:3]
    terms = [lax.psum_scatter(tables, "ctx", scatter_dimension=0, tiled=False)]

    adj_blocks, out_tables, grad_mid = output_back(
        spots, out_sides, attended, out_first, grad_parts, mid, moe_gain[None], out_grad[0], out_second,
        inner_out, cohort, span,
    )
    adj_blocks = jnp.repeat(adj_blocks.reshape(-1, QUERY_COLS, count), ways, axis=0)
    adj_all = lax.all_to_all(adj_blocks, "ctx", 0, 0, tiled=True)
    adj_all, early = lax.optimization_barrier((adj_all, early))
    last_rows, grad_heads, grad_inner, pieces, own_seconds_grad = attend_back(
        order, qkv, adj_all, lse, own_seconds, inner, seg_col, seg_row, own_w, own_firsts,
        x_sides, out_tables, ways,
    )

    def tables_of(terms):
        return expert_tables(adapters, terms, wide, sigmoid_matrices.shape[2] // cohort)

    last_rows, grad_heads, pieces, middle = lax.optimization_barrier(
        (last_rows, grad_heads, pieces, middle)
    )

    pieces = lax.all_to_all(pieces, "ctx", 0, 0, tiled=True)
    row_sides = [
        rows_back(order, grad_heads, grad_inner, own_w, own_firsts, side) for side in x_sides[:-1]
    ] + [last_rows]

    def summed(pieces):
        total = jnp.pad(pieces.astype(f32).sum(0), ((0, RANK), (0, 0)))
        return (total + own_seconds_grad.astype(f32)).astype(bf16)

    if cohort != 8:
        groups = to_every(summed(pieces), "exp", sources)
        group_sides = gather_cohort(groups.reshape(-1, span), cohort)
        grad_normed_in = lax.psum_scatter(row_sides[0], "ctx", scatter_dimension=0).astype(f32)
        expert_grads = tables_of(terms)
    else:
        group_sides, grad_normed_in, expert_grads = staged_sums(
            pieces, row_sides, summed, terms, tables_of, cohort, sources
        )
    block_out = (mid + sum(v.astype(f32) for v in early + middle)).astype(bf16)[None]
    attention_tables = attend_tables(place, adapter_index, group_sides, width, ways)
    tokens_grad = (
        grad_mid + norm_back(rows_in, factor_in, attn_gain, grad_normed_in)
    ).astype(bf16)[None]
    gate_f, up_f, down_s, gate_s, up_s, down_f = expert_grads
    attention_tables = attend_tables(place, adapter_index, group_sides, width, ways)
    query_f, key_f, value_f, out_f, out_s, query_s, key_s, value_s = attention_tables
    return (
        block_out, tokens_grad, query_f, query_s, key_f, key_s, value_f, value_s, out_f, out_s,
        gate_f, gate_s, up_f, up_s, down_f, down_s,
    )


def solution(mesh):
    sharded = P("exp", "ctx", None)
    rows = P(("ctx", "exp"), None)
    table = P(None, "exp", None, None)
    expert = P("exp", None, None)
    in_specs = (
        (sharded, sharded, P(), P())
        + (rows,) * 4
        + (expert,) * 3
        + (P("exp", "ctx"), sharded, sharded, P())
        + (P(),) * 8
        + (table,) * 6
    )
    out_specs = (sharded, sharded) + (P(),) * 8 + (P(None, "exp", None, "ctx"),) * 6
    return jax.shard_map(body, mesh=mesh, in_specs=in_specs, out_specs=out_specs, check_vma=False)
```

```python
import functools

import jax
import jax.numpy as jnp
from jax import lax
from jax.experimental import pallas as pl
from jax.experimental.pallas import tpu as pltpu
from jax.sharding import PartitionSpec as P

ASKING_ATTENDERS = 24
PAIRED_ATTENDERS = 8
ATTENTION_EXTENT = 64
HEADS_PER_PAIR = ASKING_ATTENDERS // PAIRED_ATTENDERS
QUERY_COLS = HEADS_PER_PAIR * ATTENTION_EXTENT
EXPERTS = 40
TOPK = 8
NUM_CHOICES_X = 8
CAP = 48
RANK = 16
LANES = 128

EPS = 1e-06
LOW_FACTORED = 2.0
MASKED_FLOOR = -1e30
SCALE = 0.125
VMEM_LIMIT = 56 * 1024 * 1024

bf16 = jnp.bfloat16
f32 = jnp.float32

NO_COST = pl.CostEstimate(flops=0, bytes_accessed=0, transcendentals=0)

HEAD_COLS = 384


def nn(left, right):
    return jnp.dot(left, right, preferred_element_type=f32)


def nt(left, right):
    return lax.dot_general(left, right, (((1,), (1,)), ((), ())), preferred_element_type=f32)


def tn(left, right):
    return lax.dot_general(left, right, (((0,), (0,)), ((), ())), preferred_element_type=f32)


def normed(rows, gain):
    factor = lax.rsqrt(jnp.mean(rows * rows, axis=-1, keepdims=True) + EPS)
    return rows * factor * gain, factor


def norm_back(rows, factor, gain, adjoint):
    weighted = adjoint * gain
    central = jnp.mean(weighted * rows, axis=-1, keepdims=True)
    return factor * (weighted - rows * factor * factor * central)


def whole_block(shape):
    return pl.BlockSpec(shape, lambda *ids: (0,) * len(shape))


def call_params(axes=1):
    return pltpu.CompilerParams(
        dimension_semantics=("arbitrary",) * axes, vmem_limit_bytes=VMEM_LIMIT
    )


def key_floor(seg_col, seg_row, tile, start, kmax):
    key_place = lax.broadcasted_iota(jnp.int32, (kmax, tile), 0)
    query_place = start + lax.broadcasted_iota(jnp.int32, (kmax, tile), 1)
    key_seg = seg_col[pl.ds(0, kmax), :]
    query_seg = seg_row[0:1, pl.ds(start, tile)]
    same = (key_seg == query_seg) | (key_seg == 0.0)
    floor = jnp.where((key_place <= query_place) & same, 0.0, MASKED_FLOOR)
    return jnp.concatenate([floor] * HEADS_PER_PAIR, axis=1)


def heads_beside(turned, first_row, start, tile):
    return jnp.concatenate(
        [
            turned[
                first_row + head * ATTENTION_EXTENT : first_row + (head + 1) * ATTENTION_EXTENT,
                pl.ds(start, tile),
            ]
            for head in range(HEADS_PER_PAIR)
        ],
        axis=1,
    )


def heads_below(beside, tile):
    return jnp.concatenate(
        [beside[:, head * tile : (head + 1) * tile] for head in range(HEADS_PER_PAIR)], axis=0
    )


def block_rows(spot, rows):
    return pl.ds(pl.multiple_of(spot * rows, rows), rows)


def whole_call(kernel, scalars, arrays, out_shape, scratch=(), flops=0, exps=0, name=None):
    size = sum(v.size * v.dtype.itemsize for v in (*arrays, *out_shape))
    return pl.pallas_call(
        kernel,
        grid_spec=pltpu.PrefetchScalarGridSpec(
            num_scalar_prefetch=len(scalars),
            grid=(1,),
            in_specs=[whole_block(v.shape) for v in arrays],
            out_specs=[whole_block(v.shape) for v in out_shape],
            scratch_shapes=list(scratch),
        ),
        out_shape=list(out_shape),
        compiler_params=call_params(),
        cost_estimate=NO_COST,
        name=name,
    )(*scalars, *arrays)


def struct(*shape, dtype=bf16):
    return jax.ShapeDtypeStruct(shape, dtype)


def project_attend_kernel(ways, sides, spots_ref, *refs):
    side_refs = refs[:sides]
    (
        w_ref, first_ref, second_ref, qkv_ref, inner_ref, att_ref, lse_ref, seg_col, seg_row, turned
    ) = refs[sides:]
    rows = side_refs[0].shape[1]
    width = first_ref.shape[1]
    slot = 0
    for side in side_refs:
        count = side.shape[0]
        x = side[...].reshape(count * rows, side.shape[2])
        inner = nt(x[:, :width], first_ref[...]).astype(bf16)
        qkv = nn(x[:, :width], w_ref[...]) + LOW_FACTORED * nn(inner, second_ref[...])
        qkv = qkv.astype(bf16)
        for index in range(count):
            own = slice(index * rows, (index + 1) * rows)
            here = block_rows(spots_ref[slot], rows)
            qkv_ref[here, :] = qkv[own]
            inner_ref[here, :] = inner[own]
            turned[:, here] = qkv[own].astype(f32).T.astype(bf16)
            segments = x[own, width:].astype(f32)
            seg_col[here, :] = segments[:, 0:1]
            seg_row[:, here] = segments.T[0:8, :]
            slot += 1
    part = spots_ref[slot]
    if ways > 1:
        att_ref[...] = jnp.zeros_like(att_ref)
        lse_ref[...] = jnp.zeros_like(lse_ref)
    per_tile = 2 if ways == 1 else 1
    tile = per_tile * rows
    for index in range(slot // ways // per_tile):
        kmax = (index + 1) * per_tile * ways * rows
        first_block = index * per_tile * ways + part if ways > 1 else index * per_tile
        start = pl.multiple_of(first_block * rows, rows) if ways > 1 else first_block * rows
        keys = qkv_ref[pl.ds(0, kmax), 0:LANES]
        values_t = turned[ATTENTION_EXTENT:LANES, pl.ds(0, kmax)]
        queries = heads_beside(turned, LANES, start, tile) * SCALE
        queries = jnp.concatenate([queries, jnp.zeros_like(queries)], axis=0)
        score = nn(keys, queries) + key_floor(seg_col, seg_row, tile, start, kmax)
        top = jnp.max(score, axis=0, keepdims=True)
        weight = jnp.exp(score - top)
        total = jnp.sum(weight, axis=0, keepdims=True)
        prob = (weight * (1.0 / total)).astype(bf16)
        packed = heads_below(nn(values_t, prob), tile).astype(bf16)
        for block in range(per_tile):
            att_ref[first_block + block] = packed[:, block * rows : (block + 1) * rows]
        lse_ref[:, pl.ds(start, tile)] = jnp.concatenate(
            [
                heads_below(top + jnp.log(total), tile),
                jnp.zeros((8 - HEADS_PER_PAIR, tile), f32),
            ],
            axis=0,
        )


def project_attend(spots, x_sides, weights, first, second, ways):
    blocks, rows = sum(v.shape[0] for v in x_sides), x_sides[0].shape[1]
    total = blocks * rows
    return whole_call(
        functools.partial(project_attend_kernel, ways, len(x_sides)),
        (spots,),
        (*x_sides, weights, first, second),
        (
            struct(total, HEAD_COLS), struct(total, first.shape[0]),
            struct(blocks, QUERY_COLS, rows), struct(8, total, dtype=f32),
            struct(total, 1, dtype=f32), struct(8, total, dtype=f32),
        ),
        scratch=(pltpu.VMEM((HEAD_COLS, total), bf16),),
        flops=2 * total * first.shape[1] * 512 + 8 * total * total * 256,
        exps=HEADS_PER_PAIR * total * total,
        name="project_attend",
    )


def rows_of(spots, grad_ref, inner_ref, w_ref, first_ref, rows_ref):
    grad = jnp.concatenate([grad_ref[spot, :] for spot in spots], axis=0)
    inner = jnp.concatenate([inner_ref[spot, :] for spot in spots], axis=0)
    out = nt(grad, w_ref[...]) + nn(inner, first_ref[...])
    rows_ref[...] = out.astype(bf16).reshape(rows_ref.shape)


def attend_back_kernel(ways, sides, spots_ref, *refs):
    qkv_ref, adj_ref, lse_ref, second_ref, inner_ref, seg_col, seg_row, w_ref, first_ref = refs[:9]
    side_refs = refs[9 : 9 + sides]
    (
        out_tables, rows_ref, grad_ref, inner_grad_ref, pieces_ref, own_ref, turned, adj_turned,
        grad_kv,
    ) = refs[9 + sides :]
    width = first_ref.shape[1]
    blocks, rows = adj_ref.shape[0], adj_ref.shape[2]
    half = ATTENTION_EXTENT
    wide, span = width // blocks, pieces_ref.shape[2]
    part = spots_ref[blocks]
    for index in range(blocks):
        here = pl.ds(index * rows, rows)
        turned[:, here] = qkv_ref[here, :].astype(f32).T.astype(bf16)
        adj_turned[:, here] = adj_ref[index]
    grad_kv[...] = jnp.zeros_like(grad_kv)
    if ways > 1:
        grad_ref[...] = jnp.zeros_like(grad_ref)
    per_tile = 2 if ways == 1 else 1
    tile = per_tile * rows
    for index in range(blocks // ways // per_tile):
        kmax = (index + 1) * per_tile * ways * rows
        start = index * tile
        if ways > 1:
            start = pl.multiple_of((index * per_tile * ways + part) * rows, rows)
        keys = qkv_ref[pl.ds(0, kmax), 0:LANES]
        keys_t = turned[0:half, pl.ds(0, kmax)]
        queries = heads_beside(turned, LANES, start, tile) * SCALE
        blank = jnp.zeros_like(queries)
        queries = jnp.concatenate([queries, blank], axis=0)
        adjoint = jnp.concatenate([blank, heads_beside(adj_turned, 0, start, tile)], axis=0)
        lse = jnp.concatenate(
            [lse_ref[h : h + 1, pl.ds(start, tile)] for h in range(HEADS_PER_PAIR)], axis=1
        )
        floor = key_floor(seg_col, seg_row, tile, start, kmax)
        prob = jnp.exp(nn(keys, queries) - lse + floor)
        both = prob * nn(keys, adjoint)
        delta = jnp.sum(both, axis=0, keepdims=True)
        grad_score = (both - prob * delta).astype(bf16)
        grad_kv[pl.ds(0, kmax), :] += nt(grad_score, queries) + nt(prob.astype(bf16), adjoint)
        packed = heads_below(nn(keys_t, grad_score), tile) * SCALE
        packed = jnp.concatenate([packed, jnp.zeros((half, tile), f32)], axis=0)
        grad_ref[pl.ds(start, tile), LANES:] = packed.T.astype(bf16)
    grad_ref[:, 0:LANES] = grad_kv[...].astype(bf16)

    inner_grad_ref[...] = (LOW_FACTORED * nt(grad_ref[...], second_ref[...])).astype(bf16)
    slot = 0
    grad_first = None
    for side in side_refs:
        count = side.shape[0]
        inner_grad = jnp.concatenate(
            [inner_grad_ref[block_rows(spots_ref[slot + i], rows), :] for i in range(count)],
            axis=0,
        )
        x = side[...].reshape(count * rows, side.shape[2])[:, :width]
        term = tn(inner_grad, x)
        grad_first = term if grad_first is None else grad_first + term
        slot += count
    third = wide // 3
    gap = jnp.zeros((RANK, QUERY_COLS - wide), f32)
    for place in range(blocks):
        second = out_tables[place, RANK:, :].astype(f32)
        for index in range(3):
            piece = grad_first[index * RANK : (index + 1) * RANK, place * wide : (place + 1) * wide]
            chunk = second[:, index * third : (index + 1) * third]
            parts = [piece, gap, chunk] if wide < QUERY_COLS else [piece, chunk]
            pieces_ref[place, index * RANK : (index + 1) * RANK, :] = padded(
                jnp.concatenate(parts, axis=1), span
            )
        pieces_ref[place, 3 * RANK :, :] = out_tables[place, 0:RANK, :]
    count = rows_ref.shape[0]
    last = [block_rows(spots_ref[blocks - count + i], rows) for i in range(count)]
    rows_of(last, grad_ref, inner_grad_ref, w_ref, first_ref, rows_ref)
    seconds = LOW_FACTORED * tn(inner_ref[...], grad_ref[...])
    own_ref[0 : 3 * RANK, :] = jnp.zeros((3 * RANK, span), bf16)
    value = seconds[2 * RANK : 3 * RANK, half : 2 * half]
    own_ref[3 * RANK : 4 * RANK, :] = padded(
        jnp.concatenate([jnp.zeros((RANK, QUERY_COLS), f32), value], axis=1), span
    )
    query, key = seconds[0:RANK, LANES : LANES + QUERY_COLS], seconds[RANK : 2 * RANK, 0:half]
    own_ref[4 * RANK :, :] = padded(jnp.concatenate([query, key], axis=1), span)


def padded(piece, span):
    rows, size = piece.shape
    if size < span:
        piece = jnp.concatenate([piece, jnp.zeros((rows, span - size), piece.dtype)], axis=1)
    return piece.astype(bf16)


def attend_back(
    spots, qkv, adj, lse, second, inner, seg_col, seg_row, weights, first, x_sides, out_tables,
    ways,
):
    blocks, rows = adj.shape[0], adj.shape[2]
    total, span = qkv.shape[0], out_tables.shape[2]
    return whole_call(
        functools.partial(attend_back_kernel, ways, len(x_sides)),
        (spots,),
        (qkv, adj, lse, second, inner, seg_col, seg_row, weights, first, *x_sides, out_tables),
        (
            struct(x_sides[-1].shape[0], rows, first.shape[1]), struct(total, HEAD_COLS), struct(total, 3 * RANK),
            struct(blocks, 4 * RANK, span), struct(PACKED * RANK, span),
        ),
        scratch=(
            pltpu.VMEM((HEAD_COLS, total), bf16),
            pltpu.VMEM((QUERY_COLS, total), bf16),
            pltpu.VMEM((total, LANES), f32),
        ),
        flops=20 * total * total * 256,
        exps=HEADS_PER_PAIR * total * total,
        name="attend_back",
    )


def rows_back_kernel(spots_ref, grad_ref, inner_ref, w_ref, first_ref, rows_ref):
    count, rows, _ = rows_ref.shape
    spots = [block_rows(spots_ref[i], rows) for i in range(count)]
    rows_of(spots, grad_ref, inner_ref, w_ref, first_ref, rows_ref)


def rows_back(spots, grad, inner, weights, first, side):
    count, rows, _ = side.shape
    width, cols = weights.shape
    return whole_call(
        rows_back_kernel,
        (spots,),
        (grad, inner, weights, first),
        [struct(count, rows, width)],
        flops=4 * count * rows * width * cols,
        name="rows_back",
    )[0]


OUT_STEPS = 2


def side_specs(sides):
    steps = OUT_STEPS // len(sides)
    specs = []
    for index, side in enumerate(sides):
        shape = (side.shape[0] // steps,) + side.shape[1:]
        specs.append(
            pl.BlockSpec(
                shape,
                lambda i, *_, base=index * steps, last=steps - 1: (
                    jnp.clip(i - base, 0, last), 0, 0
                ),
            )
        )
    return specs


def each_step(side_refs, spots_ref, visit):
    step = pl.program_id(0)
    steps = OUT_STEPS // len(side_refs)
    per_step, wide, width = side_refs[0].shape
    for index, side in enumerate(side_refs):

        @pl.when((step >= index * steps) & (step < (index + 1) * steps))
        def _():
            spots = [
                block_rows(spots_ref[step * per_step + block], wide) for block in range(per_step)
            ]
            visit(spots, side[...].reshape(per_step * wide, width))


def output_project_kernel(sides, spots_ref, *refs):
    side_refs = refs[:sides]
    (
        att_ref, first_ref, second_ref, rows_ref, gain_ref, mid_ref, normed_ref, inner_ref, total
    ) = refs[sides:]
    step = pl.program_id(0)

    @pl.when(step == 0)
    def _():
        total[...] = rows_ref[...].astype(f32)

    def visit(spots, weights):
        att = jnp.concatenate([att_ref[rows, :] for rows in spots], axis=0)
        total[...] += tn(att, weights)

    each_step(side_refs, spots_ref, visit)

    @pl.when(step == OUT_STEPS - 1)
    def _():
        inner = tn(att_ref[...], first_ref[...]).astype(bf16)
        mid = total[...] + LOW_FACTORED * nn(inner, second_ref[...])
        mid_ref[...] = mid
        inner_ref[...] = inner
        normed_ref[...] = normed(mid, gain_ref[...])[0].astype(bf16)


def output_project(spots, w_sides, att, first, second, rows, gain):
    count, width = rows.shape
    outs = (struct(count, width, dtype=f32), struct(count, width), struct(count, LANES))
    rest = (att, first, second, rows, gain)
    return pl.pallas_call(
        functools.partial(output_project_kernel, len(w_sides)),
        grid_spec=pltpu.PrefetchScalarGridSpec(
            num_scalar_prefetch=1,
            grid=(OUT_STEPS,),
            in_specs=side_specs(w_sides) + [whole_block(v.shape) for v in rest],
            out_specs=[whole_block(v.shape) for v in outs],
            scratch_shapes=[pltpu.VMEM((count, width), f32)],
        ),
        out_shape=outs,
        compiler_params=call_params(),
        cost_estimate=NO_COST,
        name="output_project",
    )(spots, *w_sides, *rest)


def output_back_kernel(sides, parts, spots_ref, *refs):
    side_refs, part_refs = refs[:sides], refs[sides : sides + parts]
    (
        att_ref, first_ref, mid_ref, gain_ref, out_grad_ref, second_ref, inner_ref,
        adj_ref, tables_ref, grad_mid_ref, branch, grad_inner,
    ) = refs[sides + parts :]
    step = pl.program_id(0)
    places, _, span = tables_ref.shape
    wide = mid_ref.shape[1] // places

    @pl.when(step == 0)
    def _():
        grad = sum([v[...].astype(f32) for v in part_refs[1:]], part_refs[0][...].astype(f32))
        mid = mid_ref[...]
        factor = lax.rsqrt(jnp.mean(mid * mid, axis=-1, keepdims=True) + EPS)
        grad_mid = out_grad_ref[...].astype(f32) + norm_back(mid, factor, gain_ref[...], grad)
        grad_mid_ref[...] = grad_mid
        low = grad_mid.astype(bf16)
        branch[...] = low
        grad_inner[...] = (LOW_FACTORED * nt(low, second_ref[...])).astype(bf16)

    def visit(spots, weights):
        first = jnp.concatenate([first_ref[rows, :] for rows in spots], axis=0)
        adj = (nt(weights, branch[...]) + nt(first, grad_inner[...])).astype(bf16)
        wide = adj.shape[0] // len(spots)
        for index, rows in enumerate(spots):
            adj_ref[rows, :] = adj[index * wide : (index + 1) * wide]

    each_step(side_refs, spots_ref, visit)

    @pl.when(step == OUT_STEPS - 1)
    def _():
        firsts = tn(grad_inner[...], att_ref[...].T)
        seconds = LOW_FACTORED * tn(inner_ref[...], branch[...])
        for place in range(places):
            own = slice(place * wide, (place + 1) * wide)
            tables_ref[place, 0:RANK, :] = padded(firsts[0:RANK, own], span)
            tables_ref[place, RANK:, :] = padded(seconds[0:RANK, own], span)


def output_back(
    spots, w_sides, att, first, parts, mid, gain, out_grad, second, inner, places, span
):
    count, width = mid.shape
    outs = (
        struct(*att.shape), struct(places, 2 * RANK, span), struct(count, width, dtype=f32)
    )
    rest = (*parts, att, first, mid, gain, out_grad, second, inner)
    return pl.pallas_call(
        functools.partial(output_back_kernel, len(w_sides), len(parts)),
        grid_spec=pltpu.PrefetchScalarGridSpec(
            num_scalar_prefetch=1,
            grid=(OUT_STEPS,),
            in_specs=side_specs(w_sides) + [whole_block(v.shape) for v in rest],
            out_specs=[whole_block(v.shape) for v in outs],
            scratch_shapes=[
                pltpu.VMEM((count, width), bf16), pltpu.VMEM((count, LANES), bf16)
            ],
        ),
        out_shape=outs,
        compiler_params=call_params(),
        cost_estimate=NO_COST,
        name="output_back",
    )(spots, *w_sides, *rest)


PACKED = 5


def attend_tables_kernel(ways, sides, place_ref, adapter_ref, *refs):
    side_refs, out_refs = refs[:sides], refs[sides:]
    per_side, sources = side_refs[0].shape[0], side_refs[0].shape[1] // (PACKED * RANK)
    blocks = per_side * sides
    wide = out_refs[0].shape[2] // blocks
    third = wide // 3
    half = ATTENTION_EXTENT

    def read(place, source, index):
        slot = place_ref[place]
        rows = pl.ds((source * PACKED + index) * RANK, RANK)
        value = side_refs[0][lax.rem(slot, per_side), rows, :]
        if sides > 1:
            value = jnp.where(slot < per_side, value, side_refs[1][lax.rem(slot, per_side), rows, :])
        return value.astype(f32)

    def by_head(pieces):
        return [
            sum(pieces[h * ways + 1 : (h + 1) * ways], pieces[h * ways])
            for h in range(PAIRED_ATTENDERS)
        ]

    for out_ref in out_refs:
        out_ref[...] = jnp.zeros_like(out_ref)
    for source in range(sources):
        adapter = adapter_ref[source]
        got = [[read(c, source, index) for c in range(blocks)] for index in range(PACKED)]
        pieces = [[v[:, :wide] for v in got[index]] for index in range(4)]
        pieces.append([
            got[index][c][:, QUERY_COLS : QUERY_COLS + third]
            for c in range(blocks) for index in range(3)
        ])
        pieces.append(by_head([v[:, :QUERY_COLS] for v in got[4]]))
        pieces.append(by_head([v[:, QUERY_COLS : QUERY_COLS + half] for v in got[4]]))
        pieces.append(by_head([v[:, QUERY_COLS : QUERY_COLS + half] for v in got[3]]))
        for parts, out_ref in zip(pieces, out_refs):
            out_ref[adapter] = out_ref[adapter] + jnp.concatenate(parts, axis=1)


def attend_tables(place, adapters, sides, width, ways):
    key_cols = PAIRED_ATTENDERS * ATTENTION_EXTENT
    cols = (width,) * 5 + (ASKING_ATTENDERS * ATTENTION_EXTENT, key_cols, key_cols)
    return whole_call(
        functools.partial(attend_tables_kernel, ways, len(sides)),
        (place, adapters),
        sides,
        [struct(NUM_CHOICES_X, RANK, size, dtype=f32) for size in cols],
        name="attend_tables",
    )


def expert_tables_kernel(sizes, sources, terms, adapter_ref, *refs):
    term_refs, out_refs = refs[:terms], refs[terms:]
    adapter = pl.program_id(0)
    for out_ref in out_refs:
        out_ref[...] = jnp.zeros_like(out_ref)
    for source in range(sources):

        @pl.when(adapter_ref[source] == adapter)
        def _():
            for expert in range(term_refs[0].shape[0]):
                own = None
                for term_ref in term_refs:
                    term = term_ref[expert, source * RANK : (source + 1) * RANK, :].astype(f32)
                    own = term if own is None else own + term
                start = 0
                for size, out_ref in zip(sizes, out_refs):
                    out_ref[0, expert] += own[:, start : start + size]
                    start += size


def expert_tables(adapters, terms, wide, slim):
    experts, sources = terms[0].shape[0], adapters.shape[0]
    sizes = (wide,) * 3 + (slim,) * 3
    return pl.pallas_call(
        functools.partial(expert_tables_kernel, sizes, sources, len(terms)),
        grid_spec=pltpu.PrefetchScalarGridSpec(
            num_scalar_prefetch=1,
            grid=(NUM_CHOICES_X,),
            in_specs=[whole_block(v.shape) for v in terms],
            out_specs=[
                pl.BlockSpec((1, experts, RANK, size), lambda a, adapters: (a, 0, 0, 0))
                for size in sizes
            ],
        ),
        out_shape=[
            jax.ShapeDtypeStruct((NUM_CHOICES_X, experts, RANK, size), f32) for size in sizes
        ],
        compiler_params=call_params(),
        cost_estimate=NO_COST,
        name="expert_tables",
    )(adapters, *terms)


def source_mask(shape, sources):
    row = lax.broadcasted_iota(jnp.int32, shape, 0)
    col = lax.broadcasted_iota(jnp.int32, shape, 1)
    keep = None
    for source in range(sources):
        inside = (row >= source * CAP) & (row < (source + 1) * CAP)
        inside &= (lax.rem(col, sources * RANK) >= source * RANK) & (
            lax.rem(col, sources * RANK) < (source + 1) * RANK
        )
        keep = inside if keep is None else keep | inside
    return keep


def masked(values, sources):
    return jnp.where(source_mask(values.shape, sources), values, 0.0)


def picks(slot_ref, pair, tokens, unit=0):
    slots = slot_ref[unit, :, pair * 2 * tokens : (pair + 1) * 2 * tokens]
    place = lax.broadcasted_iota(jnp.int32, (2 * CAP, 2 * tokens), 0)
    return place == slots


def picked_rows(slot_ref, rows_ref, sources, unit=0):
    tokens = rows_ref.shape[0] // sources
    parts = []
    for pair in range(sources // 2):
        pick = picks(slot_ref, pair, tokens, unit).astype(f32).astype(bf16)
        rows = rows_ref[pair * 2 * tokens : (pair + 1) * 2 * tokens, :]
        parts.append(nn(pick, rows))
    return jnp.concatenate(parts, axis=0)


def picked_gates(slot_ref, gate_ref, sources, unit=0):
    tokens = gate_ref.shape[2] // sources
    parts = []
    for pair in range(sources // 2):
        gate = gate_ref[unit, :, pair * 2 * tokens : (pair + 1) * 2 * tokens]
        kept = jnp.where(picks(slot_ref, pair, tokens, unit), gate, 0.0)
        parts.append(jnp.sum(kept, axis=1, keepdims=True))
    return jnp.concatenate(parts, axis=0)


def combine(target_ref, values, out_refs):
    sources = len(out_refs)
    tokens = target_ref.shape[0] // sources
    slots = values.shape[1]
    for source, out_ref in enumerate(out_refs):
        target = target_ref[source * tokens : (source + 1) * tokens, :]
        place = lax.broadcasted_iota(jnp.int32, (tokens, slots), 1)
        hit = place == target[:, 0:1]
        for choice in range(1, TOPK):
            hit |= place == target[:, choice : choice + 1]
        out_ref[...] = nn(hit.astype(f32).astype(bf16), values[source]).astype(bf16)


def keep_rows(values, rows, expert, sources):
    for source in range(sources):
        values[source, pl.ds(pl.multiple_of(expert * CAP, CAP), CAP), :] = rows[
            source * CAP : (source + 1) * CAP
        ]


def joined(refs, unit=0):
    return jnp.concatenate([ref[0, unit] for ref in refs], axis=0)


def experts_pre_kernel(sources, adapter_ref, slot_ref, gate_ref, grads_ref, down_ref, *refs):
    down_first, down_second = joined(refs[:sources]), joined(refs[sources : 2 * sources])
    picked_ref, hidden_ref, inner_ref = refs[2 * sources :]
    grads = picked_rows(slot_ref, grads_ref, sources)
    grads = (grads * picked_gates(slot_ref, gate_ref, sources)).astype(bf16)
    picked_ref[0] = grads
    inner = LOW_FACTORED * nt(grads, down_second)
    inner = masked(inner, sources).astype(bf16)
    inner_ref[0] = inner
    hidden_ref[0] = nt(grads, down_ref[0]) + nn(inner, down_first)


def experts_main_kernel(
    sources, adapter_ref, slot_ref, gate_w, up_w, grad_hidden, target_ref, *refs
):
    x_refs, refs = refs[:sources], refs[sources:]
    groups = [refs[i * sources : (i + 1) * sources] for i in range(4)]
    picked_ref, hidden_ref, adj_ref, inner_ref, *out_refs, values, x_ref = refs[4 * sources :]
    per_step, width, inner_size = gate_w.shape
    span = 2 * sources * RANK

    @pl.when(pl.program_id(0) == 0)
    def _():
        tokens = x_refs[0].shape[0]
        for source in range(sources):
            x_ref[source * tokens : (source + 1) * tokens, :] = x_refs[source][...]

    firsts, seconds = [], []
    for unit in range(per_step):
        firsts.append(
            jnp.concatenate([joined(groups[0], unit), joined(groups[1], unit)], axis=0)
        )
        gate_second, up_second = joined(groups[2], unit), joined(groups[3], unit)
        blank = jnp.zeros_like(gate_second)
        seconds.append(
            jnp.concatenate(
                [
                    jnp.concatenate([gate_second, blank], axis=1),
                    jnp.concatenate([blank, up_second], axis=1),
                ],
                axis=0,
            )
        )
        picked_ref[unit] = picked_rows(slot_ref, x_ref, sources, unit).astype(bf16)
        inner = masked(LOW_FACTORED * nt(picked_ref[unit], firsts[unit]), sources)
        inner_ref[unit, :, :span] = inner.astype(bf16)
    for unit in range(per_step):
        x = picked_ref[unit]
        inner = inner_ref[unit, :, :span]
        for start in range(0, inner_size, 2 * LANES):
            cols = slice(start, start + 2 * LANES)
            ups = slice(inner_size + start, inner_size + start + 2 * LANES)
            gate = nn(x, gate_w[unit, :, cols]) + nn(inner, seconds[unit][:, cols])
            up = nn(x, up_w[unit, :, cols]) + nn(inner, seconds[unit][:, ups])
            sigma = 1.0 / (1.0 + jnp.exp(-gate))
            active = gate * sigma
            hidden_ref[unit, :, cols] = (active * up).astype(bf16)
            adj = grad_hidden[unit, :, cols]
            grad_gate = adj * up * sigma * (1.0 + gate * (1.0 - sigma))
            adj_ref[unit, :, cols] = grad_gate.astype(bf16)
            adj_ref[unit, :, ups] = (adj * active).astype(bf16)
    for unit in range(per_step):
        grad_inner = masked(LOW_FACTORED * nt(adj_ref[unit], seconds[unit]), sources)
        inner_ref[unit, :, span:] = grad_inner.astype(bf16)
    for unit in range(per_step):
        rows = nt(adj_ref[unit, :, :inner_size], gate_w[unit])
        rows = rows + nt(adj_ref[unit, :, inner_size:], up_w[unit])
        rows = rows + nn(inner_ref[unit, :, span:], firsts[unit])
        expert = pl.program_id(0) * per_step + unit
        keep_rows(values, rows.astype(bf16), expert, sources)

    @pl.when(pl.program_id(0) == pl.num_programs(0) - 1)
    def _():
        combine(target_ref, values, out_refs)


def experts_post_kernel(
    sources, cohort, adapter_ref, slot_ref, gate_ref, down_ref, picked_ref, hidden_ref, adj_ref,
    inner_ref, picked_grads, grad_inner_down, target_ref, *refs
):
    groups = [refs[i * sources : (i + 1) * sources] for i in range(2)]
    table_ref, *out_refs, values = refs[2 * sources :]
    per_step = hidden_ref.shape[0]
    units = range(per_step)
    span = sources * RANK
    width, inner_size = picked_ref.shape[2], hidden_ref.shape[2]
    wide, slim = width // cohort, inner_size // cohort
    inner_down = [
        masked(nt(hidden_ref[u], joined(groups[0], u)), sources).astype(bf16) for u in units
    ]
    for unit in units:
        answer = nn(hidden_ref[unit], down_ref[unit])
        answer = answer + LOW_FACTORED * nn(inner_down[unit], joined(groups[1], unit))
        gates = picked_gates(slot_ref, gate_ref, sources, unit)
        answer = answer.astype(bf16).astype(f32) * gates
        expert = pl.program_id(0) * per_step + unit
        keep_rows(values, answer.astype(bf16), expert, sources)
    for unit in units:
        hidden = hidden_ref[unit]
        firsts = tn(inner_ref[unit, :, 2 * span :], picked_ref[unit])
        seconds = tn(inner_ref[unit, :, : 2 * span], adj_ref[unit])
        down_firsts = tn(grad_inner_down[unit], hidden)
        down_seconds = LOW_FACTORED * tn(inner_down[unit], picked_grads[unit])
        wide_parts = (firsts[:span], firsts[span:], down_seconds)
        slim_parts = (seconds[:span, :inner_size], seconds[span:, inner_size:], down_firsts)
        for place in range(cohort):
            pieces = [v[:, place * wide : (place + 1) * wide] for v in wide_parts]
            pieces += [v[:, place * slim : (place + 1) * slim] for v in slim_parts]
            table_ref[place, unit] = jnp.concatenate(pieces, axis=1).astype(bf16)

    @pl.when(pl.program_id(0) == pl.num_programs(0) - 1)
    def _():
        combine(target_ref, values, out_refs)


def per_expert(array, per_step=1):
    rest = array.shape[1:]
    return pl.BlockSpec((per_step,) + rest, lambda e, *_: (e,) + (0,) * len(rest))


def expert_rows(rows, width, per_step=1):
    return pl.BlockSpec((per_step, rows, width), lambda e, *_: (e, 0, 0))


def adapter_blocks(table, sources, per_step):
    shape = (1, per_step) + table.shape[2:]
    return [
        pl.BlockSpec(shape, lambda e, adapters, *_, s=s: (adapters[s], e, 0, 0))
        for s in range(sources)
    ]


def expert_call(
    kernel, sources, scalars, arrays, specs, tables, out_shape, out_specs, scratch, name,
    per_step=1,
):
    experts = tables[0].shape[1]
    return pl.pallas_call(
        kernel,
        grid_spec=pltpu.PrefetchScalarGridSpec(
            num_scalar_prefetch=len(scalars),
            grid=(experts // per_step,),
            in_specs=specs
            + [spec for t in tables for spec in adapter_blocks(t, sources, per_step)],
            out_specs=out_specs,
            scratch_shapes=scratch,
        ),
        out_shape=out_shape,
        compiler_params=call_params(),
        cost_estimate=NO_COST,
        name=name,
    )(*scalars, *arrays, *[t for t in tables for _ in range(sources)])


def experts_pre(adapters, slots, gates, grads, down, down_first, down_second):
    experts, inner_size, width = down.shape
    sources = adapters.shape[0]
    rows = sources * CAP
    return expert_call(
        functools.partial(experts_pre_kernel, sources),
        sources,
        (adapters,),
        (slots, gates, grads, down),
        [
            per_expert(slots), per_expert(gates), whole_block((grads.shape[0], width)),
            per_expert(down),
        ],
        (down_first, down_second),
        [
            struct(experts, rows, width), struct(experts, rows, inner_size, dtype=f32),
            struct(experts, rows, sources * RANK),
        ],
        [expert_rows(rows, v) for v in (width, inner_size, sources * RANK)],
        [],
        "experts_pre",
    )


def experts_main(
    adapters, slots, x_blocks, gate_w, up_w, grad_hidden, target, gate_first, up_first,
    gate_second, up_second,
):
    experts, width, inner_size = gate_w.shape
    sources = adapters.shape[0]
    rows = sources * CAP
    tokens = x_blocks[0].shape[0]
    per_step = 2 if experts % 2 == 0 else 1
    outs = (width, inner_size, 2 * inner_size, 4 * sources * RANK)
    return expert_call(
        functools.partial(experts_main_kernel, sources),
        sources,
        (adapters,),
        (slots, gate_w, up_w, grad_hidden, target, *x_blocks),
        [
            per_expert(slots, per_step), per_expert(gate_w, per_step), per_expert(up_w, per_step),
            per_expert(grad_hidden, per_step), whole_block(target.shape),
        ]
        + [whole_block(v.shape) for v in x_blocks],
        (gate_first, up_first, gate_second, up_second),
        [struct(experts, rows, v) for v in outs] + [struct(tokens, width)] * sources,
        [expert_rows(rows, v, per_step) for v in outs]
        + [whole_block((tokens, width))] * sources,
        [
            pltpu.VMEM((sources, experts * CAP, width), bf16),
            pltpu.VMEM((sources * tokens, width), bf16),
        ],
        "experts_main",
        per_step,
    )


def experts_post(
    adapters, slots, gates, down, picked, hidden, adj, inner, picked_grads, grad_inner_down,
    target, down_first, down_second, cohort,
):
    experts, inner_size, width = down.shape
    sources = adapters.shape[0]
    tokens = target.shape[0] // sources
    per_step = 2 if experts % 2 == 0 else 1
    lanes = 3 * (width + inner_size) // cohort
    arrays = (
        slots, gates, down, picked, hidden, adj, inner, picked_grads, grad_inner_down
    )
    return expert_call(
        functools.partial(experts_post_kernel, sources, cohort),
        sources,
        (adapters,),
        arrays + (target,),
        [per_expert(v, per_step) for v in arrays] + [whole_block(target.shape)],
        (down_first, down_second),
        [struct(cohort, experts, sources * RANK, lanes)] + [struct(tokens, width)] * sources,
        [
            pl.BlockSpec((cohort, per_step, sources * RANK, lanes), lambda e, *_: (0, e, 0, 0)),
        ]
        + [whole_block((tokens, width))] * sources,
        [pltpu.VMEM((sources, experts * CAP, width), bf16)],
        "experts_post",
        per_step,
    )


def flipped(array, axis, size, mask):
    return lax.ppermute(array, axis, [(i, i ^ mask) for i in range(size)])


def ring_blocks(array, axis, size):
    return [array] + [
        lax.ppermute(array, axis, [(i, (i + shift) % size) for i in range(size)])
        for shift in range(1, size)
    ]


def ring_return(blocks, axis, size):
    return [blocks[0]] + [
        lax.ppermute(blocks[shift], axis, [(i, (i - shift) % size) for i in range(size)])
        for shift in range(1, size)
    ]


def to_every(array, axis, size):
    return lax.all_to_all(
        jnp.broadcast_to(array[None], (size,) + array.shape), axis, 0, 0, tiled=True
    )


def cohort_spots(size):
    place = jnp.arange(size, dtype=jnp.int32)
    if size != 8:
        return place, place
    me = lax.axis_index("ctx")
    mask = place ^ me
    return (place % 4 * 2 + place // 4) ^ me, (mask & 1) * 4 + mask // 2


def gather_cohort(array, size, halves=False, stage=lambda blocks: blocks):
    if size != 8:
        return (lax.all_gather(array, "ctx", axis=0, tiled=False),)
    if halves:
        half = array.shape[0] // 2
        near, far = flipped(array, "ctx", size, 2), flipped(array, "ctx", size, 4)
        low, high = stage(
            [flipped(near[:half], "ctx", size, 4), flipped(far[half:], "ctx", size, 2)]
        )
        blocks = [near, far, jnp.concatenate([low, high], axis=0)]
    else:
        blocks = stage([flipped(array, "ctx", size, mask) for mask in (2, 4, 6)])
    mine = jnp.stack([array] + blocks)
    return mine, flipped(mine, "ctx", size, 1)


def staged_sums(pieces, row_sides, summed, terms, tables_of, size, sources):
    tie = lax.optimization_barrier

    def plus(left, right):
        return (left.astype(f32) + right.astype(f32)).astype(bf16)

    other, row_side, pieces = tie((flipped(row_sides[1], "ctx", size, 1), row_sides[0], pieces))
    mine = plus(row_side, other)
    half = mine.shape[1] // 2
    low, high = mine[:, :half], mine[:, half:]
    near, far, slip = tie(
        (jnp.stack([low[1], low[3]]), jnp.stack([high[2], high[3]]), summed(pieces))
    )
    beside = tables_of(terms)
    near, far, groups = tie(
        (
            flipped(near, "ctx", size, 2), flipped(far, "ctx", size, 4),
            to_every(slip, "exp", sources),
        )
    )
    low_last, high_last, groups = tie(
        (plus(low[2], near[1]), plus(high[1], far[1]), groups.reshape(-1, slip.shape[1]))
    )
    low_last, high_last, blocks, beside = tie(
        (
            flipped(low_last, "ctx", size, 4), flipped(high_last, "ctx", size, 2),
            [flipped(groups, "ctx", size, mask) for mask in (2, 4, 6)], beside,
        )
    )
    mine = jnp.stack([groups] + blocks)
    low_sum = low[0].astype(f32) + near[0].astype(f32) + low_last.astype(f32)
    high_sum = high[0].astype(f32) + far[0].astype(f32) + high_last.astype(f32)
    rows = jnp.concatenate([low_sum, high_sum], axis=0)
    return (mine, flipped(mine, "ctx", size, 1)), rows, beside


def head_columns(query, key, value):
    rows = query.shape[0]

    def split(array):
        return jnp.transpose(array.reshape(rows, PAIRED_ATTENDERS, -1), (1, 0, 2))

    parts = [split(key), split(value), split(query)]
    pad = HEAD_COLS - sum(p.shape[2] for p in parts)
    parts.append(jnp.zeros((PAIRED_ATTENDERS, rows, pad), query.dtype))
    return jnp.concatenate(parts, axis=2)


def body(
    tokens, out_grad, attn_gain, moe_gain, w_query, lock_projection, content_projection, w_out,
    sigmoid_matrices, widener_matrices, reducer_matrices, segment_ids, expert_routes,
    route_weights, adapter_index, query_first, query_second, key_first, lock_final_matrices,
    value_first, content_final_matrices, output_first, output_second, gate_first, gate_second,
    upward_first, upward_second, down_first, down_second,
):
    rows_in = tokens[0].astype(f32)
    count, width = rows_in.shape
    cohort = lax.axis_size("ctx")
    sources = lax.axis_size("exp")
    experts = sigmoid_matrices.shape[0]
    ctx = lax.axis_index("ctx")
    exp = lax.axis_index("exp")
    ways = cohort // PAIRED_ATTENDERS
    head = ctx // ways
    adapter = adapter_index[exp]

    def elected(table):
        return lax.dynamic_index_in_dim(table, adapter, 0, keepdims=False)

    attended_cols = ASKING_ATTENDERS * ATTENTION_EXTENT
    wide = width // cohort
    span = -(-max(wide, QUERY_COLS) // LANES) * LANES
    spots, place = cohort_spots(cohort)
    order = jnp.concatenate([spots, (ctx % ways)[None].astype(jnp.int32)])

    normed_in, factor_in = normed(rows_in, attn_gain)
    labels = jnp.pad(segment_ids[0].astype(bf16)[:, None], ((0, 0), (0, LANES - 1)))
    x_sides = gather_cohort(
        jnp.concatenate([normed_in.astype(bf16), labels], axis=1), cohort, True
    )
    relative = (exp - jnp.arange(sources, dtype=jnp.int32) + sources) % sources
    out_rows = jnp.stack(ring_blocks(w_out, "exp", sources))[relative].reshape(-1, width)
    head_w = head_columns(w_query, lock_projection, content_projection)
    to_all = jnp.broadcast_to(
        head_w[:, None], (PAIRED_ATTENDERS, ways * sources) + head_w.shape[1:]
    ).reshape((cohort * sources,) + head_w.shape[1:])
    own_w = lax.all_to_all(to_all, ("ctx", "exp"), 0, 0, tiled=True).reshape(width, HEAD_COLS)

    routes = expert_routes[0].astype(bf16)
    weight_high = route_weights[0].astype(bf16)
    weight_low = (route_weights[0] - weight_high.astype(f32)).astype(bf16)
    parcel = jnp.concatenate(
        [
            out_grad[0], routes, weight_high, weight_low,
            jnp.zeros((count, LANES - 3 * TOPK), bf16),
        ],
        axis=1,
    )
    parcel, own_w = lax.optimization_barrier((parcel, own_w))
    parcels = ring_blocks(parcel, "exp", sources)

    own_firsts = jnp.concatenate(
        [elected(query_first), elected(key_first), elected(value_first)], axis=0
    )

    def head_part(table):
        part = elected(table)
        size = part.shape[1] // PAIRED_ATTENDERS
        return lax.dynamic_slice_in_dim(part, head * size, size, 1)

    def placed(part, row, col):
        return jnp.pad(
            part, ((row, 2 * RANK - row), (col, HEAD_COLS - col - part.shape[1]))
        )

    own_seconds = (
        placed(head_part(query_second), 0, LANES)
        + placed(head_part(lock_final_matrices), RANK, 0)
        + placed(head_part(content_final_matrices), 2 * RANK, ATTENTION_EXTENT)
    )
    qkv, inner, attended, lse, seg_col, seg_row = project_attend(
        order, x_sides, own_w, own_firsts, own_seconds, ways
    )
    shared = [lax.all_to_all(attended, "ctx", 0, 0, tiled=True)]

    def beside_attention(blocks):
        blocks, shared[0], parcels[:] = lax.optimization_barrier((blocks, shared[0], parcels))
        return blocks

    out_sides = gather_cohort(out_rows, cohort, True, beside_attention)
    attended = shared[0]
    if ways > 1:
        attended = attended.reshape(PAIRED_ATTENDERS, ways, QUERY_COLS, count)
        attended = attended.astype(f32).sum(1).astype(bf16)
    attended = attended.reshape(attended_cols, count)
    out_first = jnp.pad(elected(output_first), ((0, LANES - RANK), (0, 0)))
    out_first = out_first.T
    out_second = jnp.pad(elected(output_second), ((0, LANES - RANK), (0, 0)))
    mid, normed_mid, inner_out = output_project(
        spots, out_sides, attended, out_first, out_second, tokens[0], moe_gain[None]
    )
    x_exp = ring_blocks(normed_mid, "exp", sources)

    parcels, normed_mid = lax.optimization_barrier((parcels, normed_mid))
    parcels = jnp.concatenate(parcels, axis=0)
    extra = parcels[:, width:].astype(f32).reshape(sources, count, -1)
    all_routes = extra[:, :, :TOPK].astype(jnp.int32) - exp * experts
    all_gates = extra[:, :, TOPK : 2 * TOPK] + extra[:, :, 2 * TOPK : 3 * TOPK]
    hits = all_routes[None] == jnp.arange(experts, dtype=jnp.int32)[:, None, None, None]
    named = jnp.any(hits, axis=3)
    gates = jnp.sum(jnp.where(hits, all_gates[None], 0.0), axis=3).reshape(experts, 1, -1)
    earlier = jnp.tril(jnp.ones((count, count), bf16), -1)
    rank = lax.dot_general(
        named.astype(bf16), earlier, (((2,), (1,)), ((), ())), preferred_element_type=f32
    ).astype(jnp.int32)
    side = (jnp.arange(sources, dtype=jnp.int32) % 2 * CAP)[None, :, None]
    slots = jnp.where(named, rank + side, -1).reshape(experts, 1, -1)
    places = jnp.arange(experts, dtype=jnp.int32)[:, None, None] * CAP + rank + 1
    target = jnp.sum(jnp.where(hits, places[..., None], 0), axis=0) - 1
    target = target.reshape(sources * count, TOPK)

    adapters = adapter_index[relative]
    picked_grads, grad_hidden, grad_inner_down = experts_pre(
        adapters, slots, gates, parcels, reducer_matrices, down_first, down_second
    )
    picked, hidden, adj, inner_rows, *grad_parts = experts_main(
        adapters, slots, x_exp, sigmoid_matrices, widener_matrices, grad_hidden, target,
        gate_first, upward_first, gate_second, upward_second,
    )
    grad_parts = ring_return(grad_parts, "exp", sources)
    tables, *answers = experts_post(
        adapters, slots, gates, reducer_matrices, picked, hidden, adj, inner_rows,
        picked_grads, grad_inner_down, target, down_first, down_second, cohort,
    )
    tables, answers, grad_parts = lax.optimization_barrier((tables, answers, grad_parts))
    answers = ring_return(answers, "exp", sources)
    early, middle = answers[:2] + answers[3:], answers[2:3]
    terms = [lax.psum_scatter(tables, "ctx", scatter_dimension=0, tiled=False)]

    adj_blocks, out_tables, grad_mid = output_back(
        spots, out_sides, attended, out_first, grad_parts, mid, moe_gain[None], out_grad[0], out_second,
        inner_out, cohort, span,
    )
    adj_blocks = jnp.repeat(adj_blocks.reshape(-1, QUERY_COLS, count), ways, axis=0)
    adj_all = lax.all_to_all(adj_blocks, "ctx", 0, 0, tiled=True)
    adj_all, early = lax.optimization_barrier((adj_all, early))
    last_rows, grad_heads, grad_inner, pieces, own_seconds_grad = attend_back(
        order, qkv, adj_all, lse, own_seconds, inner, seg_col, seg_row, own_w, own_firsts,
        x_sides, out_tables, ways,
    )

    def tables_of(terms):
        return expert_tables(adapters, terms, wide, sigmoid_matrices.shape[2] // cohort)

    last_rows, grad_heads, pieces, middle = lax.optimization_barrier(
        (last_rows, grad_heads, pieces, middle)
    )

    pieces = lax.all_to_all(pieces, "ctx", 0, 0, tiled=True)
    row_sides = [
        rows_back(order, grad_heads, grad_inner, own_w, own_firsts, side) for side in x_sides[:-1]
    ] + [last_rows]

    def summed(pieces):
        total = jnp.pad(pieces.astype(f32).sum(0), ((0, RANK), (0, 0)))
        return (total + own_seconds_grad.astype(f32)).astype(bf16)

    if cohort != 8:
        groups = to_every(summed(pieces), "exp", sources)
        group_sides = gather_cohort(groups.reshape(-1, span), cohort)
        grad_normed_in = lax.psum_scatter(row_sides[0], "ctx", scatter_dimension=0).astype(f32)
        expert_grads = tables_of(terms)
    else:
        group_sides, grad_normed_in, expert_grads = staged_sums(
            pieces, row_sides, summed, terms, tables_of, cohort, sources
        )
    block_out = (mid + sum(v.astype(f32) for v in early + middle)).astype(bf16)[None]
    attention_tables = attend_tables(place, adapter_index, group_sides, width, ways)
    tokens_grad = (
        grad_mid + norm_back(rows_in, factor_in, attn_gain, grad_normed_in)
    ).astype(bf16)[None]
    gate_f, up_f, down_s, gate_s, up_s, down_f = expert_grads
    attention_tables = attend_tables(place, adapter_index, group_sides, width, ways)
    query_f, key_f, value_f, out_f, out_s, query_s, key_s, value_s = attention_tables
    return (
        block_out, tokens_grad, query_f, query_s, key_f, key_s, value_f, value_s, out_f, out_s,
        gate_f, gate_s, up_f, up_s, down_f, down_s,
    )


def solution(mesh):
    sharded = P("exp", "ctx", None)
    rows = P(("ctx", "exp"), None)
    table = P(None, "exp", None, None)
    expert = P("exp", None, None)
    in_specs = (
        (sharded, sharded, P(), P())
        + (rows,) * 4
        + (expert,) * 3
        + (P("exp", "ctx"), sharded, sharded, P())
        + (P(),) * 8
        + (table,) * 6
    )
    out_specs = (sharded, sharded) + (P(),) * 8 + (P(None, "exp", None, "ctx"),) * 6
    return jax.shard_map(body, mesh=mesh, in_specs=in_specs, out_specs=out_specs, check_vma=False)
```
